32 devices in a mesh: wide: 8 (over y, x, core), narrow: 4 (over z).
Axes of the slice: x: 2, y: 2, z: 4, core: 2. Of those that a mesh axis runs over, the one named last changes fastest.
Arguments:
- tokens: bfloat16 [16384, 1024], P(('wide', 'narrow')), may hold values from -6 to 6
- segment_ids: int32 [32, 512], P(('wide', 'narrow')), may hold values from 0 to 7, never falling along the last dimension, each value on 1 to 256 neighbouring positions
- attn_weight: bfloat16 [4096, 1024], P(('wide', 'narrow')), may hold values from -2 to 2, as said below
- vectors: bfloat16 [8192], P(('wide', 'narrow')), may hold values from -3 to 3
- ffn_weight: bfloat16 [2, 1024, 4096], P(None, 'wide', 'narrow'), may hold values from -0.1875 to 0.1875
- ffn_bias: bfloat16 [4096], P(('narrow', 'wide')), may hold values from -3 to 3
- out_grad: bfloat16 [16384, 1024], P(('wide', 'narrow')), may hold values from -6 to 6
Outputs:
- result: bfloat16 [16384, 1024], P(('wide', 'narrow'))
- grad_tokens: float32 [16384, 1024], P(('wide', 'narrow'))
- grad_attn: float32 [4096, 1024], P(('wide', 'narrow'))
- grad_vectors: float32 [8192], P(('wide', 'narrow'))
- grad_ffn: float32 [2, 1024, 4096], P(None, 'wide', 'narrow')
- grad_ffn_bias: float32 [4096], P(('narrow', 'wide'))
The draws below stay inside these ranges and needn't reach their ends.
Inputs may be any that keep to these rules, and one draw needn't show every extreme that they name: `segment_ids`: within each packed row of 512 tokens the ids never fall; each protein holds 1 to 256 tokens. `attn_weight`: entries drawn independently.
All inputs are finite; a program needn't handle non-finite values.
Results may differ from the reference program's by a relative error of at most 0.017.
Values may be sent and summed in bfloat16 or wider, within the bound.
No kernel may reach another device: no remote copies, remote signals or barrier semaphores. Data moves between devices by JAX's collectives and lax.ppermute only.
A program may use at most 192 MiB of HBM per device.

```python
import math
import jax
import jax.numpy as jnp
import numpy as np
from jax import lax

D = 1024
HEADS = 16
HEAD = 64
FF = 4096
LEN = 512
ROWS = 32
TOKENS = 16384
PROTEINS = 8


def draw_attn_weight(key, part):
    key = jax.random.fold_in(key, 7)
    dims_shape = (4 * D, D)
    base_draw = jnp.clip(jax.random.normal(key, dims_shape, jnp.float32), -4.0, 4.0)
    row_index = jnp.arange(4 * D)[:, None]
    row_scale = jnp.where(row_index < 3 * D, 1.0 / math.sqrt(D), 4.0 / math.sqrt(D))
    return (base_draw * row_scale).astype(jnp.bfloat16)


def strengthened(array, key, source, target, blocks, factor):
    owner, partner = [(jnp.arange(array.shape[axis_at]) // (array.shape[axis_at] // blocks)).reshape([-1 if axis == axis_at else 1 for axis in range(array.ndim)]) for axis_at in (source, target)]
    chosen = jax.random.permutation(key, blocks)[partner]
    strong = (owner == chosen) | (owner == (partner + blocks // 2) % blocks)
    return jnp.where(strong, factor * array, array)


def block_scale(own_key, dims, cuts, least, largest):
    def one(position, blocks):
        draws = jax.random.uniform(jax.random.fold_in(jax.random.fold_in(own_key, 6), position), (blocks,), jnp.float32, least / len(cuts), largest / len(cuts))
        return jnp.repeat(jnp.exp(draws), dims[position] // blocks).reshape((-1,) + (1,) * (len(dims) - position - 1))

    loudness = one(*cuts[0])
    for cut in cuts[1:]:
        loudness = loudness * one(*cut)
    return loudness


def length_profile(count, total, limit, lean):
    portions = [(1 << 20) // math.isqrt(standing ** lean) + 1 for standing in range(2, count + 1)]
    rest, counts = total - limit - (count - 1), [1] * (count - 1)
    while rest > 0:
        movable = [i for i in range(count - 1) if counts[i] < limit]
        pool, remaining = sum([portions[i] for i in movable]), rest
        for i in movable:
            extra = min(limit - counts[i], max(1, remaining * portions[i] // pool), rest)
            counts[i] = counts[i] + extra
            rest = rest - extra
    return np.array([limit] + counts)


def uneven_parts(key, amount, total, most, lean):
    if amount == 2:
        one = jax.random.randint(key, (), max(1, total - most), min(most, total - 1) + 1)
        return jnp.stack([one, total - one])
    lengths = jnp.asarray(length_profile(amount, total, most, lean), jnp.int32)
    couples = (amount - 1) // 2
    source_of, taker = lengths[1:1 + 2 * couples:2], lengths[2:2 + 2 * couples:2]
    slack = jnp.minimum(source_of - 1, most - taker)
    passed = jax.random.randint(jax.random.fold_in(key, 1), (couples,), 0, 1 << 20) % (slack + 1)
    lengths = lengths.at[1:1 + 2 * couples:2].set(source_of - passed).at[2:2 + 2 * couples:2].set(taker + passed)
    return lengths[jax.random.permutation(jax.random.fold_in(key, 2), amount)]


def normal_values(rng, dims, scale, most, pieces=(), kind=jnp.bfloat16):
    drawn = jax.random.normal(rng, dims, jnp.float32) * scale
    if len(pieces) > 0:
        drawn = block_scale(rng, dims, pieces, -0.22, 0.18) * drawn
    return jnp.clip(drawn, min=-most, max=most).astype(kind)


def gaussian_with(stream_key, shape, width, reach, split, heavy, held_as=jnp.bfloat16):
    values = width * jax.random.normal(stream_key, shape, jnp.float32)
    if split:
        values = values * block_scale(stream_key, shape, split, -0.22, 0.18)
    return jnp.clip(strengthened(values, jax.random.fold_in(stream_key, 3), *heavy), -reach, reach).astype(held_as)


def setup_inputs(seed: int = 0) -> dict:
    streams_of = jax.random.split(jax.random.key(seed), 8)
    tokens = normal_values(streams_of[0], (TOKENS, D), 1.0, 6.0, ((0, 32),))
    segment_ids = jax.vmap(lambda own: jnp.searchsorted(jnp.cumsum(uneven_parts(own, PROTEINS, LEN, LEN // 2, 2)), jnp.arange(LEN), side="right"))(jax.random.split(streams_of[1], ROWS)).reshape((ROWS, LEN)).astype(jnp.int32)
    attn_weight = draw_attn_weight(jax.random.fold_in(streams_of[7], 71), 0)
    vectors = normal_values(streams_of[3], (8 * D,), 0.3, 3.0, ((0, 32),))
    ffn_weight = normal_values(streams_of[4], (2, D, FF), D ** -0.5, 0.1875, ((1, 8), (2, 4)))
    ffn_bias = normal_values(streams_of[5], (FF,), 0.3, 3.0, ((0, 32),))
    out_grad = gaussian_with(streams_of[6], (TOKENS, D), 1.0, 6.0, ((0, 32),), (0, 1, 32, 2.75))
    return {"tokens": tokens, "segment_ids": segment_ids, "attn_weight": attn_weight, "vectors": vectors, "ffn_weight": ffn_weight, "ffn_bias": ffn_bias, "out_grad": out_grad}


@jax.custom_vjp
def low(v):
    return lax.optimization_barrier(v.astype(jnp.bfloat16)).astype(jnp.float32)

@jax.custom_vjp
def low_back(v):
    return v

def low_keep(v):
    return (low(v), None)

def low_pass(kept, grad):
    return (grad,)

def back_keep(v):
    return (v, None)

def back_low(kept, grad):
    return (low(grad),)
low.defvjp(low_keep, low_pass)
low_back.defvjp(back_keep, back_low)
highest = lax.Precision.HIGHEST

def layer_norm(hidden, gain_offset, shift_row):
    center = hidden - lax.optimization_barrier(jnp.mean(hidden, -1, keepdims=True))
    spread = lax.optimization_barrier(jnp.mean(center * center, -1, keepdims=True))
    return center * lax.rsqrt(spread + 1e-12) * (1.0 + gain_offset) + shift_row

def attend(queries, keys_low, values_low, segments):
    batches, length, features = queries.shape
    shaped_q = queries.reshape(batches, length, HEADS, HEAD)
    shaped_k = keys_low.reshape(batches, length, HEADS, HEAD)
    shaped_v = values_low.reshape(batches, length, HEADS, HEAD)
    scores = jnp.einsum('bqhd,bkhd->bhqk', shaped_q, shaped_k, precision=highest) * HEAD ** (-0.5)
    scores = low_back(scores)
    allowed = segments[:, None, :, None] == segments[:, None, None, :]
    scores = jnp.where(allowed, scores, -1e+30)
    weights = jax.nn.softmax(scores, axis=-1)
    mixed_heads = jnp.einsum('bhqk,bkhd->bqhd', low(weights), shaped_v, precision=highest)
    return mixed_heads.reshape(batches, length, features)

def layer_block(params, hidden_in, segments):
    attn_w, vector_rows, ffn_w, ffn_shift = params
    features = hidden_in.shape[-1]
    w_query = attn_w[0:features]
    w_key = attn_w[features:2 * features]
    w_value = attn_w[2 * features:3 * features]
    w_out = attn_w[3 * features:]
    queries = low(low_back(jnp.dot(hidden_in, w_query, precision=highest)) + vector_rows[0])
    keys_low = low(low_back(jnp.dot(hidden_in, w_key, precision=highest)))
    values_low = low(low_back(jnp.dot(hidden_in, w_value, precision=highest)) + vector_rows[1])
    mixed_heads = low(low_back(attend(queries, keys_low, values_low, segments)))
    first_sum = hidden_in + low_back(jnp.dot(mixed_heads, w_out, precision=highest)) + vector_rows[2]
    first_norm = layer_norm(first_sum, vector_rows[6], vector_rows[3])
    before = low_back(jnp.dot(low(first_norm), ffn_w[0], precision=highest)) + ffn_shift
    active = low(jax.nn.gelu(before, approximate=False))
    branch = low_back(lax.dot_general(active, ffn_w[1], (((2,), (1,)), ((), ())), precision=highest)) + vector_rows[4]
    return layer_norm(first_norm + branch, vector_rows[7], vector_rows[5])

def forward(tokens_f, attn_w, vector_flat, ffn_w, ffn_shift, segment_ids):
    features = tokens_f.shape[-1]
    total_rows = segment_ids.shape[0]
    length = segment_ids.shape[1]
    block_limit = max(1, 4096 // length)
    block_rows = 1
    for option in range(1, min(block_limit, total_rows) + 1):
        if total_rows % option == 0:
            block_rows = option
    blocks = total_rows // block_rows
    hidden_blocks = tokens_f.reshape(blocks, block_rows, length, features)
    segment_blocks = segment_ids.reshape(blocks, block_rows, length)
    vector_rows = vector_flat.reshape(8, features)

    def one_block(block_pair):
        return layer_block((attn_w, vector_rows, ffn_w, ffn_shift), block_pair[0], block_pair[1])
    outputs = lax.map(jax.checkpoint(one_block), (hidden_blocks, segment_blocks))
    return outputs.reshape(total_rows * length, features)

def reference(tokens, segment_ids, attn_weight, vectors, ffn_weight, ffn_bias, out_grad):

    def whole_layer(tokens_f, attn_w, vector_flat, ffn_w, ffn_shift):
        return forward(tokens_f, attn_w, vector_flat, ffn_w, ffn_shift, segment_ids)
    primal, pullback = jax.vjp(whole_layer, tokens.astype(jnp.float32), attn_weight.astype(jnp.float32), vectors.astype(jnp.float32), ffn_weight.astype(jnp.float32), ffn_bias.astype(jnp.float32))
    gradients = pullback(out_grad.astype(jnp.float32))
    return (primal.astype(jnp.bfloat16), gradients[0], gradients[1], gradients[2], gradients[3], gradients[4])
```

```python
import functools

import jax
import jax.numpy as jnp
from jax import lax
from jax.experimental import pallas as pl
from jax.experimental.pallas import tpu as pltpu
from jax.sharding import PartitionSpec as P

HEADS = 16
HEAD = 64
CHUNKS = 2
VMEM_LIMIT = 56 * 1024 * 1024

f32 = jnp.float32
bf16 = jnp.bfloat16

NT = (((1,), (1,)), ((), ()))
TN = (((0,), (0,)), ((), ()))


def dot(a, b):
    return jnp.dot(a, b, preferred_element_type=f32)


def dot_nt(a, b):
    return lax.dot_general(a, b, NT, preferred_element_type=f32)


def dot_tn(a, b):
    return lax.dot_general(a, b, TN, preferred_element_type=f32)


def swap_wide(v, mask):
    size = lax.axis_size("wide")
    return lax.ppermute(v, "wide", [(w, w ^ mask) for w in range(size)])


def shift_narrow(v, step):
    size = lax.axis_size("narrow")
    return lax.ppermute(v, "narrow", [(z, (z + step) % size) for z in range(size)])


def chip_bits():
    return (lax.axis_size("wide") // 2).bit_length() - 1


def gather_narrow(v, axis):
    size = lax.axis_size("narrow")
    pieces = [v] + [shift_narrow(v, s) for s in range(1, size)]
    return jnp.concatenate(pieces, axis)


def gather_chips(v, order):
    bits = chip_bits()
    done = []
    for bit in order:
        other = swap_wide(v, 2 << bit)
        axis = sum(1 for b in done if b > bit)
        v = jnp.stack([v, other], axis)
        done.append(bit)
    assert len(done) == bits
    return v


def bit_of(index, bit):
    return lax.rem(lax.div(index, 1 << bit), 2)


def pick(v, axis, index):
    return lax.dynamic_index_in_dim(v, index, axis, keepdims=False)


def to_slots(v, chip, core):
    bits = chip_bits()
    lead = v.shape[:-1]
    block = v.shape[-1] // lax.axis_size("wide")
    t = v.reshape(lead + (2,) * (bits + 1) + (block,))
    n = len(lead)
    for bit in range(bits):
        axis = n + bits - 1 - bit
        t = jnp.where(bit_of(chip, bit) == 1, jnp.flip(t, axis), t)
    t = jnp.where(core == 1, jnp.flip(t, n + bits), t)
    t = jnp.moveaxis(t, n + bits, n)
    return t.reshape(v.shape)


def from_slots(v, chip, core):
    bits = chip_bits()
    lead = v.shape[:-1]
    block = v.shape[-1] // lax.axis_size("wide")
    n = len(lead)
    t = v.reshape(lead + (2,) * (bits + 1) + (block,))
    t = jnp.moveaxis(t, n, n + bits)
    for bit in range(bits):
        axis = n + bits - 1 - bit
        t = jnp.where(bit_of(chip, bit) == 1, jnp.flip(t, axis), t)
    t = jnp.where(core == 1, jnp.flip(t, n + bits), t)
    return t.reshape(v.shape)


def load_rows(pos, geometry, own, other, matrix, first, count, place, sem):
    narrow, per_matrix = geometry

    def body(j, carry):
        block = matrix * per_matrix + first + j
        w = block // narrow
        z = block % narrow
        chip = (w // 2) ^ pos[0]
        core = (w % 2) ^ pos[1]
        step = lax.rem(pos[2] - z + narrow, narrow)

        @pl.when(core == 0)
        def _():
            pltpu.make_async_copy(own.at[chip, step], place(j), sem).start()

        @pl.when(core == 1)
        def _():
            pltpu.make_async_copy(other.at[chip, step], place(j), sem).start()

        return carry

    lax.fori_loop(0, count, body, 0)


def attend_forward(
    geometry, pos, x_ref, seg_row, seg_col, vec_ref, bo_ref, own_a, oth_a, own_b, oth_b,
    q_ref, k_ref, v_ref, p_ref, o_ref, h_ref, w_in, w_out, mask, sems,
):
    g = pl.program_id(0)
    steps = pl.num_programs(0)
    rows = own_a.shape[2]
    sources = ((own_a, oth_a), (own_b, oth_b))
    blocks = x_ref.shape[1] // rows

    @pl.when(g == 0)
    def _():
        for half in range(2):
            for m in range(3):
                load_rows(
                    pos, geometry, *sources[half], m, 0, blocks,
                    lambda j, half=half, m=m: w_in.at[half, m, pl.ds(pl.multiple_of(j * rows, rows), rows)],
                    sems.at[half],
                )
        for half in range(2):
            load_rows(
                pos, geometry, *sources[half], 3, 0, blocks,
                lambda j, half=half: w_out.at[half, pl.ds(pl.multiple_of(j * rows, rows), rows)],
                sems.at[2],
            )
        mask[...] = jnp.where(seg_col[...] == seg_row[...], 0.0, -1e30).astype(f32)
        pltpu.make_async_copy(w_in.at[0], w_in.at[0], sems.at[0]).wait()

    @pl.when(g == steps // 2)
    def _():
        pltpu.make_async_copy(w_in.at[1], w_in.at[1], sems.at[1]).wait()

    half = g // (steps // 2)
    columns = pl.ds(pl.multiple_of(lax.rem(g, steps // 2) * 256, 256), 256)
    x = x_ref[...]
    query = (dot(x, w_in[half, 0, :, columns]) + vec_ref[0:1, :]).astype(bf16)
    query = query * jnp.asarray(HEAD**-0.5, bf16)
    key = dot(x, w_in[half, 1, :, columns]).astype(bf16)
    value = (dot(x, w_in[half, 2, :, columns]) + vec_ref[1:2, :]).astype(bf16)
    q_ref[...] = query
    k_ref[...] = key
    v_ref[...] = value
    lane = lax.broadcasted_iota(jnp.int32, (1, 128), 1)
    for pair in range(2):
        part = slice(pair * 128, pair * 128 + 128)
        q2, k2, v2 = query[:, part], key[:, part], value[:, part]
        v2t = v2.T
        outs = []
        for sub in range(2):
            mine = (lane < HEAD) if sub == 0 else (lane >= HEAD)
            scores = dot_nt(k2, jnp.where(mine, q2, jnp.zeros_like(q2))) + mask[...]
            raised = jnp.exp(scores - jnp.max(scores, 0, keepdims=True))
            probs = (raised * (1.0 / jnp.sum(raised, 0, keepdims=True))).astype(bf16)
            p_ref[pair * 2 + sub] = probs
            outs.append(dot(v2t[sub * HEAD : sub * HEAD + HEAD], probs))
        mixed = jnp.concatenate(outs, 0).T.astype(bf16)
        o_ref[:, pl.ds(pl.multiple_of(g * 256 + pair * 128, 128), 128)] = mixed

    @pl.when(g == steps - 1)
    def _():
        pltpu.make_async_copy(w_out, w_out, sems.at[2]).wait()
        width = w_out.shape[2]
        for half in range(2):
            cols = slice(half * width, half * width + width)
            h_ref[:, cols] = (
                x_ref[:, cols].astype(f32) + dot(o_ref[...], w_out[half]) + bo_ref[0:1, cols]
            )


def run_attend_forward(pos, tokens, segment_ids, biases, own_a, oth_a, own_b, oth_b):
    count, features = tokens.shape
    rows = own_a.shape[2]
    narrow = own_a.shape[1]
    geometry = (narrow, features // rows)
    groups = features // 256
    whole = lambda *shape: pl.BlockSpec(shape, lambda g, pos: (0,) * len(shape))
    column = pl.BlockSpec((count, 256), lambda g, pos: (0, g))
    anywhere = pl.BlockSpec(memory_space=pl.ANY)
    width = features // 2
    return pl.pallas_call(
        functools.partial(attend_forward, geometry),
        grid_spec=pltpu.PrefetchScalarGridSpec(
            num_scalar_prefetch=1,
            grid=(groups,),
            in_specs=[
                whole(count, features), whole(1, count), whole(count, 1),
                pl.BlockSpec((8, 256), lambda g, pos: (0, g)), whole(8, features),
                anywhere, anywhere, anywhere, anywhere,
            ],
            out_specs=[
                column, column, column,
                pl.BlockSpec((4, count, count), lambda g, pos: (g, 0, 0)),
                whole(count, features), whole(count, features),
            ],
            scratch_shapes=[
                pltpu.VMEM((2, 3, features, width), bf16),
                pltpu.VMEM((2, features, width), bf16),
                pltpu.VMEM((count, count), f32),
                pltpu.SemaphoreType.DMA((3,)),
            ],
        ),
        out_shape=[
            jax.ShapeDtypeStruct((count, features), bf16),
            jax.ShapeDtypeStruct((count, features), bf16),
            jax.ShapeDtypeStruct((count, features), bf16),
            jax.ShapeDtypeStruct((HEADS, count, count), bf16),
            jax.ShapeDtypeStruct((count, features), bf16),
            jax.ShapeDtypeStruct((count, features), f32),
        ],
        compiler_params=pltpu.CompilerParams(
            vmem_limit_bytes=VMEM_LIMIT, dimension_semantics=("arbitrary",)
        ),
        cost_estimate=pl.CostEstimate(
            flops=2 * count * features * features * 8, bytes_accessed=24 << 20, transcendentals=0
        ),
        name="attend_forward",
    )(
        pos, tokens, segment_ids.reshape(1, count), segment_ids.reshape(count, 1),
        biases, biases[2:3] + jnp.zeros((8, 1), f32), own_a, oth_a, own_b, oth_b,
    )


def attend_backward(
    geometry, half, pos, dh_ref, add_ref, q_ref, k_ref, v_ref, p_ref, own_a, oth_a, own_b, oth_b,
    d_ref, dx_ref, bias_ref, w_in, w_out, sems,
):
    g = pl.program_id(0)
    rows = own_a.shape[2]
    features = dh_ref.shape[1]
    sources = ((own_a, oth_a), (own_b, oth_b))
    blocks = features // rows

    @pl.when(g == 0)
    def _():
        for part in range(2):
            load_rows(
                pos, geometry, *sources[part], 3, half * (blocks // 2), blocks // 2,
                lambda j, part=part: w_out.at[part, pl.ds(pl.multiple_of(j * rows, rows), rows)],
                sems.at[0],
            )
        for m in range(3):
            load_rows(
                pos, geometry, *sources[half], m, 0, blocks,
                lambda j, m=m: w_in.at[m, pl.ds(pl.multiple_of(j * rows, rows), rows)],
                sems.at[1],
            )
        pltpu.make_async_copy(w_out, w_out, sems.at[0]).wait()

    span = pl.ds(pl.multiple_of(g * 256, 256), 256)
    width = features // 2
    low = dh_ref[...].astype(bf16)
    grad_mixed = (
        dot_nt(low[:, :width], w_out[0, span, :]) + dot_nt(low[:, width:], w_out[1, span, :])
    ).astype(bf16)
    lane = lax.broadcasted_iota(jnp.int32, (1, 128), 1)
    lows = [[], [], []]
    sums = [[], []]
    for pair in range(2):
        part = slice(pair * 128, pair * 128 + 128)
        q2, k2, v2 = q_ref[:, part], k_ref[:, part], v_ref[:, part]
        do2 = grad_mixed[:, part]
        k2t = k2.T
        zero = jnp.zeros_like(q2)
        dv = dk = None
        dqs = []
        for sub in range(2):
            mine = (lane < HEAD) if sub == 0 else (lane >= HEAD)
            probs = p_ref[pair * 2 + sub]
            do_mine = jnp.where(mine, do2, zero)
            grad_probs = dot_nt(v2, do_mine)
            wide_probs = probs.astype(f32)
            inner = jnp.sum(wide_probs * grad_probs, 0, keepdims=True)
            grad_scores = (wide_probs * (grad_probs - inner)).astype(bf16)
            dv_part = dot(probs, do_mine)
            dk_part = dot(grad_scores, jnp.where(mine, q2, zero))
            dv = dv_part if dv is None else dv + dv_part
            dk = dk_part if dk is None else dk + dk_part
            dqs.append(dot(k2t[sub * HEAD : sub * HEAD + HEAD], grad_scores))
        dq = jnp.concatenate(dqs, 0).T * HEAD**-0.5
        sums[0].append(jnp.sum(dq, 0, keepdims=True))
        sums[1].append(jnp.sum(dv, 0, keepdims=True))
        for store, value in zip(lows, (dq, dk, dv)):
            store.append(value.astype(bf16))
    joined = [jnp.concatenate(s, 1) for s in lows]
    for m in range(3):
        d_ref[m] = joined[m]
    bias_ref[...] = jnp.concatenate(
        [jnp.concatenate(s, 1) for s in sums] + [jnp.zeros((6, 256), f32)], 0
    )

    @pl.when(g == 0)
    def _():
        pltpu.make_async_copy(w_in, w_in, sems.at[1]).wait()
        dx_ref[...] = add_ref[...]

    dx_ref[...] += (
        dot_nt(joined[0], w_in[0, :, span])
        + dot_nt(joined[1], w_in[1, :, span])
        + dot_nt(joined[2], w_in[2, :, span])
    )


def run_attend_backward(half, pos, grad_sum, added, q, k, v, probs, own_a, oth_a, own_b, oth_b):
    count, features = q.shape
    rows = own_a.shape[2]
    narrow = own_a.shape[1]
    geometry = (narrow, features // rows)
    groups = features // 512
    whole = lambda *shape: pl.BlockSpec(shape, lambda g, pos: (0,) * len(shape))
    column = pl.BlockSpec((count, 256), lambda g, pos: (0, half * groups + g))
    anywhere = pl.BlockSpec(memory_space=pl.ANY)
    width = features // 2
    return pl.pallas_call(
        functools.partial(attend_backward, geometry, half),
        grid_spec=pltpu.PrefetchScalarGridSpec(
            num_scalar_prefetch=1,
            grid=(groups,),
            in_specs=[
                whole(count, features), whole(count, features), column, column, column,
                pl.BlockSpec((4, count, count), lambda g, pos: (half * groups + g, 0, 0)),
                anywhere, anywhere, anywhere, anywhere,
            ],
            out_specs=[
                pl.BlockSpec((3, count, 256), lambda g, pos: (0, 0, g)),
                whole(count, features),
                pl.BlockSpec((8, 256), lambda g, pos: (0, g)),
            ],
            scratch_shapes=[
                pltpu.VMEM((3, features, width), bf16),
                pltpu.VMEM((2, width, width), bf16),
                pltpu.SemaphoreType.DMA((2,)),
            ],
        ),
        out_shape=[
            jax.ShapeDtypeStruct((3, count, width), bf16),
            jax.ShapeDtypeStruct((count, features), f32),
            jax.ShapeDtypeStruct((8, width), f32),
        ],
        compiler_params=pltpu.CompilerParams(
            vmem_limit_bytes=VMEM_LIMIT, dimension_semantics=("arbitrary",)
        ),
        cost_estimate=pl.CostEstimate(
            flops=2 * count * features * features * 6, bytes_accessed=16 << 20, transcendentals=0
        ),
        name="attend_backward",
    )(pos, grad_sum, added, q, k, v, probs, own_a, oth_a, own_b, oth_b)


def moments(hidden):
    center = hidden - jnp.mean(hidden, -1, keepdims=True)
    return center, lax.rsqrt(jnp.mean(center * center, -1, keepdims=True) + 1e-12)


def norm_back(grad, normed, factor):
    return factor * (
        grad
        - jnp.mean(grad, -1, keepdims=True)
        - normed * jnp.mean(grad * normed, -1, keepdims=True)
    )


def gelu_pair(a):
    z = jnp.abs(a) * (0.5**0.5)
    t = 1.0 / (1.0 + 0.3275911 * z)
    poly = t * (
        0.127414796 + t * (-0.142248368 + t * (0.7107068705 + t * (-0.7265760135 + t * 0.5307027145)))
    )
    bell = jnp.exp(-0.5 * (a * a))
    tail = poly * bell
    phi = jnp.where(a >= 0, 1.0 - tail, tail)
    return a * phi, phi + a * (bell * 0.3989422804014327)


ROWS_AT_ONCE = 128


def row_blocks(count):
    return [slice(r, r + ROWS_AT_ONCE) for r in range(0, count, ROWS_AT_ONCE)]


def ffn_forward(first, last, *refs):
    refs = list(refs)
    h_ref, vec, w1a, w1b, w2a, w2b, b1 = refs[:7]
    refs = refs[7:]
    f_in = None if first else refs.pop(0)
    dy = refs.pop(0) if last else None
    act_ref, slope_ref = refs[:2]
    refs = refs[2:]
    u_out = refs.pop(0) if first else None
    if last:
        result, dh, dh_low, sums = refs[:4]
        refs = refs[4:]
        total, u_low = refs
    else:
        total, u_low = refs
    t = pl.program_id(0)
    count, features = h_ref.shape
    width = features // 2

    @pl.when(t == 0)
    def _():
        for r in row_blocks(count):
            center, factor = moments(h_ref[r, :])
            u_low[r, :] = (center * factor * (1.0 + vec[0:1, :]) + vec[1:2, :]).astype(bf16)
        if first:
            u_out[...] = u_low[...]
            total[...] = jnp.zeros_like(total)
        else:
            total[...] = f_in[...]

    a = dot(u_low[:, :width], w1a[...]) + dot(u_low[:, width:], w1b[...]) + b1[0:1, :]
    act, slope = gelu_pair(a)
    act = act.astype(bf16)
    act_ref[...] = act
    slope_ref[...] = slope.astype(bf16)
    total[:, :width] += dot_nt(act, w2a[...])
    total[:, width:] += dot_nt(act, w2b[...])
    if last:

        @pl.when(t == pl.num_programs(0) - 1)
        def _():
            sums[...] = jnp.zeros_like(sums)
            for r in row_blocks(count):
                center, factor = moments(h_ref[r, :])
                u = center * factor * (1.0 + vec[0:1, :]) + vec[1:2, :]
                center, factor = moments(u + total[r, :] + vec[2:3, :])
                normed = center * factor
                result[r, :] = (normed * (1.0 + vec[3:4, :]) + vec[4:5, :]).astype(bf16)
                grad = dy[r, :].astype(f32)
                back = norm_back(grad * (1.0 + vec[3:4, :]), normed, factor)
                dh[r, :] = back
                dh_low[r, :] = back.astype(bf16)
                sums[0:1, :] += jnp.sum(grad, 0, keepdims=True)
                sums[1:2, :] += jnp.sum(grad * normed, 0, keepdims=True)
                sums[2:3, :] += jnp.sum(back, 0, keepdims=True)


TILE = 512


def run_ffn_forward(hidden, vec, w1, w2, b1, earlier, dy):
    count, features = hidden.shape
    width, units = w1[0].shape
    first, last = earlier is None, dy is not None
    whole = lambda *shape: pl.BlockSpec(shape, lambda t: (0,) * len(shape))
    tall = pl.BlockSpec((width, TILE), lambda t: (0, t))
    strip = pl.BlockSpec((count, TILE), lambda t: (0, t))
    ins = [hidden, vec, w1[0], w1[1], w2[0], w2[1], b1]
    in_specs = [
        whole(count, features), whole(8, features), tall, tall, tall, tall,
        pl.BlockSpec((1, TILE), lambda t: (0, t)),
    ]
    out_specs = [strip, strip]
    out_shape = [jax.ShapeDtypeStruct((count, units), bf16)] * 2
    scratch = [pltpu.VMEM((count, features), bf16)]
    if not first:
        ins.append(earlier)
        in_specs.append(whole(count, features))
    if last:
        ins.append(dy)
        in_specs.append(whole(count, features))
    if first:
        out_specs.append(whole(count, features))
        out_shape.append(jax.ShapeDtypeStruct((count, features), bf16))
    if last:
        out_specs += [whole(count, features)] * 3 + [whole(8, features)]
        out_shape += [
            jax.ShapeDtypeStruct((count, features), bf16),
            jax.ShapeDtypeStruct((count, features), f32),
            jax.ShapeDtypeStruct((count, features), bf16),
            jax.ShapeDtypeStruct((8, features), f32),
        ]
        scratch = [pltpu.VMEM((count, features), f32)] + scratch
    else:
        out_specs.append(whole(count, features))
        out_shape.append(jax.ShapeDtypeStruct((count, features), f32))
    return pl.pallas_call(
        functools.partial(ffn_forward, first, last),
        grid=(units // TILE,),
        in_specs=in_specs,
        out_specs=out_specs,
        out_shape=out_shape,
        scratch_shapes=scratch,
        compiler_params=pltpu.CompilerParams(
            vmem_limit_bytes=VMEM_LIMIT, dimension_semantics=("arbitrary",)
        ),
        cost_estimate=pl.CostEstimate(
            flops=4 * count * features * units * 2, bytes_accessed=16 << 20, transcendentals=0
        ),
        name="ffn_forward",
    )(*ins)


def ffn_backward(first, last, *refs):
    refs = list(refs)
    dh_low, w1a, w1b, w2a, w2b, slope = refs[:6]
    refs = refs[6:]
    du_in = None if first else refs.pop(0)
    if last:
        dh, h_ref, vec = refs[:3]
        refs = refs[3:]
    da_ref, db_ref = refs[:2]
    refs = refs[2:]
    if last:
        dh1, sums, total = refs
    else:
        (total,) = refs
    t = pl.program_id(0)
    count, features = dh_low.shape
    width = features // 2

    @pl.when(t == 0)
    def _():
        total[...] = jnp.zeros_like(total) if first else du_in[...]

    grad = dot(dh_low[:, :width], w2a[...]) + dot(dh_low[:, width:], w2b[...])
    grad = grad * slope[...].astype(f32)
    db_ref[...] = jnp.sum(grad, 0, keepdims=True)
    low = grad.astype(bf16)
    da_ref[...] = low
    total[:, :width] += dot_nt(low, w1a[...])
    total[:, width:] += dot_nt(low, w1b[...])
    if last:

        @pl.when(t == pl.num_programs(0) - 1)
        def _():
            sums[...] = jnp.zeros_like(sums)
            for r in row_blocks(count):
                center, factor = moments(h_ref[r, :])
                normed = center * factor
                du = total[r, :] + dh[r, :]
                back = norm_back(du * (1.0 + vec[0:1, :]), normed, factor)
                dh1[r, :] = back
                sums[0:1, :] += jnp.sum(du, 0, keepdims=True)
                sums[1:2, :] += jnp.sum(du * normed, 0, keepdims=True)
                sums[2:3, :] += jnp.sum(back, 0, keepdims=True)


def run_ffn_backward(dh_low, w1, w2, slope, earlier, tail):
    count, features = dh_low.shape
    width, units = w1[0].shape
    first, last = earlier is None, tail is not None
    whole = lambda *shape: pl.BlockSpec(shape, lambda t: (0,) * len(shape))
    tall = pl.BlockSpec((width, TILE), lambda t: (0, t))
    strip = pl.BlockSpec((count, TILE), lambda t: (0, t))
    ins = [dh_low, w1[0], w1[1], w2[0], w2[1], slope]
    in_specs = [whole(count, features), tall, tall, tall, tall, strip]
    out_specs = [strip, pl.BlockSpec((1, TILE), lambda t: (0, t))]
    out_shape = [
        jax.ShapeDtypeStruct((count, units), bf16),
        jax.ShapeDtypeStruct((1, units), f32),
    ]
    scratch = []
    if not first:
        ins.append(earlier)
        in_specs.append(whole(count, features))
    if last:
        ins += list(tail)
        in_specs += [whole(count, features), whole(count, features), whole(8, features)]
        out_specs += [whole(count, features), whole(8, features)]
        out_shape += [
            jax.ShapeDtypeStruct((count, features), f32),
            jax.ShapeDtypeStruct((8, features), f32),
        ]
        scratch = [pltpu.VMEM((count, features), f32)]
    else:
        out_specs.append(whole(count, features))
        out_shape.append(jax.ShapeDtypeStruct((count, features), f32))
    return pl.pallas_call(
        functools.partial(ffn_backward, first, last),
        grid=(units // TILE,),
        in_specs=in_specs,
        out_specs=out_specs,
        out_shape=out_shape,
        scratch_shapes=scratch,
        compiler_params=pltpu.CompilerParams(
            vmem_limit_bytes=VMEM_LIMIT, dimension_semantics=("arbitrary",)
        ),
        cost_estimate=pl.CostEstimate(
            flops=4 * count * features * units * 2, bytes_accessed=16 << 20, transcendentals=0
        ),
        name="ffn_backward",
    )(*ins)


def add_low(a, b):
    return (a.astype(f32) + b.astype(f32)).astype(bf16)


def scatter_ffn(own, other, order):
    bits = chip_bits()
    narrow = lax.axis_size("narrow")
    received = swap_wide(other().astype(bf16), 1)
    part = (own() + received.astype(f32)).astype(bf16)
    rows, columns = part.shape
    part = part.reshape((2,) * bits + (rows >> bits, columns))
    left = list(range(bits - 1, -1, -1))
    for bit in order:
        axis = left.index(bit)
        received = swap_wide(lax.index_in_dim(part, 1, axis, keepdims=False), 2 << bit)
        part = add_low(lax.index_in_dim(part, 0, axis, keepdims=False), received)
        left.remove(bit)
    part = part.reshape(rows >> bits, narrow, columns // narrow)
    total = part[:, 0].astype(f32)
    for s in range(1, narrow):
        total = total + shift_narrow(part[:, narrow - s], s).astype(f32)
    return total


def scatter_attn(own, other, order, chip, z, rows_each):
    bits = chip_bits()
    narrow = lax.axis_size("narrow")
    received = swap_wide(other().astype(bf16), 1)
    part = (own() + received.astype(f32)).astype(bf16)
    low_bits = bits - 2
    columns = part.shape[1] // 4
    part = part.reshape((2,) * low_bits + (narrow * rows_each, 2, 2, columns))
    names = list(range(low_bits - 1, -1, -1)) + [None, bits - 1, bits - 2, None]
    for bit in order:
        axis = names.index(bit)
        mine = bit_of(chip, bit)
        received = swap_wide(pick(part, axis, 1 - mine), 2 << bit)
        part = add_low(pick(part, axis, mine), received)
        names.pop(axis)
    part = part.reshape(narrow, rows_each, columns)
    total = pick(part, 0, z).astype(f32)
    for s in range(1, narrow):
        total = total + shift_narrow(pick(part, 0, lax.rem(z + s, narrow)), s).astype(f32)
    return total


def per_device(tokens, segment_ids, attn_weight, vectors, ffn_weight, ffn_bias, out_grad):
    wide, narrow = lax.axis_size("wide"), lax.axis_size("narrow")
    w, z = lax.axis_index("wide"), lax.axis_index("narrow")
    chip, core = lax.div(w, 2), lax.rem(w, 2)
    bits = chip_bits()
    up = list(range(bits))
    down = up[::-1]
    pos = jnp.stack([chip, core, z]).astype(jnp.int32)
    count, features = tokens.shape
    half = features // 2

    each, each_bias = vectors.shape[0], ffn_bias.shape[0]
    room = -(-(each + each_bias) // 128) * 128
    small = jnp.concatenate(
        [vectors, ffn_bias, jnp.zeros((room - each - each_bias,), bf16)]
    ).reshape(1, room)
    small = gather_narrow(small, 0)
    small = gather_chips(small, up).reshape(-1, room)
    small = jnp.concatenate([small, swap_wide(small, 1)], 0)
    slots = jnp.arange(wide * narrow)
    slot_core, slot_chip, slot_z = (
        slots // (wide * narrow // 2), (slots // narrow) % (wide // 2), slots % narrow,
    )
    slot_w = (slot_chip ^ chip) * 2 + (slot_core ^ core)
    whole_at = slot_w * narrow + lax.rem(z - slot_z + narrow, narrow)
    bias_at = slot_z * wide + slot_w
    spots = jnp.arange(wide * narrow)[:, None]
    vec_rows = dot((spots == whole_at[None, :]).astype(bf16), small[:, :each]).reshape(8, features)
    bias_rel = dot(
        (spots == bias_at[None, :]).astype(bf16), small[:, each : each + each_bias]
    ).reshape(narrow, CHUNKS, -1)
    bq, bv, bo, s1, bf, s2, g1, g2 = [vec_rows[i] for i in range(8)]
    slot_vec = to_slots(jnp.stack([g1, s1, bf, g2, s2, s2, s2, s2]), chip, core)
    dy = to_slots(out_grad, chip, core)

    rows_each = attn_weight.shape[0]
    halves = []
    for part, order in ((0, up), (1, down)):
        v = attn_weight[:, part * half : part * half + half].reshape(1, rows_each, half)
        v = gather_narrow(v, 0)
        v = gather_chips(v, order).reshape(wide // 2, narrow, rows_each, half)
        halves += [v, swap_wide(v, 1)]

    units = ffn_weight.shape[2] // CHUNKS
    ffn = []
    for c in range(CHUNKS):
        pair = []
        for which, order in ((0, up), (1, down)):
            v = ffn_weight[which, :, c * units : c * units + units]
            v = gather_narrow(v, 1)
            v = gather_chips(v, order).reshape(-1, narrow * units)
            pair.append((v, swap_wide(v, 1)))
        ffn.append(pair)

    biases = jnp.stack([bq, bv, bo, bo, bo, bo, bo, bo])
    q, k, v, probs, mixed, hidden = run_attend_forward(pos, tokens, segment_ids, biases, *halves)
    hidden = to_slots(hidden, chip, core)
    acts, slopes = [], []
    total = None
    for c in range(CHUNKS):
        b1 = bias_rel[:, c].reshape(1, -1)
        outs = run_ffn_forward(
            hidden, slot_vec, *ffn[c], b1, total, dy if c == CHUNKS - 1 else None
        )
        acts.append(outs[0])
        slopes.append(outs[1])
        rest = outs[2:]
        if c == 0:
            u_low = rest[0]
            rest = rest[1:]
        if c < CHUNKS - 1:
            total = rest[0]
    result, dh, dh_low, sums_two = rest
    result = from_slots(result, chip, core)

    grad_down = [
        scatter_ffn(
            functools.partial(dot_tn, dh_low[:, :half], acts[c]),
            functools.partial(dot_tn, dh_low[:, half:], acts[c]),
            down,
        )
        for c in range(CHUNKS)
    ]
    total = None
    das, dbs = [], []
    for c in range(CHUNKS):
        outs = run_ffn_backward(
            dh_low, *ffn[c], slopes[c], total, (dh, hidden, slot_vec) if c == CHUNKS - 1 else None
        )
        das.append(outs[0])
        dbs.append(outs[1])
        total = outs[2]
    grad_sum, sums_one = total, outs[3]
    grad_up = [
        scatter_ffn(
            functools.partial(dot_tn, u_low[:, :half], das[c]),
            functools.partial(dot_tn, u_low[:, half:], das[c]),
            up,
        )
        for c in range(CHUNKS)
    ]
    grad_ffn = jnp.stack(
        [jnp.concatenate(grad_up, -1), jnp.concatenate(grad_down, -1)]
    )

    grad_sum = from_slots(grad_sum, chip, core)
    grad_low = grad_sum.astype(bf16)

    def core_columns(v, which):
        t = v.reshape(count, -1, 2, narrow * rows_each)
        return pick(t, 2, which).reshape(count, half)

    x_own, x_oth = core_columns(tokens, core), core_columns(tokens, 1 - core)
    o_own, o_oth = core_columns(mixed, core), core_columns(mixed, 1 - core)
    grad_tokens = grad_sum
    grad_attn, bias_sums = [], []
    for part, order in ((0, down), (1, up)):
        grads, grad_tokens, bias_sum = run_attend_backward(
            part, pos, grad_sum, grad_tokens, q, k, v, probs, *halves
        )
        bias_sums.append(bias_sum)
        columns = slice(part * half, part * half + half)

        def weights(x_rows, o_rows, grads=grads, columns=columns):
            return jnp.concatenate(
                [dot_tn(x_rows, grads[m]) for m in range(3)]
                + [dot_tn(o_rows, grad_low[:, columns])],
                1,
            )

        grad_attn.append(
            scatter_attn(
                functools.partial(weights, x_own, o_own),
                functools.partial(weights, x_oth, o_oth),
                order, chip, z, rows_each,
            )
        )
    grad_attn = jnp.concatenate(grad_attn, 1)

    slot_sums = from_slots(jnp.concatenate([sums_one[:3], sums_two[:3]]), chip, core)
    gs1, gg1, gbo, gs2, gg2, gbf = [slot_sums[i] for i in range(6)]
    gbq = jnp.concatenate([bias_sums[0][0], bias_sums[1][0]])
    gbv = jnp.concatenate([bias_sums[0][1], bias_sums[1][1]])
    vec = jnp.concatenate([gbq, gbv, gbo, gs1, gbf, gs2, gg1, gg2]).reshape(wide, narrow, each)
    db = jnp.stack([d.reshape(narrow, -1) for d in dbs], 1).reshape(narrow, wide, each_bias)
    part = jnp.concatenate([vec, db.transpose(1, 0, 2)], 2)
    part = part.reshape((2,) * (bits + 1) + part.shape[1:])
    for bit in range(bits + 1):
        axis = bits - bit
        mine = bit_of(w, bit)
        part = pick(part, axis, mine) + swap_wide(pick(part, axis, 1 - mine), 1 << bit)
    at = lambda s: jnp.concatenate(
        [pick(part[:, :each], 0, lax.rem(z + s, narrow)), part[(narrow - s) % narrow, each:]]
    )
    tally = at(0)
    for s in range(1, narrow):
        tally = tally + shift_narrow(at(s), s)
    return (result, grad_tokens, grad_attn, tally[:each], grad_ffn, tally[each:])


def solution(mesh):
    return jax.shard_map(
        per_device,
        mesh=mesh,
        in_specs=(
            P(("wide", "narrow"), None),
            P(("wide", "narrow"), None),
            P(("wide", "narrow"), None),
            P(("wide", "narrow")),
            P(None, "wide", "narrow"),
            P(("narrow", "wide")),
            P(("wide", "narrow"), None),
        ),
        out_specs=(
            P(("wide", "narrow"), None),
            P(("wide", "narrow"), None),
            P(("wide", "narrow"), None),
            P(("wide", "narrow")),
            P(None, "wide", "narrow"),
            P(("narrow", "wide")),
        ),
        check_vma=False,
    )
```

```python
import functools

import jax
import jax.numpy as jnp
from jax import lax
from jax.experimental import pallas as pl
from jax.experimental.pallas import tpu as pltpu
from jax.sharding import PartitionSpec as P

HEADS = 16
HEAD = 64
SUBS = 4
VMEM_LIMIT = 56 * 1024 * 1024

f32 = jnp.float32
bf16 = jnp.bfloat16

NT = (((1,), (1,)), ((), ()))
TN = (((0,), (0,)), ((), ()))


def dot(a, b):
    return jnp.dot(a, b, preferred_element_type=f32)


def dot_nt(a, b):
    return lax.dot_general(a, b, NT, preferred_element_type=f32)


def dot_tn(a, b):
    return lax.dot_general(a, b, TN, preferred_element_type=f32)


def swap_wide(v, mask):
    size = lax.axis_size("wide")
    return lax.ppermute(v, "wide", [(w, w ^ mask) for w in range(size)])


def swap_narrow(v, mask):
    size = lax.axis_size("narrow")
    return lax.ppermute(v, "narrow", [(z, z ^ mask) for z in range(size)])


def chip_bits():
    return (lax.axis_size("wide") // 2).bit_length() - 1


def narrow_bits():
    return lax.axis_size("narrow").bit_length() - 1


def turned(index, bits):
    out = 0
    for bit in range(bits):
        out = out + ((index >> bit) & 1) * (1 << (bits - 1 - bit))
    return out


def gather_narrow(v, axis):
    for bit in reversed(range(narrow_bits())):
        v = jnp.concatenate([v, swap_narrow(v, 1 << bit)], axis)
    return v


def hop(v, done, bit):
    axis = sum(1 for b in done if b > bit)
    return jnp.stack([v, swap_wide(v, 2 << bit)], axis), done + [bit]


def bit_of(index, bit):
    return lax.rem(lax.div(index, 1 << bit), 2)


def pick(v, axis, index):
    return lax.dynamic_index_in_dim(v, index, axis, keepdims=False)


def to_slots(v, chip, core):
    bits = chip_bits()
    lead = v.shape[:-1]
    block = v.shape[-1] // lax.axis_size("wide")
    t = v.reshape(lead + (2,) * (bits + 1) + (block,))
    n = len(lead)
    for bit in range(bits):
        axis = n + bits - 1 - bit
        t = jnp.where(bit_of(chip, bit) == 1, jnp.flip(t, axis), t)
    t = jnp.where(core == 1, jnp.flip(t, n + bits), t)
    t = jnp.moveaxis(t, n + bits, n)
    return t.reshape(v.shape)


def from_slots(v, chip, core):
    bits = chip_bits()
    lead = v.shape[:-1]
    block = v.shape[-1] // lax.axis_size("wide")
    n = len(lead)
    t = v.reshape(lead + (2,) * (bits + 1) + (block,))
    t = jnp.moveaxis(t, n, n + bits)
    for bit in range(bits):
        axis = n + bits - 1 - bit
        t = jnp.where(bit_of(chip, bit) == 1, jnp.flip(t, axis), t)
    t = jnp.where(core == 1, jnp.flip(t, n + bits), t)
    return t.reshape(v.shape)


def slot_lanes(pos, block, wide, lanes):
    at = ((block % 2) ^ pos[1]) * (wide // 2) + ((block // 2) ^ pos[0])
    return pl.ds(pl.multiple_of(at * lanes, lanes), lanes)


def whole_lanes(pos, slot, wide, lanes):
    core, chip = divmod(slot, wide // 2)
    at = (chip ^ pos[0]) * 2 + (core ^ pos[1])
    return pl.ds(pl.multiple_of(at * lanes, lanes), lanes)


def permute_kernel(wide, pos, v_ref, out_ref):
    lanes = v_ref.shape[1] // wide
    for b in range(wide):
        out_ref[:, slot_lanes(pos, b, wide, lanes)] = v_ref[:, b * lanes : (b + 1) * lanes]


def to_slots_quick(v, pos, chip, core):
    wide = lax.axis_size("wide")
    if (v.shape[1] // wide) % 128:
        return to_slots(v, chip, core)
    return pl.pallas_call(
        functools.partial(permute_kernel, wide),
        in_specs=[pl.BlockSpec(memory_space=pltpu.SMEM), pl.BlockSpec(memory_space=pltpu.VMEM)],
        out_specs=pl.BlockSpec(memory_space=pltpu.VMEM),
        out_shape=jax.ShapeDtypeStruct(v.shape, v.dtype),
        name="permute",
    )(pos, v)


def after(v, *others):
    return lax.optimization_barrier((v,) + others)[0]


def load_rows(pos, geometry, own, other, matrix, first, count, place, sem):
    narrow, per_matrix, rows = geometry[:3]

    def body(j, carry):
        block = matrix * per_matrix + first + j
        w = block // narrow
        z = block % narrow
        chip = (w // 2) ^ pos[0]
        core = (w % 2) ^ pos[1]
        step = turned(z ^ pos[2], narrow.bit_length() - 1)

        @pl.when(core == 0)
        def _():
            pltpu.make_async_copy(own.at[chip, step, pl.ds(0, rows)], place(j), sem).start()

        @pl.when(core == 1)
        def _():
            pltpu.make_async_copy(other.at[chip, step, pl.ds(0, rows)], place(j), sem).start()

        return carry

    lax.fori_loop(0, count, body, 0)


def attend_forward(
    geometry, pos, x_ref, seg_row, seg_col, vec_ref, bo_ref, own_a, oth_a, own_b, oth_b,
    q_ref, k_ref, v_ref, p_ref, o_ref, h_ref, w_in, w_out, mask, sems,
):
    g = pl.program_id(0)
    steps = pl.num_programs(0)
    _, blocks, rows, wide = geometry
    sources = ((own_a, oth_a), (own_b, oth_b))

    @pl.when(g == 0)
    def _():
        for half in range(2):
            for m in range(3):
                load_rows(
                    pos, geometry, *sources[half], m, 0, blocks,
                    lambda j, half=half, m=m: w_in.at[half, m, pl.ds(pl.multiple_of(j * rows, rows), rows)],
                    sems.at[half],
                )
        for half in range(2):
            load_rows(
                pos, geometry, *sources[half], 3, 0, blocks,
                lambda j, half=half: w_out.at[half, pl.ds(pl.multiple_of(j * rows, rows), rows)],
                sems.at[2],
            )
        mask[...] = jnp.where(seg_col[...] == seg_row[...], 0.0, -1e30).astype(f32)
        pltpu.make_async_copy(w_in.at[0], w_in.at[0], sems.at[0]).wait()

    @pl.when(g == steps // 2)
    def _():
        pltpu.make_async_copy(w_in.at[1], w_in.at[1], sems.at[1]).wait()

    half = g // (steps // 2)
    columns = pl.ds(pl.multiple_of(lax.rem(g, steps // 2) * 256, 256), 256)
    x = x_ref[...]
    query = (dot(x, w_in[half, 0, :, columns]) + vec_ref[0:1, :]).astype(bf16)
    query = query * jnp.asarray(HEAD**-0.5, bf16)
    key = dot(x, w_in[half, 1, :, columns]).astype(bf16)
    value = (dot(x, w_in[half, 2, :, columns]) + vec_ref[1:2, :]).astype(bf16)
    q_ref[...] = query
    k_ref[...] = key
    v_ref[...] = value
    lane = lax.broadcasted_iota(jnp.int32, (1, 128), 1)
    for pair in range(2):
        part = slice(pair * 128, pair * 128 + 128)
        q2, k2, v2 = query[:, part], key[:, part], value[:, part]
        v2t = v2.T
        outs = []
        for sub in range(2):
            mine = (lane < HEAD) if sub == 0 else (lane >= HEAD)
            scores = dot_nt(k2, jnp.where(mine, q2, jnp.zeros_like(q2))) + mask[...]
            raised = jnp.exp(scores - jnp.max(scores, 0, keepdims=True))
            probs = (raised * (1.0 / jnp.sum(raised, 0, keepdims=True))).astype(bf16)
            p_ref[pair * 2 + sub] = probs
            outs.append(dot(v2t[sub * HEAD : sub * HEAD + HEAD], probs))
        mixed = jnp.concatenate(outs, 0).T.astype(bf16)
        o_ref[:, pl.ds(pl.multiple_of(g * 256 + pair * 128, 128), 128)] = mixed

    @pl.when(g == steps - 1)
    def _():
        pltpu.make_async_copy(w_out, w_out, sems.at[2]).wait()
        width = w_out.shape[2]
        lanes = 2 * width // wide
        for half in range(2):
            cols = slice(half * width, half * width + width)
            hidden = x_ref[:, cols].astype(f32) + dot(o_ref[...], w_out[half]) + bo_ref[0:1, cols]
            if lanes % 128:
                h_ref[:, cols] = hidden
            else:
                for b in range(wide // 2):
                    at = slot_lanes(pos, half * (wide // 2) + b, wide, lanes)
                    h_ref[:, at] = hidden[:, b * lanes : (b + 1) * lanes]


def run_attend_forward(pos, tokens, segment_ids, biases, own_a, oth_a, own_b, oth_b):
    count, features = tokens.shape
    rows = own_b.shape[2]
    geometry = (own_b.shape[1], features // rows, rows, own_b.shape[0] * 2)
    groups = features // 256
    whole = lambda *shape: pl.BlockSpec(shape, lambda g, pos: (0,) * len(shape))
    column = pl.BlockSpec((count, 256), lambda g, pos: (0, g))
    anywhere = pl.BlockSpec(memory_space=pl.ANY)
    width = features // 2
    return pl.pallas_call(
        functools.partial(attend_forward, geometry),
        grid_spec=pltpu.PrefetchScalarGridSpec(
            num_scalar_prefetch=1,
            grid=(groups,),
            in_specs=[
                whole(count, features), whole(1, count), whole(count, 1),
                pl.BlockSpec((8, 256), lambda g, pos: (0, g)), whole(8, features),
                anywhere, anywhere, anywhere, anywhere,
            ],
            out_specs=[
                column, column, column,
                pl.BlockSpec((4, count, count), lambda g, pos: (g, 0, 0)),
                whole(count, features), whole(count, features),
            ],
            scratch_shapes=[
                pltpu.VMEM((2, 3, features, width), bf16),
                pltpu.VMEM((2, features, width), bf16),
                pltpu.VMEM((count, count), f32),
                pltpu.SemaphoreType.DMA((3,)),
            ],
        ),
        out_shape=[
            jax.ShapeDtypeStruct((count, features), bf16),
            jax.ShapeDtypeStruct((count, features), bf16),
            jax.ShapeDtypeStruct((count, features), bf16),
            jax.ShapeDtypeStruct((HEADS, count, count), bf16),
            jax.ShapeDtypeStruct((count, features), bf16),
            jax.ShapeDtypeStruct((count, features), f32),
        ],
        compiler_params=pltpu.CompilerParams(
            vmem_limit_bytes=VMEM_LIMIT, dimension_semantics=("arbitrary",)
        ),
        cost_estimate=pl.CostEstimate(
            flops=2 * count * features * features * 8, bytes_accessed=24 << 20, transcendentals=0
        ),
        name="attend_forward",
    )(
        pos, tokens, segment_ids.reshape(1, count), segment_ids.reshape(count, 1),
        biases, biases[2:3] + jnp.zeros((8, 1), f32), own_a, oth_a, own_b, oth_b,
    )


def attend_backward(
    geometry, half, pos, dh_ref, add_ref, q_ref, k_ref, v_ref, p_ref, x_own, x_oth, o_own, o_oth,
    own_a, oth_a, own_b, oth_b, gown_ref, goth_ref, dx_ref, bias_ref, w_in, w_out, sems,
):
    g = pl.program_id(0)
    features = dh_ref.shape[1]
    _, blocks, rows, _ = geometry
    sources = ((own_a, oth_a), (own_b, oth_b))

    @pl.when(g == 0)
    def _():
        for part in range(2):
            load_rows(
                pos, geometry, *sources[part], 3, half * (blocks // 2), blocks // 2,
                lambda j, part=part: w_out.at[part, pl.ds(pl.multiple_of(j * rows, rows), rows)],
                sems.at[0],
            )
        for m in range(3):
            load_rows(
                pos, geometry, *sources[half], m, 0, blocks,
                lambda j, m=m: w_in.at[m, pl.ds(pl.multiple_of(j * rows, rows), rows)],
                sems.at[1],
            )
        pltpu.make_async_copy(w_out, w_out, sems.at[0]).wait()

    span = pl.ds(pl.multiple_of(g * 256, 256), 256)
    width = features // 2
    low = dh_ref[...].astype(bf16)
    grad_mixed = (
        dot_nt(low[:, :width], w_out[0, span, :]) + dot_nt(low[:, width:], w_out[1, span, :])
    ).astype(bf16)
    lane = lax.broadcasted_iota(jnp.int32, (1, 128), 1)
    lows = [[], [], []]
    sums = [[], []]
    for pair in range(2):
        part = slice(pair * 128, pair * 128 + 128)
        q2, k2, v2 = q_ref[:, part], k_ref[:, part], v_ref[:, part]
        do2 = grad_mixed[:, part]
        k2t = k2.T
        zero = jnp.zeros_like(q2)
        dv = dk = None
        dqs = []
        for sub in range(2):
            mine = (lane < HEAD) if sub == 0 else (lane >= HEAD)
            probs = p_ref[pair * 2 + sub]
            do_mine = jnp.where(mine, do2, zero)
            grad_probs = dot_nt(v2, do_mine)
            wide_probs = probs.astype(f32)
            inner = jnp.sum(wide_probs * grad_probs, 0, keepdims=True)
            grad_scores = (wide_probs * (grad_probs - inner)).astype(bf16)
            dv_part = dot(probs, do_mine)
            dk_part = dot(grad_scores, jnp.where(mine, q2, zero))
            dv = dv_part if dv is None else dv + dv_part
            dk = dk_part if dk is None else dk + dk_part
            dqs.append(dot(k2t[sub * HEAD : sub * HEAD + HEAD], grad_scores))
        dq = jnp.concatenate(dqs, 0).T * HEAD**-0.5
        sums[0].append(jnp.sum(dq, 0, keepdims=True))
        sums[1].append(jnp.sum(dv, 0, keepdims=True))
        for store, value in zip(lows, (dq, dk, dv)):
            store.append(value.astype(bf16))
    joined = [jnp.concatenate(s, 1) for s in lows]
    for m in range(3):
        goth_ref[m] = dot(x_oth[...], joined[m]).astype(bf16)
        gown_ref[m] = dot(x_own[...], joined[m]).astype(bf16)
    low = dh_ref[:, pl.ds(pl.multiple_of(half * width + g * 256, 256), 256)].astype(bf16)
    goth_ref[3] = dot(o_oth[...], low).astype(bf16)
    gown_ref[3] = dot(o_own[...], low).astype(bf16)
    bias_ref[...] = jnp.concatenate(
        [jnp.concatenate(s, 1) for s in sums] + [jnp.zeros((6, 256), f32)], 0
    )

    @pl.when(g == 0)
    def _():
        pltpu.make_async_copy(w_in, w_in, sems.at[1]).wait()
        dx_ref[...] = add_ref[...]

    dx_ref[...] += (
        dot_nt(joined[0], w_in[0, :, span])
        + dot_nt(joined[1], w_in[1, :, span])
        + dot_nt(joined[2], w_in[2, :, span])
    )


def run_attend_backward(half, pos, grad_sum, added, kept, rows_of, weights):
    q, k, v, probs = kept
    own_a, oth_a, own_b, oth_b = weights
    count, features = q.shape
    rows = own_b.shape[2]
    geometry = (own_b.shape[1], features // rows, rows, own_b.shape[0] * 2)
    groups = features // 512
    whole = lambda *shape: pl.BlockSpec(shape, lambda g, pos: (0,) * len(shape))
    column = pl.BlockSpec((count, 256), lambda g, pos: (0, half * groups + g))
    anywhere = pl.BlockSpec(memory_space=pl.ANY)
    width = features // 2
    return pl.pallas_call(
        functools.partial(attend_backward, geometry, half),
        grid_spec=pltpu.PrefetchScalarGridSpec(
            num_scalar_prefetch=1,
            grid=(groups,),
            in_specs=[
                whole(count, features), whole(count, features), column, column, column,
                pl.BlockSpec((4, count, count), lambda g, pos: (half * groups + g, 0, 0)),
                whole(width, count), whole(width, count), whole(width, count), whole(width, count),
                anywhere, anywhere, anywhere, anywhere,
            ],
            out_specs=[
                pl.BlockSpec((4, width, 256), lambda g, pos: (0, 0, g)),
                pl.BlockSpec((4, width, 256), lambda g, pos: (0, 0, g)),
                whole(count, features),
                pl.BlockSpec((8, 256), lambda g, pos: (0, g)),
            ],
            scratch_shapes=[
                pltpu.VMEM((3, features, width), bf16),
                pltpu.VMEM((2, width, width), bf16),
                pltpu.SemaphoreType.DMA((2,)),
            ],
        ),
        out_shape=[
            jax.ShapeDtypeStruct((4, width, width), bf16),
            jax.ShapeDtypeStruct((4, width, width), bf16),
            jax.ShapeDtypeStruct((count, features), f32),
            jax.ShapeDtypeStruct((8, width), f32),
        ],
        compiler_params=pltpu.CompilerParams(
            vmem_limit_bytes=VMEM_LIMIT, dimension_semantics=("arbitrary",)
        ),
        cost_estimate=pl.CostEstimate(
            flops=2 * count * features * features * 6, bytes_accessed=16 << 20, transcendentals=0
        ),
        name="attend_backward",
    )(pos, grad_sum, added, q, k, v, probs, *rows_of, own_a, oth_a, own_b, oth_b)


def moments(hidden):
    center = hidden - jnp.mean(hidden, -1, keepdims=True)
    return center, lax.rsqrt(jnp.mean(center * center, -1, keepdims=True) + 1e-12)


def norm_back(grad, normed, factor):
    return factor * (
        grad
        - jnp.mean(grad, -1, keepdims=True)
        - normed * jnp.mean(grad * normed, -1, keepdims=True)
    )


def gelu_pair(a):
    z = jnp.abs(a) * (0.5**0.5)
    t = 1.0 / (1.0 + 0.3275911 * z)
    poly = t * (
        0.127414796 + t * (-0.142248368 + t * (0.7107068705 + t * (-0.7265760135 + t * 0.5307027145)))
    )
    bell = jnp.exp(-0.5 * (a * a))
    tail = poly * bell
    phi = jnp.where(a >= 0, 1.0 - tail, tail)
    return a * phi, phi + a * (bell * 0.3989422804014327)


ROWS_AT_ONCE = 128


def row_blocks(count):
    return [slice(r, r + ROWS_AT_ONCE) for r in range(0, count, ROWS_AT_ONCE)]


def ffn_forward(first, last, wide, *refs):
    pos, *refs = refs
    h_ref, vec, w1a, w1b, w2a, w2b, b1 = refs[:7]
    refs = refs[7:]
    f_in = None if first else refs.pop(0)
    dy = refs.pop(0) if last else None
    act_ref, slope_ref = refs[:2]
    refs = refs[2:]
    u_out = refs.pop(0) if first else None
    if last:
        result, dh, dh_low, dh_turned, sums = refs[:5]
        refs = refs[5:]
        total, u_low = refs
    else:
        total, u_low = refs
    t = pl.program_id(0)
    count, features = h_ref.shape
    width = features // 2

    @pl.when(t == 0)
    def _():
        for r in row_blocks(count):
            center, factor = moments(h_ref[r, :])
            u_low[r, :] = (center * factor * (1.0 + vec[0:1, :]) + vec[1:2, :]).astype(bf16)
        if first:
            for r in row_blocks(count):
                u_out[:, r] = u_low[r, :].T
            total[...] = jnp.zeros_like(total)
        else:
            total[...] = f_in[...]

    a = dot(u_low[:, :width], w1a[...]) + dot(u_low[:, width:], w1b[...]) + b1[0:1, :]
    act, slope = gelu_pair(a)
    act = act.astype(bf16)
    act_ref[...] = act
    slope_ref[...] = slope.astype(bf16)
    total[:, :width] += dot_nt(act, w2a[...])
    total[:, width:] += dot_nt(act, w2b[...])
    if last:

        @pl.when(t == pl.num_programs(0) - 1)
        def _():
            sums[...] = jnp.zeros_like(sums)
            for r in row_blocks(count):
                center, factor = moments(h_ref[r, :])
                u = center * factor * (1.0 + vec[0:1, :]) + vec[1:2, :]
                center, factor = moments(u + total[r, :] + vec[2:3, :])
                normed = center * factor
                final = (normed * (1.0 + vec[3:4, :]) + vec[4:5, :]).astype(bf16)
                lanes = features // wide
                if lanes % 128:
                    result[r, :] = final
                else:
                    for slot in range(wide):
                        result[r, whole_lanes(pos, slot, wide, lanes)] = final[
                            :, slot * lanes : (slot + 1) * lanes
                        ]
                grad = dy[r, :].astype(f32)
                back = norm_back(grad * (1.0 + vec[3:4, :]), normed, factor)
                dh[r, :] = back
                low = back.astype(bf16)
                dh_low[r, :] = low
                dh_turned[:, r] = low.T
                sums[0:1, :] += jnp.sum(grad, 0, keepdims=True)
                sums[1:2, :] += jnp.sum(grad * normed, 0, keepdims=True)
                sums[2:3, :] += jnp.sum(back, 0, keepdims=True)


TILE = 512


def run_ffn_forward(pos, hidden, vec, w1, w2, b1, earlier, dy):
    count, features = hidden.shape
    width, units = w1[0].shape
    first, last = earlier is None, dy is not None
    whole = lambda *shape: pl.BlockSpec(shape, lambda t: (0,) * len(shape))
    tall = pl.BlockSpec((width, TILE), lambda t: (0, t))
    strip = pl.BlockSpec((count, TILE), lambda t: (0, t))
    ins = [pos, hidden, vec, w1[0], w1[1], w2[0], w2[1], b1]
    in_specs = [
        pl.BlockSpec(memory_space=pltpu.SMEM),
        whole(count, features), whole(8, features), tall, tall, tall, tall,
        pl.BlockSpec((1, TILE), lambda t: (0, t)),
    ]
    out_specs = [strip, strip]
    out_shape = [jax.ShapeDtypeStruct((count, units), bf16)] * 2
    scratch = [pltpu.VMEM((count, features), bf16)]
    if not first:
        ins.append(earlier)
        in_specs.append(whole(count, features))
    if last:
        ins.append(dy)
        in_specs.append(whole(count, features))
    if first:
        out_specs.append(whole(features, count))
        out_shape.append(jax.ShapeDtypeStruct((features, count), bf16))
    if last:
        out_specs += [whole(count, features)] * 3 + [whole(features, count), whole(8, features)]
        out_shape += [
            jax.ShapeDtypeStruct((count, features), bf16),
            jax.ShapeDtypeStruct((count, features), f32),
            jax.ShapeDtypeStruct((count, features), bf16),
            jax.ShapeDtypeStruct((features, count), bf16),
            jax.ShapeDtypeStruct((8, features), f32),
        ]
        scratch = [pltpu.VMEM((count, features), f32)] + scratch
    else:
        out_specs.append(whole(count, features))
        out_shape.append(jax.ShapeDtypeStruct((count, features), f32))
    return pl.pallas_call(
        functools.partial(ffn_forward, first, last, lax.axis_size("wide")),
        grid=(units // TILE,),
        in_specs=in_specs,
        out_specs=out_specs,
        out_shape=out_shape,
        scratch_shapes=scratch,
        compiler_params=pltpu.CompilerParams(
            vmem_limit_bytes=VMEM_LIMIT, dimension_semantics=("arbitrary",)
        ),
        cost_estimate=pl.CostEstimate(
            flops=4 * count * features * units * 2, bytes_accessed=16 << 20, transcendentals=0
        ),
        name="ffn_forward",
    )(*ins)


def ffn_backward(first, last, wide, *refs):
    pos, dh_low, dh_turned, u_turned, w1a, w1b, w2a, w2b, act, slope, *refs = refs
    du_in = None if first else refs.pop(0)
    if last:
        dh, h_ref, vec = refs[:3]
        refs = refs[3:]
    own_ref, oth_ref, db_ref = refs[:3]
    refs = refs[3:]
    if last:
        dh1, sums, total = refs
    else:
        (total,) = refs
    t = pl.program_id(0)
    count, features = dh_low.shape
    width = features // 2

    @pl.when(t == 0)
    def _():
        total[...] = jnp.zeros_like(total) if first else du_in[...]

    active = act[...]
    block = features // wide

    def store(ref, which, value):
        value = value.astype(bf16)
        for k in range(wide // 2):
            ref[k, which] = value[k * block : (k + 1) * block]

    store(oth_ref, 1, dot(dh_turned[width:, :], active))
    store(own_ref, 1, dot(dh_turned[:width, :], active))
    grad = dot(dh_low[:, :width], w2a[...]) + dot(dh_low[:, width:], w2b[...])
    grad = grad * slope[...].astype(f32)
    db_ref[...] = jnp.sum(grad, 0, keepdims=True)
    low = grad.astype(bf16)
    store(oth_ref, 0, dot(u_turned[width:, :], low))
    store(own_ref, 0, dot(u_turned[:width, :], low))
    total[:, :width] += dot_nt(low, w1a[...])
    total[:, width:] += dot_nt(low, w1b[...])
    if last:

        @pl.when(t == pl.num_programs(0) - 1)
        def _():
            sums[...] = jnp.zeros_like(sums)
            lanes = features // wide
            for r in row_blocks(count):
                center, factor = moments(h_ref[r, :])
                normed = center * factor
                du = total[r, :] + dh[r, :]
                back = norm_back(du * (1.0 + vec[0:1, :]), normed, factor)
                if lanes % 128:
                    dh1[r, :] = back
                else:
                    for slot in range(wide):
                        dh1[r, whole_lanes(pos, slot, wide, lanes)] = back[
                            :, slot * lanes : (slot + 1) * lanes
                        ]
                sums[0:1, :] += jnp.sum(du, 0, keepdims=True)
                sums[1:2, :] += jnp.sum(du * normed, 0, keepdims=True)
                sums[2:3, :] += jnp.sum(back, 0, keepdims=True)


def run_ffn_backward(sub, units, pos, dh_low, dh_turned, u_turned, w1, w2, act, slope, earlier, tail):
    count, features = dh_low.shape
    width = w1[0].shape[0]
    wide = lax.axis_size("wide")
    first, last = earlier is None, tail is not None
    tiles = units // TILE
    whole = lambda *shape: pl.BlockSpec(shape, lambda t: (0,) * len(shape))
    tall = pl.BlockSpec((width, TILE), lambda t: (0, sub * tiles + t))
    strip = pl.BlockSpec((count, TILE), lambda t: (0, sub * tiles + t))
    ins = [pos, dh_low, dh_turned, u_turned, w1[0], w1[1], w2[0], w2[1], act, slope]
    in_specs = [
        pl.BlockSpec(memory_space=pltpu.SMEM),
        whole(count, features), whole(features, count), whole(features, count),
        tall, tall, tall, tall, strip, strip,
    ]
    shape = (wide // 2, 2, features // wide, units)
    grads = pl.BlockSpec(shape[:3] + (TILE,), lambda t: (0, 0, 0, t))
    out_specs = [grads, grads, pl.BlockSpec((1, TILE), lambda t: (0, t))]
    out_shape = [
        jax.ShapeDtypeStruct(shape, bf16),
        jax.ShapeDtypeStruct(shape, bf16),
        jax.ShapeDtypeStruct((1, units), f32),
    ]
    scratch = []
    if not first:
        ins.append(earlier)
        in_specs.append(whole(count, features))
    if last:
        ins += list(tail)
        in_specs += [whole(count, features), whole(count, features), whole(8, features)]
        out_specs += [whole(count, features), whole(8, features)]
        out_shape += [
            jax.ShapeDtypeStruct((count, features), f32),
            jax.ShapeDtypeStruct((8, features), f32),
        ]
        scratch = [pltpu.VMEM((count, features), f32)]
    else:
        out_specs.append(whole(count, features))
        out_shape.append(jax.ShapeDtypeStruct((count, features), f32))
    return pl.pallas_call(
        functools.partial(ffn_backward, first, last, lax.axis_size("wide")),
        grid=(tiles,),
        in_specs=in_specs,
        out_specs=out_specs,
        out_shape=out_shape,
        scratch_shapes=scratch,
        compiler_params=pltpu.CompilerParams(
            vmem_limit_bytes=VMEM_LIMIT, dimension_semantics=("arbitrary",)
        ),
        cost_estimate=pl.CostEstimate(
            flops=8 * count * features * units, bytes_accessed=16 << 20, transcendentals=0
        ),
        name="ffn_backward",
    )(*ins)


def swap_hop(v, hop):
    kind, bit = hop
    return swap_wide(v, 2 << bit) if kind == "wide" else swap_narrow(v, 1 << bit)


class Scatter:
    def __init__(self, own, other, axes, mine, extra=None):
        self.parts = [(own, ())]
        self.other = other
        self.axes, self.mine = dict(axes), mine
        self.extra = [] if extra is None else [(extra[0], ())]
        self.extra_other = None if extra is None else extra[1]

    def cross(self):
        own = self.parts[0][0]
        self.parts.append((swap_wide(self.other, 1).reshape(own.shape), ()))
        if self.extra:
            self.extra.append((swap_wide(self.extra_other, 1), ()))

    def send(self, hop):
        self.hop = hop
        axis = self.axes.pop(hop, None)
        keep = 0 if axis is None else self.mine[hop]
        more = lambda parts, i: [(v, path + ((axis, i),)) for v, path in parts]
        self.leaving = low_of(more(self.parts, 1 - keep))
        self.parts = more(self.parts, keep)
        if self.extra:
            self.leaving = jnp.concatenate([self.leaving, low_of(more(self.extra, 1 - keep))], -2)
            self.extra = more(self.extra, keep)
        if axis is not None:
            self.axes = {h: a - (a > axis) for h, a in self.axes.items()}
        return self.leaving

    def receive(self):
        came = swap_hop(self.leaving, self.hop)
        if self.extra:
            rows = self.parts[0][0].shape[-2]
            self.extra.append((came[..., rows:, :], ()))
            came = came[..., :rows, :]
        self.parts.append((came, ()))

    def hold(self, *others):
        self.parts = [(after(v, *others), path) for v, path in self.parts]


def taken(part):
    v, path = part
    for axis, i in path:
        if axis is None:
            size = v.shape[-1] // 2
            v = v[..., i * size : i * size + size]
        elif isinstance(i, int):
            v = lax.index_in_dim(v, i, axis, keepdims=False)
        else:
            v = pick(v, axis, i)
    return v


def sum_of(parts, view=lambda v: v):
    return sum(view(taken(p)).astype(f32) for p in parts)


def low_of(parts, view=lambda v: v):
    return sum_of(parts, view).astype(bf16)


def per_device(tokens, segment_ids, attn_weight, vectors, ffn_weight, ffn_bias, out_grad):
    wide, narrow = lax.axis_size("wide"), lax.axis_size("narrow")
    w, z = lax.axis_index("wide"), lax.axis_index("narrow")
    chip, core = lax.div(w, 2), lax.rem(w, 2)
    bits = chip_bits()
    up = list(range(bits))
    down = up[::-1]
    pos = jnp.stack([chip, core, z]).astype(jnp.int32)
    count, features = tokens.shape
    half = features // 2

    rows_each = attn_weight.shape[0]
    each, each_bias = vectors.shape[0], ffn_bias.shape[0]
    small = jnp.concatenate([vectors, ffn_bias, jnp.zeros((features - each - each_bias,), bf16)])
    small = jnp.concatenate([small[None], jnp.zeros((7, features), bf16)])
    v = jnp.concatenate([attn_weight, small])
    attn_whole = gather_narrow(v[None], 0)
    units = ffn_weight.shape[2]
    width = units // SUBS
    tail = units - width
    orders = (up, down)

    def climb(trees, first, last, waits=()):
        for step in range(first, last):
            trees = [
                (*hop(after(v, *waits) if waits else v, done, order[step]), order)
                for v, done, order in trees
            ]
            waits = ()
        return trees

    late = climb([(ffn_weight[i, :, tail:], [], orders[i]) for i in range(2)], 0, bits)
    attn = [
        (attn_whole[:, :, :half], [], up),
        (attn_whole[:, :rows_each, half:], [], down),
    ]
    attn = climb(attn, 0, 1, [v for v, _, _ in late])
    early_whole = gather_narrow(after(ffn_weight[:, :, :tail], attn_whole), 2)
    v = jnp.stack([v.reshape(half, width) for v, _, _ in late])
    late_whole = gather_narrow(after(v, early_whole), 2)
    attn = climb(attn, 1, bits)
    halves = []
    for v, _, _ in attn:
        v = v.reshape((wide // 2,) + v.shape[bits:])
        halves += [v, swap_wide(v, 1)]
    early = [
        (
            jnp.concatenate(
                [
                    early_whole[which, :, at * tail + sub * width :][:, :width]
                    for sub in range(SUBS - 1)
                    for at in range(narrow)
                ],
                1,
            ),
            [],
            orders[which],
        )
        for which in range(2)
    ]
    early = climb(early, 0, 1, [halves[1], halves[3]])
    tokens_now = after(tokens, late_whole)
    early = climb(early, 1, bits)
    late = [(late_whole[which], swap_wide(late_whole[which], 1)) for which in range(2)]

    small = jnp.concatenate([h[:, :, rows_each, : each + each_bias] for h in halves[:2]])
    small = small.reshape(-1, each + each_bias)
    slots = jnp.arange(wide * narrow)
    slot_core, slot_chip, slot_z = (
        slots // (wide * narrow // 2), (slots // narrow) % (wide // 2), slots % narrow,
    )
    slot_w = (slot_chip ^ chip) * 2 + (slot_core ^ core)
    whole_at = slot_w * narrow + (turned(slot_z, narrow_bits()) ^ z)
    bias_at = slot_z * wide + slot_w
    spots = jnp.arange(wide * narrow)[:, None]
    vec_rows = dot((spots == whole_at[None, :]).astype(bf16), small[:, :each]).reshape(8, features)
    bias_rel = dot((spots == bias_at[None, :]).astype(bf16), small[:, each:])
    bias_rel = bias_rel.reshape(narrow, SUBS, width).transpose(1, 0, 2).reshape(SUBS, -1)
    bq, bv, bo, s1, bf, s2, g1, g2 = [vec_rows[i] for i in range(8)]
    slot_vec = to_slots_quick(jnp.stack([g1, s1, bf, g2, s2, s2, s2, s2]), pos, chip, core)
    dy = to_slots_quick(out_grad, pos, chip, core)
    in_kernel = (features // wide) % 128 == 0

    def core_rows(v, which):
        t = v.reshape(count, -1, 2, narrow * rows_each)
        return pick(t, 2, which).reshape(count, half).T

    x_rows = [core_rows(tokens, core), core_rows(tokens, 1 - core)]

    biases = jnp.stack([bq, bv, bo, bo, bo, bo, bo, bo])
    *kept, mixed, hidden = run_attend_forward(pos, tokens_now, segment_ids, biases, *halves)
    o_rows = [core_rows(mixed, core), core_rows(mixed, 1 - core)]
    hidden = after(hidden, *o_rows)
    if not in_kernel:
        hidden = to_slots(hidden, chip, core)
    early = [after(v.reshape(half, -1), hidden) for v, _, _ in early]
    early = [(v, swap_wide(v, 1)) for v in early]
    act_late, slope_late, u_turned, total = run_ffn_forward(
        pos, hidden, slot_vec, *late, bias_rel[-1].reshape(1, -1), None, None
    )
    act, slope, result, dh, dh_low, dh_turned, sums_two = run_ffn_forward(
        pos, hidden, slot_vec, *early, bias_rel[:-1].reshape(1, -1), total, dy
    )
    if not in_kernel:
        result = from_slots(result, chip, core)

    sources = [(0, late, act_late, slope_late)]
    sources += [(sub, early, act, slope) for sub in range(SUBS - 1)]
    total = None
    dbs, units = [], []
    chips = lambda order: [("wide", bit) for bit in order]
    along = [("narrow", bit) for bit in range(narrow_bits())]
    routes = [along + chips(down), chips(down), chips(up), chips(down)]
    low = dh_low
    for j, (sub, weights, active, steep) in enumerate(sources):
        outs = run_ffn_backward(
            sub, narrow * width, pos, low, dh_turned, u_turned, *weights, active, steep, total,
            (dh, hidden, slot_vec) if j == SUBS - 1 else None,
        )
        shape = (2,) * bits + outs[0].shape[1:]
        axes = {("wide", bit): bits - 1 - bit for bit in range(bits)}
        unit = Scatter(outs[0].reshape(shape), outs[1], axes, dict.fromkeys(axes, 0))
        unit.cross()
        units.append(unit)
        dbs.append(outs[2])
        total = outs[3]
        if j >= 1 and j < 3:
            low = after(low, units[j - 1].send(routes[j - 1][0]))
            units[j - 1].receive()
    grad_sum, sums_one = total, outs[4]
    if not in_kernel:
        grad_sum = from_slots(grad_sum, chip, core)

    low_bits = bits - 2
    names = chips([bits - 1, bits - 2] + list(range(low_bits))[::-1]) + along[::-1]
    attn_axes = {name: axis for axis, name in enumerate(names)}
    mine = {("wide", bit): bit_of(chip, bit) for bit in range(bits)}
    mine.update({("narrow", bit): bit_of(z, bit) for bit in range(narrow_bits())})
    added = grad_sum
    bias_sums, attn_units = [], []
    slot_sums = from_slots(jnp.concatenate([sums_one[:3], sums_two[:3]]), chip, core)
    gs1, gg1, gbo, gs2, gg2, gbf = [slot_sums[i] for i in range(6)]
    dbs = dbs[1:] + dbs[:1]
    db = jnp.stack([d.reshape(narrow, -1) for d in dbs], 1).reshape(narrow, wide, each_bias)
    at = turned(jnp.arange(narrow) ^ z, narrow_bits())
    db = jnp.stack([pick(db, 0, at[i]) for i in range(narrow)], 1)

    def small_rows():
        gbq = jnp.concatenate([bias_sums[0][0], bias_sums[1][0]])
        gbv = jnp.concatenate([bias_sums[0][1], bias_sums[1][1]])
        vec = jnp.concatenate([gbq, gbv, gbo, gs1, gbf, gs2, gg1, gg2]).reshape(wide, narrow, each)
        rows = jnp.concatenate([vec, db], 2)
        rows = jnp.pad(rows[:, :, None], ((0, 0), (0, 0), (0, 7), (0, half - each - each_bias)))
        rows = rows.astype(bf16).reshape((2,) * (bits + 1 + narrow_bits()) + rows.shape[2:])
        return pick(rows, bits, core), pick(rows, bits, 1 - core)

    waiting = [[(2, 0), (3, 0), (1, 1), (0, 1)], [(2, 1), (3, 1), (0, 2)]]
    for part in range(2):
        leaving = []
        for j, step in waiting[part]:
            leaving.append(units[j].send(routes[j][step]))
            units[j].receive()
        low = after(grad_sum, *leaving)
        own, other, added, bias_sum = run_attend_backward(
            part, pos, low, added, kept, x_rows + o_rows, halves
        )
        bias_sums.append(bias_sum)
        shape = (2,) * len(names) + (rows_each, half)
        unit = Scatter(
            own.reshape(shape), other, attn_axes, mine, None if part == 0 else small_rows()
        )
        unit.cross()
        attn_units.append(unit)
    grad_tokens = added

    for unit in units:
        unit.hold(added)
    for unit, route in zip(units, routes):
        for hop_to in route[3 if unit is units[0] else 2 :]:
            unit.send(hop_to)
            unit.receive()
    rest = units[1:]
    for hop_to in along:
        leaving = [u.send(hop_to) for u in rest]
        came = swap_hop(jnp.concatenate(leaving, -1), hop_to)
        size = leaving[0].shape[-1]
        for i, u in enumerate(rest):
            u.parts.append((came[..., i * size : i * size + size], ()))
    grad_ffn = jnp.concatenate([sum_of(u.parts) for u in rest + units[:1]], -1)
    for step in range(bits + len(along)):
        for unit, order in zip(attn_units, (down, up)):
            unit.send((chips(order) + along)[step])
            unit.receive()
    grad_attn = jnp.concatenate([sum_of(u.parts) for u in attn_units], -1)
    tally = sum_of(attn_units[1].extra)[0]
    return (
        result, grad_tokens, grad_attn, tally[:each], grad_ffn, tally[each : each + each_bias],
    )


def solution(mesh):
    return jax.shard_map(
        per_device,
        mesh=mesh,
        in_specs=(
            P(("wide", "narrow"), None),
            P(("wide", "narrow"), None),
            P(("wide", "narrow"), None),
            P(("wide", "narrow")),
            P(None, "wide", "narrow"),
            P(("narrow", "wide")),
            P(("wide", "narrow"), None),
        ),
        out_specs=(
            P(("wide", "narrow"), None),
            P(("wide", "narrow"), None),
            P(("wide", "narrow"), None),
            P(("wide", "narrow")),
            P(None, "wide", "narrow"),
            P(("narrow", "wide")),
        ),
        check_vma=False,
    )
```

```python
import functools

import jax
import jax.numpy as jnp
from jax import lax
from jax.experimental import pallas as pl
from jax.experimental.pallas import tpu as pltpu
from jax.sharding import PartitionSpec as P

HEADS = 16
HEAD = 64
SUBS = 4
VMEM_LIMIT = 56 * 1024 * 1024
FFN_LIMIT = 56 * 1024 * 1024

f32 = jnp.float32
bf16 = jnp.bfloat16

NT = (((1,), (1,)), ((), ()))
TN = (((0,), (0,)), ((), ()))


def dot(a, b):
    return jnp.dot(a, b, preferred_element_type=f32)


def dot_nt(a, b):
    return lax.dot_general(a, b, NT, preferred_element_type=f32)


def dot_tn(a, b):
    return lax.dot_general(a, b, TN, preferred_element_type=f32)


def swap_wide(v, mask):
    size = lax.axis_size("wide")
    return lax.ppermute(v, "wide", [(w, w ^ mask) for w in range(size)])


def swap_narrow(v, mask):
    size = lax.axis_size("narrow")
    return lax.ppermute(v, "narrow", [(z, z ^ mask) for z in range(size)])


def chip_bits():
    return (lax.axis_size("wide") // 2).bit_length() - 1


def narrow_bits():
    return lax.axis_size("narrow").bit_length() - 1


def turned(index, bits):
    out = 0
    for bit in range(bits):
        out = out + ((index >> bit) & 1) * (1 << (bits - 1 - bit))
    return out


def gather_narrow(v, axis):
    for bit in reversed(range(narrow_bits())):
        v = jnp.concatenate([v, swap_narrow(v, 1 << bit)], axis)
    return v


def hop(v, done, bit):
    axis = sum(1 for b in done if b > bit)
    return jnp.stack([v, swap_wide(v, 2 << bit)], axis), done + [bit]


def bit_of(index, bit):
    return lax.rem(lax.div(index, 1 << bit), 2)


def pick(v, axis, index):
    return lax.dynamic_index_in_dim(v, index, axis, keepdims=False)


def to_slots(v, chip, core):
    bits = chip_bits()
    lead = v.shape[:-1]
    block = v.shape[-1] // lax.axis_size("wide")
    t = v.reshape(lead + (2,) * (bits + 1) + (block,))
    n = len(lead)
    for bit in range(bits):
        axis = n + bits - 1 - bit
        t = jnp.where(bit_of(chip, bit) == 1, jnp.flip(t, axis), t)
    t = jnp.where(core == 1, jnp.flip(t, n + bits), t)
    t = jnp.moveaxis(t, n + bits, n)
    return t.reshape(v.shape)


def from_slots(v, chip, core):
    bits = chip_bits()
    lead = v.shape[:-1]
    block = v.shape[-1] // lax.axis_size("wide")
    n = len(lead)
    t = v.reshape(lead + (2,) * (bits + 1) + (block,))
    t = jnp.moveaxis(t, n, n + bits)
    for bit in range(bits):
        axis = n + bits - 1 - bit
        t = jnp.where(bit_of(chip, bit) == 1, jnp.flip(t, axis), t)
    t = jnp.where(core == 1, jnp.flip(t, n + bits), t)
    return t.reshape(v.shape)


def slot_lanes(pos, block, wide, lanes):
    at = ((block % 2) ^ pos[1]) * (wide // 2) + ((block // 2) ^ pos[0])
    return pl.ds(pl.multiple_of(at * lanes, lanes), lanes)


def whole_lanes(pos, slot, wide, lanes):
    core, chip = divmod(slot, wide // 2)
    at = (chip ^ pos[0]) * 2 + (core ^ pos[1])
    return pl.ds(pl.multiple_of(at * lanes, lanes), lanes)


def permute_kernel(wide, pos, v_ref, out_ref):
    lanes = v_ref.shape[1] // wide
    for b in range(wide):
        out_ref[:, slot_lanes(pos, b, wide, lanes)] = v_ref[:, b * lanes : (b + 1) * lanes]


def to_slots_quick(v, pos, chip, core):
    wide = lax.axis_size("wide")
    if (v.shape[1] // wide) % 128:
        return to_slots(v, chip, core)
    return pl.pallas_call(
        functools.partial(permute_kernel, wide),
        in_specs=[pl.BlockSpec(memory_space=pltpu.SMEM), pl.BlockSpec(memory_space=pltpu.VMEM)],
        out_specs=pl.BlockSpec(memory_space=pltpu.VMEM),
        out_shape=jax.ShapeDtypeStruct(v.shape, v.dtype),
        name="permute",
    )(pos, v)


def tie(*values):
    return lax.optimization_barrier(values)


def load_rows(pos, geometry, own, other, matrix, first, count, place, sem):
    narrow, per_matrix, rows = geometry[:3]

    def body(j, carry):
        block = matrix * per_matrix + first + j
        w = block // narrow
        z = block % narrow
        chip = (w // 2) ^ pos[0]
        core = (w % 2) ^ pos[1]
        step = turned(z ^ pos[2], narrow.bit_length() - 1)

        @pl.when(core == 0)
        def _():
            pltpu.make_async_copy(own.at[chip, step, pl.ds(0, rows)], place(j), sem).start()

        @pl.when(core == 1)
        def _():
            pltpu.make_async_copy(other.at[chip, step, pl.ds(0, rows)], place(j), sem).start()

        return carry

    lax.fori_loop(0, count, body, 0)


def attend_forward(
    geometry, pos, x_ref, seg_row, seg_col, vec_ref, bo_ref, own_a, oth_a, own_b, oth_b,
    q_ref, k_ref, v_ref, p_ref, o_ref, h_ref, w_in, w_out, mask, sems,
):
    g = pl.program_id(0)
    steps = pl.num_programs(0)
    _, blocks, rows, wide = geometry
    sources = ((own_a, oth_a), (own_b, oth_b))

    @pl.when(g == 0)
    def _():
        for half in range(2):
            for m in range(3):
                load_rows(
                    pos, geometry, *sources[half], m, 0, blocks,
                    lambda j, half=half, m=m: w_in.at[half, m, pl.ds(pl.multiple_of(j * rows, rows), rows)],
                    sems.at[half],
                )
        for half in range(2):
            load_rows(
                pos, geometry, *sources[half], 3, 0, blocks,
                lambda j, half=half: w_out.at[half, pl.ds(pl.multiple_of(j * rows, rows), rows)],
                sems.at[2],
            )
        mask[...] = jnp.where(seg_col[...] == seg_row[...], 0.0, -1e30).astype(f32)
        pltpu.make_async_copy(w_in.at[0], w_in.at[0], sems.at[0]).wait()

    @pl.when(g == steps // 2)
    def _():
        pltpu.make_async_copy(w_in.at[1], w_in.at[1], sems.at[1]).wait()

    half = g // (steps // 2)
    columns = pl.ds(pl.multiple_of(lax.rem(g, steps // 2) * 256, 256), 256)
    x = x_ref[...]
    query = (dot(x, w_in[half, 0, :, columns]) + vec_ref[0:1, :]).astype(bf16)
    query = query * jnp.asarray(HEAD**-0.5, bf16)
    key = dot(x, w_in[half, 1, :, columns]).astype(bf16)
    value = (dot(x, w_in[half, 2, :, columns]) + vec_ref[1:2, :]).astype(bf16)
    q_ref[...] = query
    k_ref[...] = key
    v_ref[...] = value
    lane = lax.broadcasted_iota(jnp.int32, (1, 128), 1)
    for pair in range(2):
        part = slice(pair * 128, pair * 128 + 128)
        q2, k2, v2 = query[:, part], key[:, part], value[:, part]
        v2t = v2.T
        outs = []
        for sub in range(2):
            mine = (lane < HEAD) if sub == 0 else (lane >= HEAD)
            scores = dot_nt(k2, jnp.where(mine, q2, jnp.zeros_like(q2))) + mask[...]
            raised = jnp.exp(scores - jnp.max(scores, 0, keepdims=True))
            probs = (raised * (1.0 / jnp.sum(raised, 0, keepdims=True))).astype(bf16)
            p_ref[pair * 2 + sub] = probs
            outs.append(dot(v2t[sub * HEAD : sub * HEAD + HEAD], probs))
        mixed = jnp.concatenate(outs, 0).T.astype(bf16)
        o_ref[:, pl.ds(pl.multiple_of(g * 256 + pair * 128, 128), 128)] = mixed

    @pl.when(g == steps - 1)
    def _():
        pltpu.make_async_copy(w_out, w_out, sems.at[2]).wait()
        width = w_out.shape[2]
        lanes = 2 * width // wide
        for half in range(2):
            cols = slice(half * width, half * width + width)
            hidden = x_ref[:, cols].astype(f32) + dot(o_ref[...], w_out[half]) + bo_ref[0:1, cols]
            if lanes % 128:
                h_ref[:, cols] = hidden
            else:
                for b in range(wide // 2):
                    at = slot_lanes(pos, half * (wide // 2) + b, wide, lanes)
                    h_ref[:, at] = hidden[:, b * lanes : (b + 1) * lanes]


def run_attend_forward(pos, tokens, segment_ids, biases, own_a, oth_a, own_b, oth_b):
    count, features = tokens.shape
    rows = own_b.shape[2]
    geometry = (own_b.shape[1], features // rows, rows, own_b.shape[0] * 2)
    groups = features // 256
    whole = lambda *shape: pl.BlockSpec(shape, lambda g, pos: (0,) * len(shape))
    column = pl.BlockSpec((count, 256), lambda g, pos: (0, g))
    anywhere = pl.BlockSpec(memory_space=pl.ANY)
    width = features // 2
    return pl.pallas_call(
        functools.partial(attend_forward, geometry),
        grid_spec=pltpu.PrefetchScalarGridSpec(
            num_scalar_prefetch=1,
            grid=(groups,),
            in_specs=[
                whole(count, features), whole(1, count), whole(count, 1),
                pl.BlockSpec((8, 256), lambda g, pos: (0, g)), whole(8, features),
                anywhere, anywhere, anywhere, anywhere,
            ],
            out_specs=[
                column, column, column,
                pl.BlockSpec((4, count, count), lambda g, pos: (g, 0, 0)),
                whole(count, features), whole(count, features),
            ],
            scratch_shapes=[
                pltpu.VMEM((2, 3, features, width), bf16),
                pltpu.VMEM((2, features, width), bf16),
                pltpu.VMEM((count, count), f32),
                pltpu.SemaphoreType.DMA((3,)),
            ],
        ),
        out_shape=[
            jax.ShapeDtypeStruct((count, features), bf16),
            jax.ShapeDtypeStruct((count, features), bf16),
            jax.ShapeDtypeStruct((count, features), bf16),
            jax.ShapeDtypeStruct((HEADS, count, count), bf16),
            jax.ShapeDtypeStruct((count, features), bf16),
            jax.ShapeDtypeStruct((count, features), f32),
        ],
        compiler_params=pltpu.CompilerParams(
            vmem_limit_bytes=VMEM_LIMIT, dimension_semantics=("arbitrary",)
        ),
        cost_estimate=pl.CostEstimate(
            flops=2 * count * features * features * 8, bytes_accessed=24 << 20, transcendentals=0
        ),
        name="attend_forward",
    )(
        pos, tokens, segment_ids.reshape(1, count), segment_ids.reshape(count, 1),
        biases, biases[2:3] + jnp.zeros((8, 1), f32), own_a, oth_a, own_b, oth_b,
    )


def attend_backward(
    geometry, half, pos, dh_ref, add_ref, sums_in, q_ref, k_ref, v_ref, p_ref, x_own, x_oth, o_own, o_oth,
    own_a, oth_a, own_b, oth_b, gown_ref, goth_ref, dx_ref, bias_ref, w_in, w_out, sems,
):
    g = pl.program_id(0)
    features = dh_ref.shape[1]
    _, blocks, rows, _ = geometry
    sources = ((own_a, oth_a), (own_b, oth_b))

    @pl.when(g == 0)
    def _():
        for part in range(2):
            load_rows(
                pos, geometry, *sources[part], 3, half * (blocks // 2), blocks // 2,
                lambda j, part=part: w_out.at[part, pl.ds(pl.multiple_of(j * rows, rows), rows)],
                sems.at[0],
            )
        for m in range(3):
            load_rows(
                pos, geometry, *sources[half], m, 0, blocks,
                lambda j, m=m: w_in.at[m, pl.ds(pl.multiple_of(j * rows, rows), rows)],
                sems.at[1],
            )
        pltpu.make_async_copy(w_out, w_out, sems.at[0]).wait()

    span = pl.ds(pl.multiple_of(g * 256, 256), 256)
    width = features // 2
    low = dh_ref[...].astype(bf16)
    grad_mixed = (
        dot_nt(low[:, :width], w_out[0, span, :]) + dot_nt(low[:, width:], w_out[1, span, :])
    ).astype(bf16)
    lane = lax.broadcasted_iota(jnp.int32, (1, 128), 1)
    lows = [[], [], []]
    sums = [[], []]
    for pair in range(2):
        part = slice(pair * 128, pair * 128 + 128)
        q2, k2, v2 = q_ref[:, part], k_ref[:, part], v_ref[:, part]
        do2 = grad_mixed[:, part]
        k2t = k2.T
        zero = jnp.zeros_like(q2)
        dv = dk = None
        dqs = []
        for sub in range(2):
            mine = (lane < HEAD) if sub == 0 else (lane >= HEAD)
            probs = p_ref[pair * 2 + sub]
            do_mine = jnp.where(mine, do2, zero)
            grad_probs = dot_nt(v2, do_mine)
            wide_probs = probs.astype(f32)
            inner = jnp.sum(wide_probs * grad_probs, 0, keepdims=True)
            grad_scores = (wide_probs * (grad_probs - inner)).astype(bf16)
            dv_part = dot(probs, do_mine)
            dk_part = dot(grad_scores, jnp.where(mine, q2, zero))
            dv = dv_part if dv is None else dv + dv_part
            dk = dk_part if dk is None else dk + dk_part
            dqs.append(dot(k2t[sub * HEAD : sub * HEAD + HEAD], grad_scores))
        dq = jnp.concatenate(dqs, 0).T * HEAD**-0.5
        sums[0].append(jnp.sum(dq, 0, keepdims=True))
        sums[1].append(jnp.sum(dv, 0, keepdims=True))
        for store, value in zip(lows, (dq, dk, dv)):
            store.append(value.astype(bf16))
    joined = [jnp.concatenate(s, 1) for s in lows]
    for m in range(3):
        goth_ref[m] = dot(x_oth[...], joined[m]).astype(bf16)
        gown_ref[m] = dot(x_own[...], joined[m]).astype(bf16)
    low = dh_ref[:, pl.ds(pl.multiple_of(half * width + g * 256, 256), 256)].astype(bf16)
    goth_ref[3] = dot(o_oth[...], low).astype(bf16)
    gown_ref[3] = dot(o_own[...], low).astype(bf16)
    @pl.when(g == 0)
    def _():
        bias_ref[...] = sums_in[...]

    for row in range(2):
        at = pl.ds(pl.multiple_of(half * width + g * 256, 256), 256)
        bias_ref[row : row + 1, at] = jnp.concatenate(sums[row], 1)

    @pl.when(g == 0)
    def _():
        pltpu.make_async_copy(w_in, w_in, sems.at[1]).wait()
        dx_ref[...] = add_ref[...]

    dx_ref[...] += (
        dot_nt(joined[0], w_in[0, :, span])
        + dot_nt(joined[1], w_in[1, :, span])
        + dot_nt(joined[2], w_in[2, :, span])
    )


def run_attend_backward(half, pos, grad_sum, added, sums, kept, rows_of, weights):
    q, k, v, probs = kept
    own_a, oth_a, own_b, oth_b = weights
    count, features = q.shape
    rows = own_b.shape[2]
    geometry = (own_b.shape[1], features // rows, rows, own_b.shape[0] * 2)
    groups = features // 512
    whole = lambda *shape: pl.BlockSpec(shape, lambda g, pos: (0,) * len(shape))
    column = pl.BlockSpec((count, 256), lambda g, pos: (0, half * groups + g))
    anywhere = pl.BlockSpec(memory_space=pl.ANY)
    width = features // 2
    return pl.pallas_call(
        functools.partial(attend_backward, geometry, half),
        grid_spec=pltpu.PrefetchScalarGridSpec(
            num_scalar_prefetch=1,
            grid=(groups,),
            in_specs=[
                whole(count, features), whole(count, features), whole(8, features), column, column,
                column,
                pl.BlockSpec((4, count, count), lambda g, pos: (half * groups + g, 0, 0)),
                whole(width, count), whole(width, count), whole(width, count), whole(width, count),
                anywhere, anywhere, anywhere, anywhere,
            ],
            out_specs=[
                pl.BlockSpec((4, width, 256), lambda g, pos: (0, 0, g)),
                pl.BlockSpec((4, width, 256), lambda g, pos: (0, 0, g)),
                whole(count, features),
                whole(8, features),
            ],
            scratch_shapes=[
                pltpu.VMEM((3, features, width), bf16),
                pltpu.VMEM((2, width, width), bf16),
                pltpu.SemaphoreType.DMA((2,)),
            ],
        ),
        out_shape=[
            jax.ShapeDtypeStruct((4, width, width), bf16),
            jax.ShapeDtypeStruct((4, width, width), bf16),
            jax.ShapeDtypeStruct((count, features), f32),
            jax.ShapeDtypeStruct((8, features), f32),
        ],
        compiler_params=pltpu.CompilerParams(
            vmem_limit_bytes=VMEM_LIMIT, dimension_semantics=("arbitrary",)
        ),
        cost_estimate=pl.CostEstimate(
            flops=2 * count * features * features * 6, bytes_accessed=16 << 20, transcendentals=0
        ),
        name="attend_backward",
    )(pos, grad_sum, added, sums, q, k, v, probs, *rows_of, own_a, oth_a, own_b, oth_b)


def moments(hidden):
    center = hidden - jnp.mean(hidden, -1, keepdims=True)
    return center, lax.rsqrt(jnp.mean(center * center, -1, keepdims=True) + 1e-12)


def norm_back(grad, normed, factor):
    return factor * (
        grad
        - jnp.mean(grad, -1, keepdims=True)
        - normed * jnp.mean(grad * normed, -1, keepdims=True)
    )


def gelu_pair(a):
    z = jnp.abs(a) * (0.5**0.5)
    t = 1.0 / (1.0 + 0.3275911 * z)
    poly = t * (
        0.127414796 + t * (-0.142248368 + t * (0.7107068705 + t * (-0.7265760135 + t * 0.5307027145)))
    )
    bell = jnp.exp(-0.5 * (a * a))
    tail = poly * bell
    phi = jnp.where(a >= 0, 1.0 - tail, tail)
    return a * phi, phi + a * (bell * 0.3989422804014327)


ROWS_AT_ONCE = 128
TILE = 1024


def row_blocks(count, step=ROWS_AT_ONCE):
    return [slice(r, r + step) for r in range(0, count, step)]


def turn_into_whole(ref, rows, value, pos, wide):
    features = value.shape[1]
    lanes = features // wide
    if lanes % 128:
        ref[rows, :] = value
    else:
        for slot in range(wide):
            ref[rows, whole_lanes(pos, slot, wide, lanes)] = value[
                :, slot * lanes : (slot + 1) * lanes
            ]


def store_blocks(ref, turned_rows, right):
    chips, block = ref.shape[0], ref.shape[1]
    step = max(1, 256 // block)
    for k in range(0, chips, step):
        value = dot(turned_rows[k * block : (k + step) * block, :], right).astype(bf16)
        for i in range(step):
            ref[k + i] = value[i * block : (i + 1) * block]


def once(*shape):
    return pl.BlockSpec(
        shape, lambda t: (0,) * len(shape), pipeline_mode=pl.Buffered(buffer_count=1)
    )


def ffn_forward(
    wide, tiles, pos, h_ref, vec, dy, b1, l1a, l1b, l2a, l2b, e1a, e1b, e2a, e2b,
    slope_ref, act_ref, u_out, result, dh, dh_low, dh_own, sums, oth_ref,
    total, u_low, act_all, dh_turned,
):
    t = pl.program_id(0)
    count, features = h_ref.shape
    width = features // 2

    @pl.when(t == 0)
    def _():
        for r in row_blocks(count):
            center, factor = moments(h_ref[r, :])
            low = (center * factor * (1.0 + vec[0:1, :]) + vec[1:2, :]).astype(bf16)
            u_low[r, :] = low
            u_out[:, r] = low.T

    def tile(w1a, w1b, w2a, w2b, first):
        columns = pl.ds(pl.multiple_of(t * TILE, TILE), TILE)
        for r in row_blocks(count, 256):
            a = dot(u_low[r, :width], w1a[...]) + dot(u_low[r, width:], w1b[...]) + b1[0:1, columns]
            act, slope = gelu_pair(a)
            act = act.astype(bf16)
            act_all[r, columns] = act
            act_ref[r, :] = act
            slope_ref[r, :] = slope.astype(bf16)
            left, right = dot_nt(act, w2a[...]), dot_nt(act, w2b[...])
            if first:
                total[r, :width] = left
                total[r, width:] = right
            else:
                total[r, :width] += left
                total[r, width:] += right

    @pl.when(t == 0)
    def _():
        tile(l1a, l1b, l2a, l2b, True)

    @pl.when((t > 0) & (t < tiles))
    def _():
        tile(e1a, e1b, e2a, e2b, False)

    @pl.when(t == tiles - 1)
    def _():
        sums[...] = jnp.zeros_like(sums)
        for r in row_blocks(count):
            center, factor = moments(h_ref[r, :])
            u = center * factor * (1.0 + vec[0:1, :]) + vec[1:2, :]
            center, factor = moments(u + total[r, :] + vec[2:3, :])
            normed = center * factor
            final = (normed * (1.0 + vec[3:4, :]) + vec[4:5, :]).astype(bf16)
            turn_into_whole(result, r, final, pos, wide)
            grad = dy[r, :].astype(f32)
            back = norm_back(grad * (1.0 + vec[3:4, :]), normed, factor)
            dh[r, :] = back
            low = back.astype(bf16)
            dh_low[r, :] = low
            dh_own[:, r] = low[:, :width].T
            dh_turned[:, r] = low[:, width:].T
            sums[0:1, :] += jnp.sum(grad, 0, keepdims=True)
            sums[1:2, :] += jnp.sum(grad * normed, 0, keepdims=True)
            sums[2:3, :] += jnp.sum(back, 0, keepdims=True)

    @pl.when(t >= tiles)
    def _():
        columns = pl.ds(pl.multiple_of((t - tiles) * TILE, TILE), TILE)
        store_blocks(oth_ref, dh_turned[...], act_all[:, columns])


def down_kernel(left, right, out_ref):
    store_blocks(out_ref, left[...], right[...])


def run_down(dh_own, act):
    width, count = dh_own.shape
    units = act.shape[1]
    wide = lax.axis_size("wide")
    block = 2 * width // wide
    return pl.pallas_call(
        down_kernel,
        grid=(units // TILE,),
        in_specs=[once(width, count), pl.BlockSpec((count, TILE), lambda t: (0, t))],
        out_specs=pl.BlockSpec((wide // 2, block, TILE), lambda t: (0, 0, t)),
        out_shape=jax.ShapeDtypeStruct((wide // 2, block, units), bf16),
        compiler_params=pltpu.CompilerParams(
            vmem_limit_bytes=24 << 20, dimension_semantics=("arbitrary",)
        ),
        cost_estimate=pl.CostEstimate(
            flops=2 * count * width * units, bytes_accessed=9 << 20, transcendentals=0
        ),
        name="down_own",
    )(dh_own, act)


def run_ffn_forward(pos, hidden, vec, dy, b1, late, early):
    count, features = hidden.shape
    wide = lax.axis_size("wide")
    width = features // 2
    units = b1.shape[1]
    tiles = units // TILE
    block = features // wide
    tall = pl.BlockSpec((width, TILE), lambda t: (0, jnp.clip(t - 1, 0, tiles - 2)))
    grads = pl.BlockSpec((wide // 2, block, TILE), lambda t: (0, 0, jnp.maximum(t - tiles, 0)))
    grad_shape = jax.ShapeDtypeStruct((wide // 2, block, units), bf16)
    return pl.pallas_call(
        functools.partial(ffn_forward, wide, tiles),
        grid=(2 * tiles,),
        in_specs=[
            pl.BlockSpec(memory_space=pltpu.SMEM), once(count, features), once(8, features),
            once(count, features), once(1, units),
        ] + [once(width, TILE)] * 4 + [tall] * 4,
        out_specs=[
            pl.BlockSpec((count, TILE), lambda t: (0, jnp.minimum(t, tiles - 1))),
            pl.BlockSpec((count, TILE), lambda t: (0, jnp.minimum(t, tiles - 1))),
            once(features, count), once(count, features), once(count, features),
            once(count, features), once(width, count), once(8, features), grads,
        ],
        out_shape=[
            jax.ShapeDtypeStruct((count, units), bf16),
            jax.ShapeDtypeStruct((count, units), bf16),
            jax.ShapeDtypeStruct((features, count), bf16),
            jax.ShapeDtypeStruct((count, features), bf16),
            jax.ShapeDtypeStruct((count, features), f32),
            jax.ShapeDtypeStruct((count, features), bf16),
            jax.ShapeDtypeStruct((width, count), bf16),
            jax.ShapeDtypeStruct((8, features), f32),
            grad_shape,
        ],
        scratch_shapes=[
            pltpu.VMEM((count, features), f32),
            pltpu.VMEM((count, features), bf16),
            pltpu.VMEM((count, units), bf16),
            pltpu.VMEM((width, count), bf16),
        ],
        compiler_params=pltpu.CompilerParams(
            vmem_limit_bytes=FFN_LIMIT, dimension_semantics=("arbitrary",)
        ),
        cost_estimate=pl.CostEstimate(
            flops=6 * count * features * units, bytes_accessed=34 << 20, transcendentals=0
        ),
        name="ffn_forward",
    )(pos, hidden, vec, dy, b1, *late[0], *late[1], *early[0], *early[1])


def ffn_backward(wide, last, late_tiles, *refs):
    pos, dh_low, u_turned, slope, *refs = refs
    weights, refs = refs[: 4 if last else 8], refs[4 if last else 8 :]
    if last:
        du_in, dh, h_ref, vec, own_ref, oth_ref, db_ref, dh1, sums, total, low_all = refs
    else:
        own_ref, oth_ref, db_ref, total, low_all = refs
    t = pl.program_id(0)
    count, features = dh_low.shape
    width = features // 2

    def tile(w1a, w1b, w2a, w2b, before):
        db = 0.0
        for r in row_blocks(count, 256):
            grad = dot(dh_low[r, :width], w2a[...]) + dot(dh_low[r, width:], w2b[...])
            grad = grad * slope[r, :].astype(f32)
            db = db + jnp.sum(grad, 0, keepdims=True)
            low = grad.astype(bf16)
            low_all[r, :] = low
            left, right = dot_nt(low, w1a[...]), dot_nt(low, w1b[...])
            if before is None:
                total[r, :width] = left
                total[r, width:] = right
            else:
                total[r, :width] = before[r, :width] + left
                total[r, width:] = before[r, width:] + right
        db_ref[...] = db
        low = low_all[...]
        store_blocks(oth_ref, u_turned[width:, :], low)
        store_blocks(own_ref, u_turned[:width, :], low)

    @pl.when(t == 0)
    def _():
        tile(*weights[:4], du_in if last else None)

    if not last:

        @pl.when((t > 0) & (t < late_tiles))
        def _():
            tile(*weights[:4], total)

    @pl.when(t >= (1 if last else late_tiles))
    def _():
        tile(*weights[-4:], total)

    if last:

        @pl.when(t == pl.num_programs(0) - 1)
        def _():
            sums[...] = jnp.zeros_like(sums)
            for r in row_blocks(count):
                center, factor = moments(h_ref[r, :])
                normed = center * factor
                du = total[r, :] + dh[r, :]
                back = norm_back(du * (1.0 + vec[0:1, :]), normed, factor)
                turn_into_whole(dh1, r, back, pos, wide)
                sums[0:1, :] += jnp.sum(du, 0, keepdims=True)
                sums[1:2, :] += jnp.sum(du * normed, 0, keepdims=True)
                sums[2:3, :] += jnp.sum(back, 0, keepdims=True)


BACK_TILE = 512


def run_ffn_backward(pos, dh_low, u_turned, slope, late, early, tail):
    count, features = dh_low.shape
    wide = lax.axis_size("wide")
    width = features // 2
    block = features // wide
    last = tail is not None
    late_tiles = late[0][0].shape[1] // BACK_TILE
    half_tiles = early[0][0].shape[1] // BACK_TILE // 2
    tiles = half_tiles if last else late_tiles + half_tiles
    ins = [pos, dh_low, u_turned, slope]
    if last:
        at_slope = lambda t: (0, late_tiles + t)
        at_early = lambda t: (0, t)
    else:
        at_slope = lambda t: (0, jnp.where(t < late_tiles, t, t + half_tiles))
        at_early = lambda t: (0, half_tiles + jnp.maximum(t - late_tiles, 0))
    in_specs = [
        pl.BlockSpec(memory_space=pltpu.SMEM), once(count, features), once(features, count),
        pl.BlockSpec((count, BACK_TILE), at_slope),
    ]
    if not last:
        late_spec = pl.BlockSpec((width, BACK_TILE), lambda t: (0, jnp.minimum(t, late_tiles - 1)))
        in_specs += [late_spec] * 4
        ins += [*late[0], *late[1]]
    in_specs += [pl.BlockSpec((width, BACK_TILE), at_early)] * 4
    ins += [*early[0], *early[1]]
    grads = pl.BlockSpec((wide // 2, block, BACK_TILE), lambda t: (0, 0, t))
    grad_shape = jax.ShapeDtypeStruct((wide // 2, block, tiles * BACK_TILE), bf16)
    out_specs = [grads, grads, pl.BlockSpec((1, BACK_TILE), lambda t: (0, t))]
    out_shape = [grad_shape, grad_shape, jax.ShapeDtypeStruct((1, tiles * BACK_TILE), f32)]
    scratch = [pltpu.VMEM((count, BACK_TILE), bf16)]
    if last:
        ins += list(tail)
        in_specs += [once(count, features)] * 3 + [once(8, features)]
        out_specs += [once(count, features), once(8, features)]
        out_shape += [
            jax.ShapeDtypeStruct((count, features), f32),
            jax.ShapeDtypeStruct((8, features), f32),
        ]
        scratch = [pltpu.VMEM((count, features), f32)] + scratch
    else:
        out_specs.append(once(count, features))
        out_shape.append(jax.ShapeDtypeStruct((count, features), f32))
    return pl.pallas_call(
        functools.partial(ffn_backward, wide, last, late_tiles),
        grid=(tiles,),
        in_specs=in_specs,
        out_specs=out_specs,
        out_shape=out_shape,
        scratch_shapes=scratch,
        compiler_params=pltpu.CompilerParams(
            vmem_limit_bytes=FFN_LIMIT, dimension_semantics=("arbitrary",)
        ),
        cost_estimate=pl.CostEstimate(
            flops=6 * count * features * tiles * BACK_TILE, bytes_accessed=17 << 20, transcendentals=0
        ),
        name="ffn_backward",
    )(*ins)


def swap_hop(v, hop):
    kind, bit = hop
    return swap_wide(v, 2 << bit) if kind == "wide" else swap_narrow(v, 1 << bit)


class Scatter:
    def __init__(self, own, other, axes, mine, extra=None):
        self.parts = [] if own is None else [(own, ())]
        self.other = other
        self.axes, self.mine = dict(axes), mine
        self.extra = [] if extra is None else [(extra[0], ())]
        self.extra_other = None if extra is None else extra[1]

    def cross(self):
        own = self.parts[0][0]
        self.parts.append((swap_wide(self.other, 1).reshape(own.shape), ()))
        if self.extra:
            self.extra.append((swap_wide(self.extra_other, 1), ()))

    def columns(self, first, count):
        unit = Scatter(None, None, self.axes, self.mine)
        unit.parts = [(v, path + (("columns", (first, count)),)) for v, path in self.parts]
        return unit

    def send(self, hop):
        self.hop = hop
        axis = self.axes.pop(hop, None)
        keep = 0 if axis is None else self.mine[hop]
        more = lambda parts, i: [(v, path + ((axis, i),)) for v, path in parts]
        self.leaving = low_of(more(self.parts, 1 - keep))
        self.parts = more(self.parts, keep)
        if self.extra:
            self.leaving = jnp.concatenate([self.leaving, low_of(more(self.extra, 1 - keep))], -2)
            self.extra = more(self.extra, keep)
        if axis is not None:
            self.axes = {h: a - (a > axis) for h, a in self.axes.items()}

    def receive(self):
        came = swap_hop(self.leaving, self.hop)
        if self.extra:
            rows = self.parts[0][0].shape[-2]
            self.extra.append((came[..., rows:, :], ()))
            came = came[..., :rows, :]
        self.parts.append((came, ()))


def join(values, *units):
    values, came = lax.optimization_barrier((values, [unit.parts[-1][0] for unit in units]))
    for unit, v in zip(units, came):
        unit.parts[-1] = (v, unit.parts[-1][1])
    return values


def start(first, *sends):
    for unit, hop_to in sends:
        unit.send(hop_to)
    first, *leaving = tie(first, *[unit.leaving for unit, _ in sends])
    for (unit, _), v in zip(sends, leaving):
        unit.leaving = v
        unit.receive()
    return first


def taken(part):
    v, path = part
    starts, sizes, axes = [0] * v.ndim, list(v.shape), list(range(v.ndim))
    for axis, i in path:
        if axis is None:
            sizes[-1] //= 2
            starts[-1] += i * sizes[-1]
        elif axis == "columns":
            starts[-1] += i[0]
            sizes[-1] = i[1]
        else:
            at = axes.pop(axis)
            starts[at], sizes[at] = i, 1
    if all(isinstance(i, int) for i in starts):
        v = lax.slice(v, starts, [i + n for i, n in zip(starts, sizes)])
    else:
        v = lax.dynamic_slice(v, [jnp.int32(i) for i in starts], sizes)
    return v.reshape([sizes[at] for at in axes])


def sum_of(parts, view=lambda v: v):
    return sum(view(taken(p)).astype(f32) for p in parts)


def low_of(parts, view=lambda v: v):
    return sum_of(parts, view).astype(bf16)


def per_device(tokens, segment_ids, attn_weight, vectors, ffn_weight, ffn_bias, out_grad):
    wide, narrow = lax.axis_size("wide"), lax.axis_size("narrow")
    w, z = lax.axis_index("wide"), lax.axis_index("narrow")
    chip, core = lax.div(w, 2), lax.rem(w, 2)
    bits = chip_bits()
    up = list(range(bits))
    down = up[::-1]
    pos = jnp.stack([chip, core, z]).astype(jnp.int32)
    count, features = tokens.shape
    half = features // 2

    rows_each = attn_weight.shape[0]
    each, each_bias = vectors.shape[0], ffn_bias.shape[0]
    small = jnp.concatenate([vectors, ffn_bias, jnp.zeros((features - each - each_bias,), bf16)])
    small = jnp.concatenate([small[None], jnp.zeros((7, features), bf16)])
    v = jnp.concatenate([attn_weight, small])
    attn = v[None]
    units = ffn_weight.shape[2]
    width = units // SUBS
    tail = units - width
    every = range(bits)
    steps = list(range(narrow_bits()))[::-1]
    orders = (up, down)

    def along(v, step, axis):
        return jnp.concatenate([v, swap_narrow(v, 1 << step)], axis)

    late = [(ffn_weight[i, :, tail:], []) for i in range(2)]
    for i, step in enumerate(steps):
        attn = along(attn, step, 0)
        if i == 0:
            (attn, *v) = tie(attn, *[v for v, _ in late])
            late = [(v, done) for v, (_, done) in zip(v, late)]
    for i in every:
        late = [hop(v, done, order[i]) for (v, done), order in zip(late, orders)]
    late = jnp.stack([v.reshape(half, width) for v, _ in late])
    early, attn, late = tie(ffn_weight[:, :, :tail], attn, late)
    attn = [(attn[:, :, :half], []), (attn[:, :rows_each, half:], [])]
    for i in range(max(bits, len(steps))):
        if i < bits:
            attn = [hop(v, done, order[i]) for (v, done), order in zip(attn, orders)]
        if i < len(steps):
            early = along(early, steps[i], 2)
        early, a, b = tie(early, *[v for v, _ in attn])
        attn = [(a, attn[0][1]), (b, attn[1][1])]
    attn_a, attn_b = [v.reshape((wide // 2,) + v.shape[bits:]) for v, _ in attn]
    early = [(early[which], []) for which in range(2)]
    late, attn_a, attn_b, *firsts = tie(late, attn_a, attn_b, *[v for v, _ in early])
    halves = [attn_a, swap_wide(attn_a, 1), attn_b, swap_wide(attn_b, 1)]
    for i in every[:-1]:
        early = [hop(v, done, order[i]) for v, (_, done), order in zip(firsts, early, orders)]
        if i < len(steps) - 1:
            late = along(late, steps[i], 2)
        if i == 0:
            tokens_now, late, *firsts = tie(tokens, late, *[v for v, _ in early])
        else:
            firsts = [v for v, _ in early]
    for step in steps[bits - 1 : -1]:
        late = along(late, step, 2)
    late_came = swap_narrow(late, 1 << steps[-1])

    small = jnp.concatenate([h[:, :, rows_each, : each + each_bias] for h in halves[:2]])
    small = small.reshape(-1, each + each_bias)
    slots = jnp.arange(wide * narrow)
    slot_core, slot_chip, slot_z = (
        slots // (wide * narrow // 2), (slots // narrow) % (wide // 2), slots % narrow,
    )
    slot_w = (slot_chip ^ chip) * 2 + (slot_core ^ core)
    whole_at = slot_w * narrow + (turned(slot_z, narrow_bits()) ^ z)
    bias_at = slot_z * wide + slot_w
    spots = jnp.arange(wide * narrow)[:, None]
    vec_rows = dot((spots == whole_at[None, :]).astype(bf16), small[:, :each]).reshape(8, features)
    bias_rel = dot((spots == bias_at[None, :]).astype(bf16), small[:, each:])
    bias_rel = bias_rel.reshape(narrow, units)
    bias_rel = jnp.concatenate(
        [bias_rel[:, tail:].reshape(1, -1), bias_rel[:, :tail].reshape(1, -1)], 1
    )
    bq, bv, bo, s1, bf, s2, g1, g2 = [vec_rows[i] for i in range(8)]
    slot_vec = to_slots_quick(jnp.stack([g1, s1, bf, g2, s2, s2, s2, s2]), pos, chip, core)
    dy = to_slots_quick(out_grad, pos, chip, core)
    in_kernel = (features // wide) % 128 == 0

    def core_rows(v, which):
        t = v.reshape(count, -1, 2, narrow * rows_each)
        return pick(t, 2, which).reshape(count, half).T

    x_rows = [core_rows(tokens, core), core_rows(tokens, 1 - core)]

    biases = jnp.stack([bq, bv, bo, bo, bo, bo, bo, bo])
    *kept, mixed, hidden = run_attend_forward(pos, tokens_now, segment_ids, biases, *halves)
    o_rows = [core_rows(mixed, core), core_rows(mixed, 1 - core)]
    early = [
        hop(v, done, order[-1])[0].reshape(half, -1)
        for v, (_, done), order in zip(firsts, early, orders)
    ]
    hidden, late_came, *o_rows = tie(hidden, late_came, *o_rows)
    late = jnp.concatenate([late, late_came], 2)
    if not in_kernel:
        hidden = to_slots(hidden, chip, core)
    hidden, *early = tie(hidden, *early)
    early = [(v, swap_wide(v, 1)) for v in early]
    late = [(late[which], swap_wide(late[which], 1)) for which in range(2)]
    slope, act, u_turned, result, dh, dh_low, dh_own, sums_two, other = run_ffn_forward(
        pos, hidden, slot_vec, dy, bias_rel, late, early
    )
    if not in_kernel:
        result = from_slots(result, chip, core)

    late_width, half_early = narrow * width, narrow * tail // 2
    axes = {("wide", bit): bits - 1 - bit for bit in range(bits)}
    chips = lambda order: [("wide", bit) for bit in order]
    along = [("narrow", bit) for bit in range(narrow_bits())]

    def ffn_unit(own, other):
        own = own.reshape((2,) * bits + own.shape[1:])
        unit = Scatter(own, other, axes, dict.fromkeys(axes, 0))
        unit.cross()
        return unit

    downs = ffn_unit(run_down(dh_own, act), other)
    down_0, down_a, down_b = (
        downs.columns(0, late_width), downs.columns(late_width, half_early),
        downs.columns(late_width + half_early, half_early),
    )
    low = start(
        dh_low, (down_0, along[0]), (down_a, ("wide", down[0])), (down_b, ("wide", up[0]))
    )
    own, other, *rest = run_ffn_backward(pos, low, u_turned, slope, late, early, None)
    dbs = [rest[0]]
    up_a = ffn_unit(own, other)
    own, other, *rest = run_ffn_backward(
        pos, low, u_turned, slope, late, early, (rest[1], dh, hidden, slot_vec)
    )
    own, other, *rest = join([own, other, *rest], up_a, down_0, down_a, down_b)
    dbs.append(rest[0])
    grad_sum, sums_one = rest[1:]
    up_b = ffn_unit(own, other)
    up_late, up_upper = up_a.columns(0, late_width), up_a.columns(late_width, half_early)
    if not in_kernel:
        grad_sum = from_slots(grad_sum, chip, core)

    low_bits = bits - 2
    names = chips([bits - 1, bits - 2] + list(range(low_bits))[::-1]) + along[::-1]
    attn_axes = {name: axis for axis, name in enumerate(names)}
    mine = {("wide", bit): bit_of(chip, bit) for bit in range(bits)}
    mine.update({("narrow", bit): bit_of(z, bit) for bit in range(narrow_bits())})
    added = grad_sum
    attn_units = []
    slot_sums = from_slots(jnp.concatenate([sums_one[:3], sums_two[:3]]), chip, core)
    gs1, gg1, gbo, gs2, gg2, gbf = [slot_sums[i] for i in range(6)]
    db = jnp.concatenate([dbs[1], dbs[0][:, late_width:]], 1).reshape(narrow, tail)
    db = jnp.concatenate([db, dbs[0][:, :late_width].reshape(narrow, width)], 1)
    db = db.reshape(narrow, wide, each_bias)
    db = jnp.stack([pick(db, 0, turned(i ^ z, narrow_bits())) for i in range(narrow)], 1)

    def small_rows(vec):
        rows = jnp.concatenate([vec.reshape(wide, narrow, each), db], 2)
        rows = jnp.pad(rows[:, :, None], ((0, 0), (0, 0), (0, 7), (0, half - each - each_bias)))
        rows = rows.astype(bf16).reshape((2,) * (bits + 1 + narrow_bits()) + rows.shape[2:])
        return pick(rows, bits, core), pick(rows, bits, 1 - core)

    sums = jnp.stack([jnp.zeros_like(gs1)] * 2 + [gbo, gs1, gbf, gs2, gg1, gg2])
    for part in range(2):
        if part == 0:
            sends = [(up_late, ("wide", up[0])), (up_upper, ("wide", down[0])), (down_0, along[1])]
            sends += [(down_a, hop_to) for hop_to in chips(down[1:2])]
            low = start(grad_sum, *sends)
        else:
            sends = [(up_late, hop_to) for hop_to in chips(up[1:2])]
            sends += [(up_upper, hop_to) for hop_to in chips(down[1:2])]
            sends += [(down_b, hop_to) for hop_to in chips(up[1:2])]
            sends += [(up_b, ("wide", up[0])), (attn_units[0], ("wide", down[0]))]
            low = start(low, *sends)
        own, other, added, sums = run_attend_backward(
            part, pos, low, added, sums, kept, x_rows + o_rows, halves
        )
        if part == 0:
            ready = (up_late, up_upper, down_0, down_a, up_b)
        else:
            ready = (up_late, up_upper, down_b)
        own, other, added, sums = join([own, other, added, sums], *ready)
        shape = (2,) * len(names) + (rows_each, half)
        unit = Scatter(
            own.reshape(shape), other, attn_axes, mine, None if part == 0 else small_rows(sums)
        )
        unit.cross()
        attn_units.append(unit)
    grad_tokens = added

    routes = [chips(down) + along, chips(up) + along]
    for step in range(bits):
        for unit, route in zip(attn_units, routes):
            if step or unit is attn_units[1]:
                unit.send(route[step])
                unit.receive()
        if step == 0:
            for unit, hops in (
                (up_b, chips(up[1:])), (up_late, chips(up[2:])), (up_upper, chips(down[2:])),
                (down_0, along[2:] + chips(down)), (down_a, chips(down[2:])), (down_b, chips(up[2:])),
            ):
                for hop_to in hops:
                    unit.send(hop_to)
                    unit.receive()
    for step, hop_to in enumerate(along):
        for unit in attn_units:
            unit.send(hop_to)
            unit.receive()
        up_late.send(hop_to)
        if step == 0:
            leaving = [up_late.leaving, low_of(up_upper.parts), low_of(down_b.parts)]
        else:
            up_b.send(hop_to)
            down_a.send(hop_to)
            leaving = [up_late.leaving, up_b.leaving, down_a.leaving]
        came = swap_hop(jnp.concatenate(leaving, -1), hop_to)
        first = 0
        for unit, v in zip((up_late, up_b, down_a), leaving):
            unit.parts.append((came, (("columns", (first, v.shape[-1])),)))
            first += v.shape[-1]
    grad_ffn = jnp.stack(
        [
            jnp.concatenate([sum_of(up_b.parts), sum_of(up_late.parts)], -1),
            jnp.concatenate([sum_of(down_a.parts), sum_of(down_0.parts)], -1),
        ]
    )
    grad_attn = jnp.concatenate([sum_of(u.parts) for u in attn_units], -1)
    tally = sum_of(attn_units[1].extra)[0]
    return (
        result, grad_tokens, grad_attn, tally[:each], grad_ffn, tally[each : each + each_bias],
    )


def solution(mesh):
    return jax.shard_map(
        per_device,
        mesh=mesh,
        in_specs=(
            P(("wide", "narrow"), None),
            P(("wide", "narrow"), None),
            P(("wide", "narrow"), None),
            P(("wide", "narrow")),
            P(None, "wide", "narrow"),
            P(("narrow", "wide")),
            P(("wide", "narrow"), None),
        ),
        out_specs=(
            P(("wide", "narrow"), None),
            P(("wide", "narrow"), None),
            P(("wide", "narrow"), None),
            P(("wide", "narrow")),
            P(None, "wide", "narrow"),
            P(("narrow", "wide")),
        ),
        check_vma=False,
    )
```

```python
import functools

import jax
import jax.numpy as jnp
from jax import lax
from jax.experimental import pallas as pl
from jax.experimental.pallas import tpu as pltpu
from jax.sharding import PartitionSpec as P

HEADS = 16
HEAD = 64
SUBS = 4
VMEM_LIMIT = 56 * 1024 * 1024
FFN_LIMIT = 44 * 1024 * 1024
BACK_LIMIT = 40 * 1024 * 1024

f32 = jnp.float32
bf16 = jnp.bfloat16

NT = (((1,), (1,)), ((), ()))
TN = (((0,), (0,)), ((), ()))


def dot(a, b):
    return jnp.dot(a, b, preferred_element_type=f32)


def dot_nt(a, b):
    return lax.dot_general(a, b, NT, preferred_element_type=f32)


def dot_tn(a, b):
    return lax.dot_general(a, b, TN, preferred_element_type=f32)


def swap_wide(v, mask):
    size = lax.axis_size("wide")
    return lax.ppermute(v, "wide", [(w, w ^ mask) for w in range(size)])


def swap_narrow(v, mask):
    size = lax.axis_size("narrow")
    return lax.ppermute(v, "narrow", [(z, z ^ mask) for z in range(size)])


def chip_bits():
    return (lax.axis_size("wide") // 2).bit_length() - 1


def narrow_bits():
    return lax.axis_size("narrow").bit_length() - 1


def turned(index, bits):
    out = 0
    for bit in range(bits):
        out = out + ((index >> bit) & 1) * (1 << (bits - 1 - bit))
    return out


def gather_narrow(v, axis):
    for bit in reversed(range(narrow_bits())):
        v = jnp.concatenate([v, swap_narrow(v, 1 << bit)], axis)
    return v


def hop(v, done, bit):
    axis = sum(1 for b in done if b > bit)
    return jnp.stack([v, swap_wide(v, 2 << bit)], axis), done + [bit]


def bit_of(index, bit):
    return lax.rem(lax.div(index, 1 << bit), 2)


def pick(v, axis, index):
    return lax.dynamic_index_in_dim(v, index, axis, keepdims=False)


def to_slots(v, chip, core):
    bits = chip_bits()
    lead = v.shape[:-1]
    block = v.shape[-1] // lax.axis_size("wide")
    t = v.reshape(lead + (2,) * (bits + 1) + (block,))
    n = len(lead)
    for bit in range(bits):
        axis = n + bits - 1 - bit
        t = jnp.where(bit_of(chip, bit) == 1, jnp.flip(t, axis), t)
    t = jnp.where(core == 1, jnp.flip(t, n + bits), t)
    t = jnp.moveaxis(t, n + bits, n)
    return t.reshape(v.shape)


def from_slots(v, chip, core):
    bits = chip_bits()
    lead = v.shape[:-1]
    block = v.shape[-1] // lax.axis_size("wide")
    n = len(lead)
    t = v.reshape(lead + (2,) * (bits + 1) + (block,))
    t = jnp.moveaxis(t, n, n + bits)
    for bit in range(bits):
        axis = n + bits - 1 - bit
        t = jnp.where(bit_of(chip, bit) == 1, jnp.flip(t, axis), t)
    t = jnp.where(core == 1, jnp.flip(t, n + bits), t)
    return t.reshape(v.shape)


def slot_lanes(pos, block, wide, lanes):
    at = ((block % 2) ^ pos[1]) * (wide // 2) + ((block // 2) ^ pos[0])
    return pl.ds(pl.multiple_of(at * lanes, lanes), lanes)


def whole_lanes(pos, slot, wide, lanes):
    core, chip = divmod(slot, wide // 2)
    at = (chip ^ pos[0]) * 2 + (core ^ pos[1])
    return pl.ds(pl.multiple_of(at * lanes, lanes), lanes)


def permute_kernel(wide, pos, v_ref, out_ref):
    lanes = v_ref.shape[1] // wide
    for b in range(wide):
        out_ref[:, slot_lanes(pos, b, wide, lanes)] = v_ref[:, b * lanes : (b + 1) * lanes]


def to_slots_quick(v, pos, chip, core):
    wide = lax.axis_size("wide")
    if (v.shape[1] // wide) % 128:
        return to_slots(v, chip, core)
    return pl.pallas_call(
        functools.partial(permute_kernel, wide),
        in_specs=[pl.BlockSpec(memory_space=pltpu.SMEM), pl.BlockSpec(memory_space=pltpu.VMEM)],
        out_specs=pl.BlockSpec(memory_space=pltpu.VMEM),
        out_shape=jax.ShapeDtypeStruct(v.shape, v.dtype),
        name="permute",
    )(pos, v)


def tie(*values):
    return lax.optimization_barrier(values)


def load_rows(pos, geometry, own, other, matrix, first, count, place, sem):
    narrow, per_matrix, rows = geometry[:3]

    def body(j, carry):
        block = matrix * per_matrix + first + j
        w = block // narrow
        z = block % narrow
        chip = (w // 2) ^ pos[0]
        core = (w % 2) ^ pos[1]
        step = turned(z ^ pos[2], narrow.bit_length() - 1)

        @pl.when(core == 0)
        def _():
            pltpu.make_async_copy(own.at[chip, step, pl.ds(0, rows)], place(j), sem).start()

        @pl.when(core == 1)
        def _():
            pltpu.make_async_copy(other.at[chip, step, pl.ds(0, rows)], place(j), sem).start()

        return carry

    lax.fori_loop(0, count, body, 0)


def attend_forward(
    geometry, pos, x_ref, seg_row, seg_col, vec_ref, bo_ref, own_a, oth_a, own_b, oth_b,
    q_ref, k_ref, v_ref, p_ref, o_ref, h_ref, w_in, w_out, mask, sems,
):
    g = pl.program_id(0)
    steps = pl.num_programs(0)
    _, blocks, rows, wide = geometry
    sources = ((own_a, oth_a), (own_b, oth_b))

    @pl.when(g == 0)
    def _():
        for half in range(2):
            for m in range(3):
                load_rows(
                    pos, geometry, *sources[half], m, 0, blocks,
                    lambda j, half=half, m=m: w_in.at[half, m, pl.ds(pl.multiple_of(j * rows, rows), rows)],
                    sems.at[half],
                )
        for half in range(2):
            load_rows(
                pos, geometry, *sources[half], 3, 0, blocks,
                lambda j, half=half: w_out.at[half, pl.ds(pl.multiple_of(j * rows, rows), rows)],
                sems.at[2],
            )
        mask[...] = jnp.where(seg_col[...] == seg_row[...], 0.0, -1e30).astype(f32)
        pltpu.make_async_copy(w_in.at[0], w_in.at[0], sems.at[0]).wait()

    @pl.when(g == steps // 2)
    def _():
        pltpu.make_async_copy(w_in.at[1], w_in.at[1], sems.at[1]).wait()

    half = g // (steps // 2)
    columns = pl.ds(pl.multiple_of(lax.rem(g, steps // 2) * 256, 256), 256)
    x = x_ref[...]
    query = (dot(x, w_in[half, 0, :, columns]) + vec_ref[0:1, :]).astype(bf16)
    query = query * jnp.asarray(HEAD**-0.5, bf16)
    key = dot(x, w_in[half, 1, :, columns]).astype(bf16)
    value = (dot(x, w_in[half, 2, :, columns]) + vec_ref[1:2, :]).astype(bf16)
    q_ref[...] = query
    k_ref[...] = key
    v_ref[...] = value
    lane = lax.broadcasted_iota(jnp.int32, (1, 128), 1)
    for pair in range(2):
        part = slice(pair * 128, pair * 128 + 128)
        q2, k2, v2 = query[:, part], key[:, part], value[:, part]
        v2t = v2.T
        outs = []
        for sub in range(2):
            mine = (lane < HEAD) if sub == 0 else (lane >= HEAD)
            scores = dot_nt(k2, jnp.where(mine, q2, jnp.zeros_like(q2))) + mask[...]
            raised = jnp.exp(scores - jnp.max(scores, 0, keepdims=True))
            probs = (raised * (1.0 / jnp.sum(raised, 0, keepdims=True))).astype(bf16)
            p_ref[pair * 2 + sub] = probs
            outs.append(dot(v2t[sub * HEAD : sub * HEAD + HEAD], probs))
        mixed = jnp.concatenate(outs, 0).T.astype(bf16)
        o_ref[:, pl.ds(pl.multiple_of(g * 256 + pair * 128, 128), 128)] = mixed

    @pl.when(g == steps - 1)
    def _():
        pltpu.make_async_copy(w_out, w_out, sems.at[2]).wait()
        width = w_out.shape[2]
        lanes = 2 * width // wide
        for half in range(2):
            cols = slice(half * width, half * width + width)
            hidden = x_ref[:, cols].astype(f32) + dot(o_ref[...], w_out[half]) + bo_ref[0:1, cols]
            if lanes % 128:
                h_ref[:, cols] = hidden
            else:
                for b in range(wide // 2):
                    at = slot_lanes(pos, half * (wide // 2) + b, wide, lanes)
                    h_ref[:, at] = hidden[:, b * lanes : (b + 1) * lanes]


def run_attend_forward(pos, tokens, segment_ids, biases, own_a, oth_a, own_b, oth_b):
    count, features = tokens.shape
    rows = own_b.shape[2]
    geometry = (own_b.shape[1], features // rows, rows, own_b.shape[0] * 2)
    groups = features // 256
    whole = lambda *shape: pl.BlockSpec(shape, lambda g, pos: (0,) * len(shape))
    column = pl.BlockSpec((count, 256), lambda g, pos: (0, g))
    anywhere = pl.BlockSpec(memory_space=pl.ANY)
    width = features // 2
    return pl.pallas_call(
        functools.partial(attend_forward, geometry),
        grid_spec=pltpu.PrefetchScalarGridSpec(
            num_scalar_prefetch=1,
            grid=(groups,),
            in_specs=[
                whole(count, features), whole(1, count), whole(count, 1),
                pl.BlockSpec((8, 256), lambda g, pos: (0, g)), whole(8, features),
                anywhere, anywhere, anywhere, anywhere,
            ],
            out_specs=[
                column, column, column,
                pl.BlockSpec((4, count, count), lambda g, pos: (g, 0, 0)),
                whole(count, features), whole(count, features),
            ],
            scratch_shapes=[
                pltpu.VMEM((2, 3, features, width), bf16),
                pltpu.VMEM((2, features, width), bf16),
                pltpu.VMEM((count, count), f32),
                pltpu.SemaphoreType.DMA((3,)),
            ],
        ),
        out_shape=[
            jax.ShapeDtypeStruct((count, features), bf16),
            jax.ShapeDtypeStruct((count, features), bf16),
            jax.ShapeDtypeStruct((count, features), bf16),
            jax.ShapeDtypeStruct((HEADS, count, count), bf16),
            jax.ShapeDtypeStruct((count, features), bf16),
            jax.ShapeDtypeStruct((count, features), f32),
        ],
        compiler_params=pltpu.CompilerParams(
            vmem_limit_bytes=VMEM_LIMIT, dimension_semantics=("arbitrary",)
        ),
        cost_estimate=pl.CostEstimate(
            flops=2 * count * features * features * 8, bytes_accessed=24 << 20, transcendentals=0
        ),
        name="attend_forward",
    )(
        pos, tokens, segment_ids.reshape(1, count), segment_ids.reshape(count, 1),
        biases, biases[2:3] + jnp.zeros((8, 1), f32), own_a, oth_a, own_b, oth_b,
    )


def attend_backward(
    geometry, half, pos, dh_ref, add_ref, sums_in, q_ref, k_ref, v_ref, p_ref, x_own, x_oth, o_own, o_oth,
    own_a, oth_a, own_b, oth_b, gown_ref, goth_ref, dx_ref, bias_ref, w_in, w_out, sems,
):
    g = pl.program_id(0)
    features = dh_ref.shape[1]
    _, blocks, rows, _ = geometry
    sources = ((own_a, oth_a), (own_b, oth_b))

    @pl.when(g == 0)
    def _():
        for part in range(2):
            load_rows(
                pos, geometry, *sources[part], 3, half * (blocks // 2), blocks // 2,
                lambda j, part=part: w_out.at[part, pl.ds(pl.multiple_of(j * rows, rows), rows)],
                sems.at[0],
            )
        for m in range(3):
            load_rows(
                pos, geometry, *sources[half], m, 0, blocks,
                lambda j, m=m: w_in.at[m, pl.ds(pl.multiple_of(j * rows, rows), rows)],
                sems.at[1],
            )
        pltpu.make_async_copy(w_out, w_out, sems.at[0]).wait()

    span = pl.ds(pl.multiple_of(g * 256, 256), 256)
    width = features // 2
    low = dh_ref[...].astype(bf16)
    grad_mixed = (
        dot_nt(low[:, :width], w_out[0, span, :]) + dot_nt(low[:, width:], w_out[1, span, :])
    ).astype(bf16)
    lane = lax.broadcasted_iota(jnp.int32, (1, 128), 1)
    lows = [[], [], []]
    sums = [[], []]
    for pair in range(2):
        part = slice(pair * 128, pair * 128 + 128)
        q2, k2, v2 = q_ref[:, part], k_ref[:, part], v_ref[:, part]
        do2 = grad_mixed[:, part]
        k2t = k2.T
        zero = jnp.zeros_like(q2)
        dv = dk = None
        dqs = []
        for sub in range(2):
            mine = (lane < HEAD) if sub == 0 else (lane >= HEAD)
            probs = p_ref[pair * 2 + sub]
            do_mine = jnp.where(mine, do2, zero)
            grad_probs = dot_nt(v2, do_mine)
            wide_probs = probs.astype(f32)
            inner = jnp.sum(wide_probs * grad_probs, 0, keepdims=True)
            grad_scores = (wide_probs * (grad_probs - inner)).astype(bf16)
            dv_part = dot(probs, do_mine)
            dk_part = dot(grad_scores, jnp.where(mine, q2, zero))
            dv = dv_part if dv is None else dv + dv_part
            dk = dk_part if dk is None else dk + dk_part
            dqs.append(dot(k2t[sub * HEAD : sub * HEAD + HEAD], grad_scores))
        dq = jnp.concatenate(dqs, 0).T * HEAD**-0.5
        sums[0].append(jnp.sum(dq, 0, keepdims=True))
        sums[1].append(jnp.sum(dv, 0, keepdims=True))
        for store, value in zip(lows, (dq, dk, dv)):
            store.append(value.astype(bf16))
    joined = [jnp.concatenate(s, 1) for s in lows]
    for m in range(3):
        goth_ref[m] = dot(x_oth[...], joined[m]).astype(bf16)
        gown_ref[m] = dot(x_own[...], joined[m]).astype(bf16)
    low = dh_ref[:, pl.ds(pl.multiple_of(half * width + g * 256, 256), 256)].astype(bf16)
    goth_ref[3] = dot(o_oth[...], low).astype(bf16)
    gown_ref[3] = dot(o_own[...], low).astype(bf16)
    @pl.when(g == 0)
    def _():
        bias_ref[...] = sums_in[...]

    for row in range(2):
        at = pl.ds(pl.multiple_of(half * width + g * 256, 256), 256)
        bias_ref[row : row + 1, at] = jnp.concatenate(sums[row], 1)

    @pl.when(g == 0)
    def _():
        pltpu.make_async_copy(w_in, w_in, sems.at[1]).wait()
        dx_ref[...] = add_ref[...]

    dx_ref[...] += (
        dot_nt(joined[0], w_in[0, :, span])
        + dot_nt(joined[1], w_in[1, :, span])
        + dot_nt(joined[2], w_in[2, :, span])
    )


def run_attend_backward(half, pos, grad_sum, added, sums, kept, rows_of, weights):
    q, k, v, probs = kept
    own_a, oth_a, own_b, oth_b = weights
    count, features = q.shape
    rows = own_b.shape[2]
    geometry = (own_b.shape[1], features // rows, rows, own_b.shape[0] * 2)
    groups = features // 512
    whole = lambda *shape: pl.BlockSpec(shape, lambda g, pos: (0,) * len(shape))
    column = pl.BlockSpec((count, 256), lambda g, pos: (0, half * groups + g))
    anywhere = pl.BlockSpec(memory_space=pl.ANY)
    width = features // 2
    return pl.pallas_call(
        functools.partial(attend_backward, geometry, half),
        grid_spec=pltpu.PrefetchScalarGridSpec(
            num_scalar_prefetch=1,
            grid=(groups,),
            in_specs=[
                whole(count, features), whole(count, features), whole(8, features), column, column,
                column,
                pl.BlockSpec((4, count, count), lambda g, pos: (half * groups + g, 0, 0)),
                whole(width, count), whole(width, count), whole(width, count), whole(width, count),
                anywhere, anywhere, anywhere, anywhere,
            ],
            out_specs=[
                pl.BlockSpec((4, width, 256), lambda g, pos: (0, 0, g)),
                pl.BlockSpec((4, width, 256), lambda g, pos: (0, 0, g)),
                whole(count, features),
                whole(8, features),
            ],
            scratch_shapes=[
                pltpu.VMEM((3, features, width), bf16),
                pltpu.VMEM((2, width, width), bf16),
                pltpu.SemaphoreType.DMA((2,)),
            ],
        ),
        out_shape=[
            jax.ShapeDtypeStruct((4, width, width), bf16),
            jax.ShapeDtypeStruct((4, width, width), bf16),
            jax.ShapeDtypeStruct((count, features), f32),
            jax.ShapeDtypeStruct((8, features), f32),
        ],
        compiler_params=pltpu.CompilerParams(
            vmem_limit_bytes=VMEM_LIMIT, dimension_semantics=("arbitrary",)
        ),
        cost_estimate=pl.CostEstimate(
            flops=2 * count * features * features * 6, bytes_accessed=16 << 20, transcendentals=0
        ),
        name="attend_backward",
    )(pos, grad_sum, added, sums, q, k, v, probs, *rows_of, own_a, oth_a, own_b, oth_b)


def moments(hidden):
    center = hidden - jnp.mean(hidden, -1, keepdims=True)
    return center, lax.rsqrt(jnp.mean(center * center, -1, keepdims=True) + 1e-12)


def norm_back(grad, normed, factor):
    return factor * (
        grad
        - jnp.mean(grad, -1, keepdims=True)
        - normed * jnp.mean(grad * normed, -1, keepdims=True)
    )


def gelu_pair(a):
    z = jnp.abs(a) * (0.5**0.5)
    t = 1.0 / (1.0 + 0.3275911 * z)
    poly = t * (
        0.127414796 + t * (-0.142248368 + t * (0.7107068705 + t * (-0.7265760135 + t * 0.5307027145)))
    )
    bell = jnp.exp(-0.5 * (a * a))
    tail = poly * bell
    phi = jnp.where(a >= 0, 1.0 - tail, tail)
    return a * phi, phi + a * (bell * 0.3989422804014327)


ROWS_AT_ONCE = 128
TILE = 1024


def row_blocks(count, step=ROWS_AT_ONCE):
    return [slice(r, r + step) for r in range(0, count, step)]


def turn_into_whole(ref, rows, value, pos, wide):
    features = value.shape[1]
    lanes = features // wide
    if lanes % 128:
        ref[rows, :] = value
    else:
        for slot in range(wide):
            ref[rows, whole_lanes(pos, slot, wide, lanes)] = value[
                :, slot * lanes : (slot + 1) * lanes
            ]


def store_blocks(ref, turned_rows, right):
    chips, block = ref.shape[0], ref.shape[1]
    step = max(1, 256 // block)
    for k in range(0, chips, step):
        value = dot(turned_rows[k * block : (k + step) * block, :], right).astype(bf16)
        for i in range(step):
            ref[k + i] = value[i * block : (i + 1) * block]


def once(*shape):
    return pl.BlockSpec(
        shape, lambda t: (0,) * len(shape), pipeline_mode=pl.Buffered(buffer_count=1)
    )


def odd_last_places(wide):
    half = wide // 2
    return [slot // half * half + slot % 2 * (half // 2) + slot % half // 2 for slot in range(wide)]


def ffn_forward(
    wide, tiles, pos, h_ref, vec, dy, b1, l0a, l0b, l1a, l1b, *refs
):
    ups, downs, refs = refs[:4], refs[4:8], refs[8:]
    (
    slope_ref, act_ref, u_out, result, dh, dh_low, dh_own, sums, oth_ref,
    total, u_low, act_all, dh_turned,
    ) = refs
    t = pl.program_id(0)
    count, features = h_ref.shape
    width = features // 2
    quarter = width // 2
    block = features // wide
    odd_last = [block * p for p in odd_last_places(wide)]

    @pl.when(t == 0)
    def _():
        for r in row_blocks(count):
            center, factor = moments(h_ref[r, :])
            low = (center * factor * (1.0 + vec[0:1, :]) + vec[1:2, :]).astype(bf16)
            u_low[r, :] = low
            u_out[:, r] = low.T

    def tile(ups, downs, first, at, size):
        columns = pl.ds(pl.multiple_of(t * TILE + at, 256), size)
        step = features // len(ups)
        for r in row_blocks(count, 256):
            a = b1[0:1, columns]
            for i, w in enumerate(ups):
                a = a + dot(u_low[r, i * step : i * step + step], w[...])
            act, slope = gelu_pair(a)
            act = act.astype(bf16)
            act_all[r, columns] = act
            act_ref[r, at : at + size] = act
            slope_ref[r, at : at + size] = slope.astype(bf16)
            for i, w in enumerate(downs):
                value = dot_nt(act, w[...])
                if first:
                    total[r, i * step : i * step + step] = value
                else:
                    total[r, i * step : i * step + step] += value

    @pl.when(t == 0)
    def _():
        size = TILE // 2
        tile((l0a.at[0], l0b.at[0]), (l0a.at[1], l0b.at[1]), True, 0, size)
        tile((l1a.at[0], l1b.at[0]), (l1a.at[1], l1b.at[1]), False, size, size)

    @pl.when((t > 0) & (t < tiles))
    def _():
        tile(ups, downs, False, 0, TILE)

    @pl.when(t == tiles - 1)
    def _():
        sums[...] = jnp.zeros_like(sums)
        for r in row_blocks(count):
            center, factor = moments(h_ref[r, :])
            u = center * factor * (1.0 + vec[0:1, :]) + vec[1:2, :]
            ffn = jnp.concatenate([total[r, at : at + block] for at in odd_last], 1)
            center, factor = moments(u + ffn + vec[2:3, :])
            normed = center * factor
            final = (normed * (1.0 + vec[3:4, :]) + vec[4:5, :]).astype(bf16)
            turn_into_whole(result, r, final, pos, wide)
            grad = dy[r, :].astype(f32)
            back = norm_back(grad * (1.0 + vec[3:4, :]), normed, factor)
            dh[r, :] = back
            low = back.astype(bf16)
            for slot, at in enumerate(odd_last):
                dh_low[r, at : at + block] = low[:, slot * block : (slot + 1) * block]
            dh_own[:, r] = low[:, :width].T
            dh_turned[:, r] = low[:, width:].T
            sums[0:1, :] += jnp.sum(grad, 0, keepdims=True)
            sums[1:2, :] += jnp.sum(grad * normed, 0, keepdims=True)
            sums[2:3, :] += jnp.sum(back, 0, keepdims=True)

    @pl.when(t >= tiles)
    def _():
        columns = pl.ds(pl.multiple_of((t - tiles) * TILE, TILE), TILE)
        store_blocks(oth_ref, dh_turned[...], act_all[:, columns])


def down_kernel(left, right, out_ref):
    store_blocks(out_ref, left[...], right[...])


def run_down(dh_own, act):
    width, count = dh_own.shape
    units = act.shape[1]
    wide = lax.axis_size("wide")
    block = 2 * width // wide
    return pl.pallas_call(
        down_kernel,
        grid=(units // TILE,),
        in_specs=[once(width, count), pl.BlockSpec((count, TILE), lambda t: (0, t))],
        out_specs=pl.BlockSpec((wide // 2, block, TILE), lambda t: (0, 0, t)),
        out_shape=jax.ShapeDtypeStruct((wide // 2, block, units), bf16),
        compiler_params=pltpu.CompilerParams(
            vmem_limit_bytes=24 << 20, dimension_semantics=("arbitrary",)
        ),
        cost_estimate=pl.CostEstimate(
            flops=2 * count * width * units, bytes_accessed=9 << 20, transcendentals=0
        ),
        name="down_own",
    )(dh_own, act)


def run_ffn_forward(pos, hidden, vec, dy, b1, late, early):
    count, features = hidden.shape
    wide = lax.axis_size("wide")
    width = features // 2
    units = b1.shape[1]
    tiles = units // TILE
    block = features // wide
    tall = pl.BlockSpec((width // 2, TILE), lambda t: (0, jnp.clip(t - 1, 0, tiles - 2)))
    grads = pl.BlockSpec((wide // 2, block, TILE), lambda t: (0, 0, jnp.maximum(t - tiles, 0)))
    grad_shape = jax.ShapeDtypeStruct((wide // 2, block, units), bf16)
    return pl.pallas_call(
        functools.partial(ffn_forward, wide, tiles),
        grid=(2 * tiles,),
        in_specs=[
            pl.BlockSpec(memory_space=pltpu.SMEM), once(count, features), once(8, features),
            once(count, features), once(1, units),
        ] + [once(2, width, TILE // 2)] * 4 + [tall] * 8,
        out_specs=[
            pl.BlockSpec((count, TILE), lambda t: (0, jnp.minimum(t, tiles - 1))),
            pl.BlockSpec((count, TILE), lambda t: (0, jnp.minimum(t, tiles - 1))),
            once(features, count), once(count, features), once(count, features),
            once(count, features), once(width, count), once(8, features), grads,
        ],
        out_shape=[
            jax.ShapeDtypeStruct((count, units), bf16),
            jax.ShapeDtypeStruct((count, units), bf16),
            jax.ShapeDtypeStruct((features, count), bf16),
            jax.ShapeDtypeStruct((count, features), bf16),
            jax.ShapeDtypeStruct((count, features), f32),
            jax.ShapeDtypeStruct((count, features), bf16),
            jax.ShapeDtypeStruct((width, count), bf16),
            jax.ShapeDtypeStruct((8, features), f32),
            grad_shape,
        ],
        scratch_shapes=[
            pltpu.VMEM((count, features), f32),
            pltpu.VMEM((count, features), bf16),
            pltpu.VMEM((count, units), bf16),
            pltpu.VMEM((width, count), bf16),
        ],
        compiler_params=pltpu.CompilerParams(
            vmem_limit_bytes=FFN_LIMIT, dimension_semantics=("arbitrary",)
        ),
        cost_estimate=pl.CostEstimate(
            flops=6 * count * features * units, bytes_accessed=34 << 20, transcendentals=0
        ),
        name="ffn_forward",
    )(pos, hidden, vec, dy, b1, *late, *early[0], *early[1])


def ffn_backward(wide, last, *refs):
    pos, dh_low, u_turned, slope, *refs = refs
    late, refs = ([], refs) if last else (refs[:4], refs[4:])
    ups, downs, refs = refs[:4], refs[4:8], refs[8:]
    if last:
        du_in, dh, h_ref, vec, own_ref, oth_ref, db_ref, dh1, sums, total, low_all = refs
    else:
        own_ref, oth_ref, db_ref, total, low_all = refs
    t = pl.program_id(0)
    count, features = dh_low.shape
    width = features // 2

    def tile(ups, downs, before):
        db = 0.0
        step = features // len(ups)
        for r in row_blocks(count, 256):
            grad = 0.0
            for i, w in enumerate(downs):
                grad = grad + dot(dh_low[r, i * step : i * step + step], w[...])
            grad = grad * slope[r, :].astype(f32)
            db = db + jnp.sum(grad, 0, keepdims=True)
            low = grad.astype(bf16)
            low_all[r, :] = low
            for i, w in enumerate(ups):
                value = dot_nt(low, w[...])
                columns = slice(i * step, i * step + step)
                total[r, columns] = value if before is None else before[r, columns] + value
        db_ref[...] = db
        low = low_all[...]
        store_blocks(oth_ref, u_turned[width:, :], low)
        store_blocks(own_ref, u_turned[:width, :], low)

    if last:

        @pl.when(t == 0)
        def _():
            tile(ups, downs, du_in)

    else:
        for i in range(2):

            @pl.when(t == i)
            def _(i=i):
                a, b = late[2 * i : 2 * i + 2]
                tile((a.at[0], b.at[0]), (a.at[1], b.at[1]), total if i else None)

    @pl.when(t >= (1 if last else 2))
    def _():
        tile(ups, downs, total)

    if last:

        @pl.when(t == pl.num_programs(0) - 1)
        def _():
            sums[...] = jnp.zeros_like(sums)
            for r in row_blocks(count):
                center, factor = moments(h_ref[r, :])
                normed = center * factor
                du = total[r, :] + dh[r, :]
                back = norm_back(du * (1.0 + vec[0:1, :]), normed, factor)
                turn_into_whole(dh1, r, back, pos, wide)
                sums[0:1, :] += jnp.sum(du, 0, keepdims=True)
                sums[1:2, :] += jnp.sum(du * normed, 0, keepdims=True)
                sums[2:3, :] += jnp.sum(back, 0, keepdims=True)


BACK_TILE = 512


def run_ffn_backward(pos, dh_low, u_turned, slope, late, early, tail):
    count, features = dh_low.shape
    wide = lax.axis_size("wide")
    width = features // 2
    block = features // wide
    last = tail is not None
    late_tiles = 2
    assert late[0].shape[2] == BACK_TILE
    half_tiles = early[0][0].shape[1] // BACK_TILE // 2
    tiles = half_tiles if last else late_tiles + half_tiles
    ins = [pos, dh_low, u_turned, slope]
    if last:
        at_slope = lambda t: (0, late_tiles + t)
        at_early = lambda t: (0, t)
    else:
        at_slope = lambda t: (0, jnp.where(t < late_tiles, t, t + half_tiles))
        at_early = lambda t: (0, half_tiles + jnp.maximum(t - late_tiles, 0))
    in_specs = [
        pl.BlockSpec(memory_space=pltpu.SMEM), once(count, features), once(features, count),
        pl.BlockSpec((count, BACK_TILE), at_slope),
    ]
    if not last:
        in_specs += [once(2, width, BACK_TILE)] * 4
        ins += list(late)
    in_specs += [pl.BlockSpec((width // 2, BACK_TILE), at_early)] * 8
    ins += [*early[0], *early[1]]
    grads = pl.BlockSpec((wide // 2, block, BACK_TILE), lambda t: (0, 0, t))
    grad_shape = jax.ShapeDtypeStruct((wide // 2, block, tiles * BACK_TILE), bf16)
    out_specs = [grads, grads, pl.BlockSpec((1, BACK_TILE), lambda t: (0, t))]
    out_shape = [grad_shape, grad_shape, jax.ShapeDtypeStruct((1, tiles * BACK_TILE), f32)]
    scratch = [pltpu.VMEM((count, BACK_TILE), bf16)]
    if last:
        ins += list(tail)
        in_specs += [once(count, features)] * 3 + [once(8, features)]
        out_specs += [once(count, features), once(8, features)]
        out_shape += [
            jax.ShapeDtypeStruct((count, features), f32),
            jax.ShapeDtypeStruct((8, features), f32),
        ]
        scratch = [pltpu.VMEM((count, features), f32)] + scratch
    else:
        out_specs.append(once(count, features))
        out_shape.append(jax.ShapeDtypeStruct((count, features), f32))
    return pl.pallas_call(
        functools.partial(ffn_backward, wide, last),
        grid=(tiles,),
        in_specs=in_specs,
        out_specs=out_specs,
        out_shape=out_shape,
        scratch_shapes=scratch,
        compiler_params=pltpu.CompilerParams(
            vmem_limit_bytes=BACK_LIMIT, dimension_semantics=("arbitrary",)
        ),
        cost_estimate=pl.CostEstimate(
            flops=6 * count * features * tiles * BACK_TILE, bytes_accessed=17 << 20, transcendentals=0
        ),
        name="ffn_backward",
    )(*ins)


def swap_hop(v, hop):
    kind, bit = hop
    return swap_wide(v, 2 << bit) if kind == "wide" else swap_narrow(v, 1 << bit)


class Scatter:
    def __init__(self, own, other, axes, mine, extra=None):
        self.parts = [] if own is None else [(own, ())]
        self.other = other
        self.axes, self.mine = dict(axes), mine
        self.extra = [] if extra is None else [(extra[0], ())]
        self.extra_other = None if extra is None else extra[1]

    def cross(self):
        own = self.parts[0][0]
        self.parts.append((swap_wide(self.other, 1).reshape(own.shape), ()))
        if self.extra:
            self.extra.append((swap_wide(self.extra_other, 1), ()))

    def columns(self, first, count):
        unit = Scatter(None, None, self.axes, self.mine)
        unit.parts = [(v, path + (("columns", (first, count)),)) for v, path in self.parts]
        return unit

    def send(self, hop):
        self.hop = hop
        axis = self.axes.pop(hop, None)
        keep = 0 if axis is None else self.mine[hop]
        more = lambda parts, i: [(v, path + ((axis, i),)) for v, path in parts]
        self.leaving = low_of(more(self.parts, 1 - keep))
        self.parts = more(self.parts, keep)
        if self.extra:
            self.leaving = jnp.concatenate([self.leaving, low_of(more(self.extra, 1 - keep))], -2)
            self.extra = more(self.extra, keep)
        if axis is not None:
            self.axes = {h: a - (a > axis) for h, a in self.axes.items()}

    def receive(self):
        came = swap_hop(self.leaving, self.hop)
        if self.extra:
            rows = self.parts[0][0].shape[-2]
            self.extra.append((came[..., rows:, :], ()))
            came = came[..., :rows, :]
        self.parts.append((came, ()))


def join(values, *units):
    values, came = lax.optimization_barrier((values, [unit.parts[-1][0] for unit in units]))
    for unit, v in zip(units, came):
        unit.parts[-1] = (v, unit.parts[-1][1])
    return values


def start(first, *sends):
    for unit, hop_to in sends:
        unit.send(hop_to)
    first, *leaving = tie(first, *[unit.leaving for unit, _ in sends])
    for (unit, _), v in zip(sends, leaving):
        unit.leaving = v
        unit.receive()
    return first


class Given:
    def __init__(self, giver, taker):
        self.giver, self.taker = giver, taker

    def send(self, hop_to):
        self.hop = hop_to
        self.leaving = low_of(self.giver.parts)

    def receive(self):
        self.taker.parts.append((swap_hop(self.leaving, self.hop), ()))


class Several:
    def __init__(self, *units):
        self.units = units

    def send(self, hop_to):
        self.hop = hop_to
        for unit in self.units:
            unit.send(hop_to)
        self.sizes = [unit.leaving.shape[-1] for unit in self.units]
        self.leaving = jnp.concatenate([unit.leaving for unit in self.units], -1)

    def receive(self):
        came = swap_hop(self.leaving, self.hop)
        first = 0
        for unit, size in zip(self.units, self.sizes):
            taker = unit.taker if isinstance(unit, Given) else unit
            taker.parts.append((came, (("columns", (first, size)),)))
            first += size


def taken(part):
    v, path = part
    starts, sizes, axes = [0] * v.ndim, list(v.shape), list(range(v.ndim))
    for axis, i in path:
        if axis is None:
            sizes[-1] //= 2
            starts[-1] += i * sizes[-1]
        elif axis == "columns":
            starts[-1] += i[0]
            sizes[-1] = i[1]
        else:
            at = axes.pop(axis)
            starts[at], sizes[at] = i, 1
    if all(isinstance(i, int) for i in starts):
        v = lax.slice(v, starts, [i + n for i, n in zip(starts, sizes)])
    else:
        v = lax.dynamic_slice(v, [jnp.int32(i) for i in starts], sizes)
    return v.reshape([sizes[at] for at in axes])


def sum_of(parts, view=lambda v: v):
    return sum(view(taken(p)).astype(f32) for p in parts)


def low_of(parts, view=lambda v: v):
    return sum_of(parts, view).astype(bf16)


def per_device(tokens, segment_ids, attn_weight, vectors, ffn_weight, ffn_bias, out_grad):
    wide, narrow = lax.axis_size("wide"), lax.axis_size("narrow")
    w, z = lax.axis_index("wide"), lax.axis_index("narrow")
    chip, core = lax.div(w, 2), lax.rem(w, 2)
    bits = chip_bits()
    up = list(range(bits))
    down = up[::-1]
    pos = jnp.stack([chip, core, z]).astype(jnp.int32)
    count, features = tokens.shape
    half = features // 2

    rows_each = attn_weight.shape[0]
    each, each_bias = vectors.shape[0], ffn_bias.shape[0]
    small = jnp.concatenate([vectors, ffn_bias, jnp.zeros((features - each - each_bias,), bf16)])
    small = jnp.concatenate([small[None], jnp.zeros((7, features), bf16)])
    v = jnp.concatenate([attn_weight, small])
    attn = v[None]
    units = ffn_weight.shape[2]
    width = units // SUBS
    tail = units - width
    every = range(bits)
    steps = list(range(narrow_bits()))[::-1]
    orders = (up, down)

    def along(v, step, axis):
        return jnp.concatenate([v, swap_narrow(v, 1 << step)], axis)

    late = [(ffn_weight[i, :, tail:], []) for i in range(2)]
    for i, step in enumerate(steps):
        attn = along(attn, step, 0)
        if i == 0:
            (attn, *v) = tie(attn, *[v for v, _ in late])
            late = [(v, done) for v, (_, done) in zip(v, late)]
    for i in every:
        late = [hop(v, done, order[i]) for (v, done), order in zip(late, orders)]
    late = [v.reshape(half, width) for v, _ in late]
    rows = features // wide
    late[1] = late[1].reshape(-1, 2, rows, width).swapaxes(0, 1).reshape(half, width)
    late = jnp.stack(late)
    early, attn, late = tie(ffn_weight[:, :, :tail], attn, late)
    attn = [(attn[:, :, :half], []), (attn[:, :rows_each, half:], [])]
    for i in range(max(bits, len(steps))):
        if i < bits:
            attn = [hop(v, done, order[i]) for (v, done), order in zip(attn, orders)]
        if i < len(steps):
            early = along(early, steps[i], 2)
        early, a, b = tie(early, *[v for v, _ in attn])
        attn = [(a, attn[0][1]), (b, attn[1][1])]
    attn_a, attn_b = [v.reshape((wide // 2,) + v.shape[bits:]) for v, _ in attn]
    early = [(early[which], []) for which in range(2)]
    late, attn_a, attn_b, *firsts = tie(late, attn_a, attn_b, *[v for v, _ in early])
    halves = [attn_a, swap_wide(attn_a, 1), attn_b, swap_wide(attn_b, 1)]
    for i in every[:-1]:
        early = [hop(v, done, order[i]) for v, (_, done), order in zip(firsts, early, orders)]
        if i < len(steps) - 1:
            late = along(late, steps[i], 2)
        if i == 0:
            tokens_now, *firsts = tie(tokens, *[v for v, _ in early])
        else:
            firsts = [v for v, _ in early]
    for step in steps[bits - 1 : -1]:
        late = along(late, step, 2)
    late_came = swap_narrow(late, 1 << steps[-1])

    small = jnp.concatenate([h[:, :, rows_each, : each + each_bias] for h in halves[:2]])
    small = small.reshape(-1, each + each_bias)
    slots = jnp.arange(wide * narrow)
    slot_core, slot_chip, slot_z = (
        slots // (wide * narrow // 2), (slots // narrow) % (wide // 2), slots % narrow,
    )
    slot_w = (slot_chip ^ chip) * 2 + (slot_core ^ core)
    whole_at = slot_w * narrow + (turned(slot_z, narrow_bits()) ^ z)
    bias_at = slot_z * wide + slot_w
    spots = jnp.arange(wide * narrow)[:, None]
    vec_rows = dot((spots == whole_at[None, :]).astype(bf16), small[:, :each]).reshape(8, features)
    bias_rel = dot((spots == bias_at[None, :]).astype(bf16), small[:, each:])
    bias_rel = bias_rel.reshape(narrow, units)
    bias_rel = jnp.concatenate(
        [bias_rel[:, tail:].reshape(1, -1), bias_rel[:, :tail].reshape(1, -1)], 1
    )
    bq, bv, bo, s1, bf, s2, g1, g2 = [vec_rows[i] for i in range(8)]
    slot_vec = to_slots_quick(jnp.stack([g1, s1, bf, g2, s2, s2, s2, s2]), pos, chip, core)
    dy = to_slots_quick(out_grad, pos, chip, core)
    in_kernel = (features // wide) % 128 == 0

    def core_rows(v, which):
        t = v.reshape(count, -1, 2, narrow * rows_each)
        return pick(t, 2, which).reshape(count, half).T

    x_rows = [core_rows(tokens, core), core_rows(tokens, 1 - core)]

    biases = jnp.stack([bq, bv, bo, bo, bo, bo, bo, bo])
    tokens_now, dy, slot_vec, bias_rel, *x_rows = tie(tokens_now, dy, slot_vec, bias_rel, *x_rows)
    *kept, mixed, hidden = run_attend_forward(pos, tokens_now, segment_ids, biases, *halves)
    o_rows = [core_rows(mixed, core), core_rows(mixed, 1 - core)]
    last_hop = [swap_wide(v, 2 << order[-1]) for v, order in zip(firsts, orders)]
    late = [late, late_came]
    firsts = [v.reshape(half // 2, -1) for v in firsts]
    first_crossed = [swap_wide(v, 1) for v in firsts]
    hidden, *late = tie(hidden, *late)
    late_crossed = swap_wide(late[0], 1)
    hidden, *rest = tie(hidden, *first_crossed, *o_rows)
    first_crossed, o_rows = rest[:2], rest[2:]
    if not in_kernel:
        hidden = to_slots(hidden, chip, core)
    hidden, *last_hop = tie(hidden, *[v.reshape(half // 2, -1) for v in last_hop])
    early = [
        (own, v, crossed, swap_wide(v, 1))
        for own, v, crossed in zip(firsts, last_hop, first_crossed)
    ]
    late = [late[0], late_crossed, late[1], swap_wide(late[1], 1)]
    slope, act, u_turned, result, dh, dh_low, dh_own, sums_two, other = run_ffn_forward(
        pos, hidden, slot_vec, dy, bias_rel, late, early
    )
    if not in_kernel:
        result = from_slots(result, chip, core)

    late_width, half_early = narrow * width, narrow * tail // 2
    axes = {("wide", bit): bits - 1 - bit for bit in range(bits)}
    chips = lambda order: [("wide", bit) for bit in order]
    along = [("narrow", bit) for bit in range(narrow_bits())]

    def ffn_unit(own, other):
        own = own.reshape((2,) * bits + own.shape[1:])
        unit = Scatter(own, other, axes, dict.fromkeys(axes, 0))
        unit.cross()
        return unit

    downs = ffn_unit(run_down(dh_own, act), other)
    down_0, down_a, down_b = (
        downs.columns(0, late_width), downs.columns(late_width, half_early),
        downs.columns(late_width + half_early, half_early),
    )
    low = start(
        dh_low, (down_0, along[0]), (down_a, ("wide", down[0])), (down_b, ("wide", up[0]))
    )
    own, other, *rest = run_ffn_backward(pos, low, u_turned, slope, late, early, None)
    own, other, *rest = join([own, other, *rest], down_0, down_a, down_b)
    dbs = [rest[0]]
    up_a = ffn_unit(own, other)
    sends = [(down_a, hop_to) for hop_to in chips(down[1:2])]
    sends += [(down_b, hop_to) for hop_to in chips(up[1:2])]
    low = start(low, (down_0, along[1]), *sends)
    own, other, *rest = run_ffn_backward(
        pos, low, u_turned, slope, late, early, (rest[1], dh, hidden, slot_vec)
    )
    own, other, *rest = join([own, other, *rest], up_a, down_0, down_a, down_b)
    dbs.append(rest[0])
    grad_sum, sums_one = rest[1:]
    up_b = ffn_unit(own, other)
    up_late, up_upper = up_a.columns(0, late_width), up_a.columns(late_width, half_early)
    for unit, order in ((down_a, down), (down_b, up)):
        for hop_to in chips(order[2:]):
            unit.send(hop_to)
            unit.receive()
    if not in_kernel:
        grad_sum = from_slots(grad_sum, chip, core)

    low_bits = bits - 2
    names = chips([bits - 1, bits - 2] + list(range(low_bits))[::-1]) + along[::-1]
    attn_axes = {name: axis for axis, name in enumerate(names)}
    mine = {("wide", bit): bit_of(chip, bit) for bit in range(bits)}
    mine.update({("narrow", bit): bit_of(z, bit) for bit in range(narrow_bits())})
    added = grad_sum
    attn_units = []
    slot_sums = from_slots(jnp.concatenate([sums_one[:3], sums_two[:3]]), chip, core)
    gs1, gg1, gbo, gs2, gg2, gbf = [slot_sums[i] for i in range(6)]
    db = jnp.concatenate([dbs[1], dbs[0][:, late_width:]], 1).reshape(narrow, tail)
    db = jnp.concatenate([db, dbs[0][:, :late_width].reshape(narrow, width)], 1)
    db = db.reshape(narrow, wide, each_bias)
    db = jnp.stack([pick(db, 0, turned(i ^ z, narrow_bits())) for i in range(narrow)], 1)

    def small_rows(vec):
        lanes = lambda v: jnp.pad(v[:, :, None], ((0, 0),) * 3 + ((0, half - v.shape[2]),))
        rows = jnp.concatenate([lanes(vec.reshape(wide, narrow, each)), lanes(db)], 2)
        rows = jnp.pad(rows, ((0, 0), (0, 0), (0, 6), (0, 0)))
        rows = rows.astype(bf16).reshape((2,) * (bits + 1 + narrow_bits()) + rows.shape[2:])
        return pick(rows, bits, core), pick(rows, bits, 1 - core)

    sums = jnp.stack([jnp.zeros_like(gs1)] * 2 + [gbo, gs1, gbf, gs2, gg1, gg2])
    for part in range(2):
        if part == 0:
            sends = [(up_late, ("wide", up[0])), (up_upper, ("wide", down[0]))]
            sends += [(Given(down_b, down_a), along[0])]
            low = start(grad_sum, *sends)
        else:
            sends = [(up_late, hop_to) for hop_to in chips(up[1:2])]
            sends += [(up_upper, hop_to) for hop_to in chips(down[1:2])]
            sends += [(up_b, ("wide", up[0])), (down_a, along[1])]
            sends += [(attn_units[0], ("wide", down[0]))]
            low = start(low, *sends)
        own, other, added, sums = run_attend_backward(
            part, pos, low, added, sums, kept, x_rows + o_rows, halves
        )
        if part == 0:
            ready = (up_late, up_upper, down_a, up_b)
        else:
            ready = (up_late, up_upper, down_a, up_b)
        own, other, added, sums = join([own, other, added, sums], *ready)
        shape = (2,) * len(names) + (rows_each, half)
        unit = Scatter(
            own.reshape(shape), other, attn_axes, mine, None if part == 0 else small_rows(sums)
        )
        unit.cross()
        attn_units.append(unit)
    grad_tokens = added

    def move(unit, *hops):
        for hop_to in hops:
            unit.send(hop_to)
            unit.receive()

    a, b = attn_units
    move(up_late, *chips(up[2:]))
    move(up_upper, *chips(down[2:]))
    move(down_a, *along[2:])
    move(down_0, *along[2:])
    move(b, ("wide", up[0]))
    move(up_b, *chips(up[1:]))
    move(a, *chips(down[1:]))
    move(b, *chips(up[1:]))
    move(Several(up_late, Given(up_upper, up_b)), along[0])
    move(down_0, *chips(down))
    for hop_to in along[1:]:
        move(Several(up_late, up_b), hop_to)
    move(a, *along)
    move(b, *along)
    grad_ffn = jnp.stack(
        [
            jnp.concatenate([sum_of(up_b.parts), sum_of(up_late.parts)], -1),
            jnp.concatenate([sum_of(down_a.parts), sum_of(down_0.parts)], -1),
        ]
    )
    grad_attn = jnp.concatenate([sum_of(u.parts) for u in attn_units], -1)
    tally = sum_of(b.extra)
    return (
        result, grad_tokens, grad_attn, tally[0, :each], grad_ffn, tally[1, :each_bias],
    )


def solution(mesh):
    return jax.shard_map(
        per_device,
        mesh=mesh,
        in_specs=(
            P(("wide", "narrow"), None),
            P(("wide", "narrow"), None),
            P(("wide", "narrow"), None),
            P(("wide", "narrow")),
            P(None, "wide", "narrow"),
            P(("narrow", "wide")),
            P(("wide", "narrow"), None),
        ),
        out_specs=(
            P(("wide", "narrow"), None),
            P(("wide", "narrow"), None),
            P(("wide", "narrow"), None),
            P(("wide", "narrow")),
            P(None, "wide", "narrow"),
            P(("narrow", "wide")),
        ),
        check_vma=False,
    )
```

```python
import functools

import jax
import jax.numpy as jnp
from jax import lax
from jax.experimental import pallas as pl
from jax.experimental.pallas import tpu as pltpu
from jax.sharding import PartitionSpec as P

HEADS = 16
HEAD = 64
SUBS = 4
VMEM_LIMIT = 56 * 1024 * 1024
FFN_LIMIT = 44 * 1024 * 1024
ATTEND_BACK_LIMIT = 56 * 1024 * 1024
BACK_LIMIT = 40 * 1024 * 1024

f32 = jnp.float32
bf16 = jnp.bfloat16

NT = (((1,), (1,)), ((), ()))
TN = (((0,), (0,)), ((), ()))


def dot(a, b):
    return jnp.dot(a, b, preferred_element_type=f32)


def dot_nt(a, b):
    return lax.dot_general(a, b, NT, preferred_element_type=f32)


def dot_tn(a, b):
    return lax.dot_general(a, b, TN, preferred_element_type=f32)


def swap_wide(v, mask):
    size = lax.axis_size("wide")
    return lax.ppermute(v, "wide", [(w, w ^ mask) for w in range(size)])


def swap_narrow(v, mask):
    size = lax.axis_size("narrow")
    return lax.ppermute(v, "narrow", [(z, z ^ mask) for z in range(size)])


def chip_bits():
    return (lax.axis_size("wide") // 2).bit_length() - 1


def narrow_bits():
    return lax.axis_size("narrow").bit_length() - 1


def turned(index, bits):
    out = 0
    for bit in range(bits):
        out = out + ((index >> bit) & 1) * (1 << (bits - 1 - bit))
    return out


def gather_narrow(v, axis):
    for bit in reversed(range(narrow_bits())):
        v = jnp.concatenate([v, swap_narrow(v, 1 << bit)], axis)
    return v


def hop(v, done, bit):
    axis = sum(1 for b in done if b > bit)
    return jnp.stack([v, swap_wide(v, 2 << bit)], axis), done + [bit]


def bit_of(index, bit):
    return lax.rem(lax.div(index, 1 << bit), 2)


def pick(v, axis, index):
    return lax.dynamic_index_in_dim(v, index, axis, keepdims=False)


def to_slots(v, chip, core):
    bits = chip_bits()
    lead = v.shape[:-1]
    block = v.shape[-1] // lax.axis_size("wide")
    t = v.reshape(lead + (2,) * (bits + 1) + (block,))
    n = len(lead)
    for bit in range(bits):
        axis = n + bits - 1 - bit
        t = jnp.where(bit_of(chip, bit) == 1, jnp.flip(t, axis), t)
    t = jnp.where(core == 1, jnp.flip(t, n + bits), t)
    t = jnp.moveaxis(t, n + bits, n)
    return t.reshape(v.shape)


def from_slots(v, chip, core):
    bits = chip_bits()
    lead = v.shape[:-1]
    block = v.shape[-1] // lax.axis_size("wide")
    n = len(lead)
    t = v.reshape(lead + (2,) * (bits + 1) + (block,))
    t = jnp.moveaxis(t, n, n + bits)
    for bit in range(bits):
        axis = n + bits - 1 - bit
        t = jnp.where(bit_of(chip, bit) == 1, jnp.flip(t, axis), t)
    t = jnp.where(core == 1, jnp.flip(t, n + bits), t)
    return t.reshape(v.shape)


def slot_lanes(pos, block, wide, lanes):
    at = ((block % 2) ^ pos[1]) * (wide // 2) + ((block // 2) ^ pos[0])
    return pl.ds(pl.multiple_of(at * lanes, lanes), lanes)


def whole_lanes(pos, slot, wide, lanes):
    core, chip = divmod(slot, wide // 2)
    at = (chip ^ pos[0]) * 2 + (core ^ pos[1])
    return pl.ds(pl.multiple_of(at * lanes, lanes), lanes)


def permute_kernel(wide, pos, v_ref, out_ref):
    lanes = v_ref.shape[1] // wide
    for b in range(wide):
        out_ref[:, slot_lanes(pos, b, wide, lanes)] = v_ref[:, b * lanes : (b + 1) * lanes]


def to_slots_quick(v, pos, chip, core):
    wide = lax.axis_size("wide")
    if (v.shape[1] // wide) % 128:
        return to_slots(v, chip, core)
    return pl.pallas_call(
        functools.partial(permute_kernel, wide),
        in_specs=[pl.BlockSpec(memory_space=pltpu.SMEM), pl.BlockSpec(memory_space=pltpu.VMEM)],
        out_specs=pl.BlockSpec(memory_space=pltpu.VMEM),
        out_shape=jax.ShapeDtypeStruct(v.shape, v.dtype),
        name="permute",
    )(pos, v)


def tie(*values):
    return lax.optimization_barrier(values)


def load_rows(pos, geometry, own, other, matrix, first, count, place, sem):
    narrow, per_matrix, rows = geometry[:3]

    def body(j, carry):
        block = matrix * per_matrix + first + j
        w = block // narrow
        z = block % narrow
        chip = (w // 2) ^ pos[0]
        core = (w % 2) ^ pos[1]
        step = turned(z ^ pos[2], narrow.bit_length() - 1)

        @pl.when(core == 0)
        def _():
            pltpu.make_async_copy(own.at[chip, step, pl.ds(0, rows)], place(j), sem).start()

        @pl.when(core == 1)
        def _():
            pltpu.make_async_copy(other.at[chip, step, pl.ds(0, rows)], place(j), sem).start()

        return carry

    lax.fori_loop(0, count, body, 0)


def attend_forward(
    geometry, pos, x_ref, seg_row, seg_col, vec_ref, bo_ref, own_a, oth_a, own_b, oth_b,
    q_ref, k_ref, v_ref, p_ref, o_ref, h_ref, w_in, w_out, mask, sems,
):
    g = pl.program_id(0)
    steps = pl.num_programs(0)
    _, blocks, rows, wide = geometry
    sources = ((own_a, oth_a), (own_b, oth_b))

    @pl.when(g == 0)
    def _():
        for half in range(2):
            for m in range(3):
                load_rows(
                    pos, geometry, *sources[half], m, 0, blocks,
                    lambda j, half=half, m=m: w_in.at[half, m, pl.ds(pl.multiple_of(j * rows, rows), rows)],
                    sems.at[half],
                )
        for half in range(2):
            load_rows(
                pos, geometry, *sources[half], 3, 0, blocks,
                lambda j, half=half: w_out.at[half, pl.ds(pl.multiple_of(j * rows, rows), rows)],
                sems.at[2],
            )
        mask[...] = jnp.where(seg_col[...] == seg_row[...], 0.0, -1e30).astype(f32)
        pltpu.make_async_copy(w_in.at[0], w_in.at[0], sems.at[0]).wait()

    @pl.when(g == steps // 2)
    def _():
        pltpu.make_async_copy(w_in.at[1], w_in.at[1], sems.at[1]).wait()

    half = g // (steps // 2)
    columns = pl.ds(pl.multiple_of(lax.rem(g, steps // 2) * 256, 256), 256)
    x = x_ref[...]
    query = (dot(x, w_in[half, 0, :, columns]) + vec_ref[0:1, :]).astype(bf16)
    query = query * jnp.asarray(HEAD**-0.5, bf16)
    key = dot(x, w_in[half, 1, :, columns]).astype(bf16)
    value = (dot(x, w_in[half, 2, :, columns]) + vec_ref[1:2, :]).astype(bf16)
    q_ref[...] = query
    k_ref[...] = key
    v_ref[...] = value
    lane = lax.broadcasted_iota(jnp.int32, (1, 128), 1)
    for pair in range(2):
        part = slice(pair * 128, pair * 128 + 128)
        q2, k2, v2 = query[:, part], key[:, part], value[:, part]
        v2t = v2.T
        outs = []
        for sub in range(2):
            mine = (lane < HEAD) if sub == 0 else (lane >= HEAD)
            scores = dot_nt(k2, jnp.where(mine, q2, jnp.zeros_like(q2))) + mask[...]
            raised = jnp.exp(scores - jnp.max(scores, 0, keepdims=True))
            probs = (raised * (1.0 / jnp.sum(raised, 0, keepdims=True))).astype(bf16)
            p_ref[pair * 2 + sub] = probs
            outs.append(dot(v2t[sub * HEAD : sub * HEAD + HEAD], probs))
        mixed = jnp.concatenate(outs, 0).T.astype(bf16)
        o_ref[:, pl.ds(pl.multiple_of(g * 256 + pair * 128, 128), 128)] = mixed

    @pl.when(g == steps - 1)
    def _():
        pltpu.make_async_copy(w_out, w_out, sems.at[2]).wait()
        width = w_out.shape[2]
        lanes = 2 * width // wide
        for half in range(2):
            cols = slice(half * width, half * width + width)
            hidden = x_ref[:, cols].astype(f32) + dot(o_ref[...], w_out[half]) + bo_ref[0:1, cols]
            if lanes % 128:
                h_ref[:, cols] = hidden
            else:
                for b in range(wide // 2):
                    at = slot_lanes(pos, half * (wide // 2) + b, wide, lanes)
                    h_ref[:, at] = hidden[:, b * lanes : (b + 1) * lanes]


def run_attend_forward(pos, tokens, segment_ids, biases, own_a, oth_a, own_b, oth_b):
    count, features = tokens.shape
    rows = own_b.shape[2]
    geometry = (own_b.shape[1], features // rows, rows, own_b.shape[0] * 2)
    groups = features // 256
    whole = lambda *shape: pl.BlockSpec(shape, lambda g, pos: (0,) * len(shape))
    column = pl.BlockSpec((count, 256), lambda g, pos: (0, g))
    anywhere = pl.BlockSpec(memory_space=pl.ANY)
    width = features // 2
    return pl.pallas_call(
        functools.partial(attend_forward, geometry),
        grid_spec=pltpu.PrefetchScalarGridSpec(
            num_scalar_prefetch=1,
            grid=(groups,),
            in_specs=[
                whole(count, features), whole(1, count), whole(count, 1),
                pl.BlockSpec((8, 256), lambda g, pos: (0, g)), whole(8, features),
                anywhere, anywhere, anywhere, anywhere,
            ],
            out_specs=[
                column, column, column,
                pl.BlockSpec((4, count, count), lambda g, pos: (g, 0, 0)),
                whole(count, features), whole(count, features),
            ],
            scratch_shapes=[
                pltpu.VMEM((2, 3, features, width), bf16),
                pltpu.VMEM((2, features, width), bf16),
                pltpu.VMEM((count, count), f32),
                pltpu.SemaphoreType.DMA((3,)),
            ],
        ),
        out_shape=[
            jax.ShapeDtypeStruct((count, features), bf16),
            jax.ShapeDtypeStruct((count, features), bf16),
            jax.ShapeDtypeStruct((count, features), bf16),
            jax.ShapeDtypeStruct((HEADS, count, count), bf16),
            jax.ShapeDtypeStruct((count, features), bf16),
            jax.ShapeDtypeStruct((count, features), f32),
        ],
        compiler_params=pltpu.CompilerParams(
            vmem_limit_bytes=VMEM_LIMIT, dimension_semantics=("arbitrary",)
        ),
        cost_estimate=pl.CostEstimate(
            flops=2 * count * features * features * 8, bytes_accessed=24 << 20, transcendentals=0
        ),
        name="attend_forward",
    )(
        pos, tokens, segment_ids.reshape(1, count), segment_ids.reshape(count, 1),
        biases, biases[2:3] + jnp.zeros((8, 1), f32), own_a, oth_a, own_b, oth_b,
    )


def attend_backward(
    geometry, half, pos, dh_ref, add_ref, sums_in, q_ref, k_ref, v_ref, p_ref, x_own, x_oth, o_own, o_oth,
    own_a, oth_a, own_b, oth_b, gown_ref, goth_ref, dx_ref, bias_ref, w_in, w_out, rows_in, sems,
):
    g = pl.program_id(0)
    features = dh_ref.shape[1]
    _, blocks, rows, _ = geometry
    sources = ((own_a, oth_a), (own_b, oth_b))

    @pl.when(g == 0)
    def _():
        for part in range(2):
            load_rows(
                pos, geometry, *sources[part], 3, half * (blocks // 2), blocks // 2,
                lambda j, part=part: w_out.at[part, pl.ds(pl.multiple_of(j * rows, rows), rows)],
                sems.at[0],
            )
        for m in range(3):
            load_rows(
                pos, geometry, *sources[half], m, 0, blocks,
                lambda j, m=m: w_in.at[m, pl.ds(pl.multiple_of(j * rows, rows), rows)],
                sems.at[1],
            )
        pltpu.make_async_copy(add_ref, dx_ref, sems.at[2]).start()
        for i, source in enumerate((x_own, x_oth, o_own, o_oth)):
            pltpu.make_async_copy(source, rows_in.at[i], sems.at[3]).start()
        pltpu.make_async_copy(w_out, w_out, sems.at[0]).wait()

    span = pl.ds(pl.multiple_of(g * 256, 256), 256)
    width = features // 2
    low = dh_ref[...]
    grad_mixed = (
        dot_nt(low[:, :width], w_out[0, span, :]) + dot_nt(low[:, width:], w_out[1, span, :])
    ).astype(bf16)
    lane = lax.broadcasted_iota(jnp.int32, (1, 128), 1)
    lows = [[], [], []]
    sums = [[], []]
    for pair in range(2):
        part = slice(pair * 128, pair * 128 + 128)
        q2, k2, v2 = q_ref[:, part], k_ref[:, part], v_ref[:, part]
        do2 = grad_mixed[:, part]
        k2t = k2.T
        zero = jnp.zeros_like(q2)
        dv = dk = None
        dqs = []
        for sub in range(2):
            mine = (lane < HEAD) if sub == 0 else (lane >= HEAD)
            probs = p_ref[pair * 2 + sub]
            do_mine = jnp.where(mine, do2, zero)
            grad_probs = dot_nt(v2, do_mine)
            wide_probs = probs.astype(f32)
            inner = jnp.sum(wide_probs * grad_probs, 0, keepdims=True)
            grad_scores = (wide_probs * (grad_probs - inner)).astype(bf16)
            dv_part = dot(probs, do_mine)
            dk_part = dot(grad_scores, jnp.where(mine, q2, zero))
            dv = dv_part if dv is None else dv + dv_part
            dk = dk_part if dk is None else dk + dk_part
            dqs.append(dot(k2t[sub * HEAD : sub * HEAD + HEAD], grad_scores))
        dq = jnp.concatenate(dqs, 0).T * HEAD**-0.5
        sums[0].append(jnp.sum(dq, 0, keepdims=True))
        sums[1].append(jnp.sum(dv, 0, keepdims=True))
        for store, value in zip(lows, (dq, dk, dv)):
            store.append(value.astype(bf16))
    joined = [jnp.concatenate(s, 1) for s in lows]

    @pl.when(g == 0)
    def _():
        pltpu.make_async_copy(rows_in, rows_in, sems.at[3]).wait()

    low = dh_ref[:, pl.ds(pl.multiple_of(half * width + g * 256, 256), 256)]
    for m, right in enumerate(joined + [low]):
        first = 0 if m < 3 else 2
        goth_ref[m] = dot(rows_in[first + 1], right).astype(bf16)
        gown_ref[m] = dot(rows_in[first], right).astype(bf16)

    @pl.when(g == 0)
    def _():
        bias_ref[...] = sums_in[...]

    for row in range(2):
        at = pl.ds(pl.multiple_of(half * width + g * 256, 256), 256)
        bias_ref[row : row + 1, at] = jnp.concatenate(sums[row], 1)

    @pl.when(g == 0)
    def _():
        pltpu.make_async_copy(w_in, w_in, sems.at[1]).wait()
        pltpu.make_async_copy(dx_ref, dx_ref, sems.at[2]).wait()

    dx_ref[...] += (
        dot_nt(joined[0], w_in[0, :, span])
        + dot_nt(joined[1], w_in[1, :, span])
        + dot_nt(joined[2], w_in[2, :, span])
    )


def run_attend_backward(half, pos, grad_sum, added, sums, kept, rows_of, weights):
    q, k, v, probs = kept
    own_a, oth_a, own_b, oth_b = weights
    count, features = q.shape
    rows = own_b.shape[2]
    geometry = (own_b.shape[1], features // rows, rows, own_b.shape[0] * 2)
    groups = features // 512
    whole = lambda *shape: pl.BlockSpec(shape, lambda g, pos: (0,) * len(shape))
    column = pl.BlockSpec((count, 256), lambda g, pos: (0, half * groups + g))
    anywhere = pl.BlockSpec(memory_space=pl.ANY)
    width = features // 2
    return pl.pallas_call(
        functools.partial(attend_backward, geometry, half),
        grid_spec=pltpu.PrefetchScalarGridSpec(
            num_scalar_prefetch=1,
            grid=(groups,),
            in_specs=[
                whole(count, features), anywhere, whole(8, features), column, column, column,
                pl.BlockSpec((4, count, count), lambda g, pos: (half * groups + g, 0, 0)),
                anywhere, anywhere, anywhere, anywhere,
                anywhere, anywhere, anywhere, anywhere,
            ],
            out_specs=[
                pl.BlockSpec((4, width, 256), lambda g, pos: (0, 0, g)),
                pl.BlockSpec((4, width, 256), lambda g, pos: (0, 0, g)),
                whole(count, features),
                whole(8, features),
            ],
            scratch_shapes=[
                pltpu.VMEM((3, features, width), bf16),
                pltpu.VMEM((2, width, width), bf16),
                pltpu.VMEM((4, width, count), bf16),
                pltpu.SemaphoreType.DMA((4,)),
            ],
        ),
        out_shape=[
            jax.ShapeDtypeStruct((4, width, width), bf16),
            jax.ShapeDtypeStruct((4, width, width), bf16),
            jax.ShapeDtypeStruct((count, features), f32),
            jax.ShapeDtypeStruct((8, features), f32),
        ],
        compiler_params=pltpu.CompilerParams(
            vmem_limit_bytes=ATTEND_BACK_LIMIT, dimension_semantics=("arbitrary",)
        ),
        cost_estimate=pl.CostEstimate(
            flops=2 * count * features * features * 6, bytes_accessed=16 << 20, transcendentals=0
        ),
        name="attend_backward",
    )(pos, grad_sum, added, sums, q, k, v, probs, *rows_of, own_a, oth_a, own_b, oth_b)


def moments(hidden):
    center = hidden - jnp.mean(hidden, -1, keepdims=True)
    return center, lax.rsqrt(jnp.mean(center * center, -1, keepdims=True) + 1e-12)


def norm_back(grad, normed, factor):
    return factor * (
        grad
        - jnp.mean(grad, -1, keepdims=True)
        - normed * jnp.mean(grad * normed, -1, keepdims=True)
    )


def gelu_pair(a):
    z = jnp.abs(a) * (0.5**0.5)
    t = 1.0 / (1.0 + 0.3275911 * z)
    poly = t * (
        0.127414796 + t * (-0.142248368 + t * (0.7107068705 + t * (-0.7265760135 + t * 0.5307027145)))
    )
    bell = jnp.exp(-0.5 * (a * a))
    tail = poly * bell
    phi = jnp.where(a >= 0, 1.0 - tail, tail)
    return a * phi, phi + a * (bell * 0.3989422804014327)


ROWS_AT_ONCE = 128
TILE = 1024


def row_blocks(count, step=ROWS_AT_ONCE):
    return [slice(r, r + step) for r in range(0, count, step)]


def turn_into_whole(ref, rows, value, pos, wide):
    features = value.shape[1]
    lanes = features // wide
    if lanes % 128:
        ref[rows, :] = value
    else:
        for slot in range(wide):
            ref[rows, whole_lanes(pos, slot, wide, lanes)] = value[
                :, slot * lanes : (slot + 1) * lanes
            ]


def store_blocks(ref, turned_rows, right):
    chips, block = ref.shape[0], ref.shape[1]
    step = max(1, 256 // block)
    for k in range(0, chips, step):
        value = dot(turned_rows[k * block : (k + step) * block, :], right).astype(bf16)
        for i in range(step):
            ref[k + i] = value[i * block : (i + 1) * block]


def once(*shape):
    return pl.BlockSpec(
        shape, lambda t: (0,) * len(shape), pipeline_mode=pl.Buffered(buffer_count=1)
    )


def odd_last_places(wide):
    half = wide // 2
    return [slot // half * half + slot % 2 * (half // 2) + slot % half // 2 for slot in range(wide)]


def ffn_forward(
    wide, tiles, pos, h_ref, vec, dy, b1, l0a, l0b, l1a, l1b, *refs
):
    ups, downs, refs = refs[:4], refs[4:8], refs[8:]
    (
    slope_ref, act_ref, u_out, result, dh, dh_low, dh_own, sums, oth_ref,
    total, u_low, act_all, dh_turned,
    ) = refs
    t = pl.program_id(0)
    count, features = h_ref.shape
    width = features // 2
    quarter = width // 2
    block = features // wide
    odd_last = [block * p for p in odd_last_places(wide)]

    @pl.when(t == 0)
    def _():
        for r in row_blocks(count):
            center, factor = moments(h_ref[r, :])
            low = (center * factor * (1.0 + vec[0:1, :]) + vec[1:2, :]).astype(bf16)
            u_low[r, :] = low
            u_out[:, r] = low.T

    def tile(ups, downs, first, at, size):
        columns = pl.ds(pl.multiple_of(t * TILE + at, 256), size)
        step = features // len(ups)
        for r in row_blocks(count, 256):
            a = b1[0:1, columns]
            for i, w in enumerate(ups):
                a = a + dot(u_low[r, i * step : i * step + step], w[...])
            act, slope = gelu_pair(a)
            act = act.astype(bf16)
            act_all[r, columns] = act
            act_ref[r, at : at + size] = act
            slope_ref[r, at : at + size] = slope.astype(bf16)
            for i, w in enumerate(downs):
                value = dot_nt(act, w[...])
                if first:
                    total[r, i * step : i * step + step] = value
                else:
                    total[r, i * step : i * step + step] += value

    @pl.when(t == 0)
    def _():
        size = TILE // 2
        tile((l0a.at[0], l0b.at[0]), (l0a.at[1], l0b.at[1]), True, 0, size)
        tile((l1a.at[0], l1b.at[0]), (l1a.at[1], l1b.at[1]), False, size, size)

    @pl.when((t > 0) & (t < tiles))
    def _():
        tile(ups, downs, False, 0, TILE)

    @pl.when(t == tiles - 1)
    def _():
        sums[...] = jnp.zeros_like(sums)
        for r in row_blocks(count):
            center, factor = moments(h_ref[r, :])
            u = center * factor * (1.0 + vec[0:1, :]) + vec[1:2, :]
            ffn = jnp.concatenate([total[r, at : at + block] for at in odd_last], 1)
            center, factor = moments(u + ffn + vec[2:3, :])
            normed = center * factor
            final = (normed * (1.0 + vec[3:4, :]) + vec[4:5, :]).astype(bf16)
            turn_into_whole(result, r, final, pos, wide)
            grad = dy[r, :].astype(f32)
            back = norm_back(grad * (1.0 + vec[3:4, :]), normed, factor)
            dh[r, :] = back
            low = back.astype(bf16)
            for slot, at in enumerate(odd_last):
                dh_low[r, at : at + block] = low[:, slot * block : (slot + 1) * block]
            dh_own[:, r] = low[:, :width].T
            dh_turned[:, r] = low[:, width:].T
            sums[0:1, :] += jnp.sum(grad, 0, keepdims=True)
            sums[1:2, :] += jnp.sum(grad * normed, 0, keepdims=True)
            sums[2:3, :] += jnp.sum(back, 0, keepdims=True)

    @pl.when(t >= tiles)
    def _():
        columns = pl.ds(pl.multiple_of((t - tiles) * TILE, TILE), TILE)
        store_blocks(oth_ref, dh_turned[...], act_all[:, columns])


def down_kernel(left, right, out_ref):
    store_blocks(out_ref, left[...], right[...])


def run_down(dh_own, act):
    width, count = dh_own.shape
    units = act.shape[1]
    wide = lax.axis_size("wide")
    block = 2 * width // wide
    return pl.pallas_call(
        down_kernel,
        grid=(units // TILE,),
        in_specs=[once(width, count), pl.BlockSpec((count, TILE), lambda t: (0, t))],
        out_specs=pl.BlockSpec((wide // 2, block, TILE), lambda t: (0, 0, t)),
        out_shape=jax.ShapeDtypeStruct((wide // 2, block, units), bf16),
        compiler_params=pltpu.CompilerParams(
            vmem_limit_bytes=24 << 20, dimension_semantics=("arbitrary",)
        ),
        cost_estimate=pl.CostEstimate(
            flops=2 * count * width * units, bytes_accessed=9 << 20, transcendentals=0
        ),
        name="down_own",
    )(dh_own, act)


def run_ffn_forward(pos, hidden, vec, dy, b1, late, early):
    count, features = hidden.shape
    wide = lax.axis_size("wide")
    width = features // 2
    units = b1.shape[1]
    tiles = units // TILE
    block = features // wide
    tall = pl.BlockSpec((width // 2, TILE), lambda t: (0, jnp.clip(t - 1, 0, tiles - 2)))
    grads = pl.BlockSpec((wide // 2, block, TILE), lambda t: (0, 0, jnp.maximum(t - tiles, 0)))
    grad_shape = jax.ShapeDtypeStruct((wide // 2, block, units), bf16)
    return pl.pallas_call(
        functools.partial(ffn_forward, wide, tiles),
        grid=(2 * tiles,),
        in_specs=[
            pl.BlockSpec(memory_space=pltpu.SMEM), once(count, features), once(8, features),
            once(count, features), once(1, units),
        ] + [once(2, width, TILE // 2)] * 4 + [tall] * 8,
        out_specs=[
            pl.BlockSpec((count, TILE), lambda t: (0, jnp.minimum(t, tiles - 1))),
            pl.BlockSpec((count, TILE), lambda t: (0, jnp.minimum(t, tiles - 1))),
            once(features, count), once(count, features), once(count, features),
            once(count, features), once(width, count), once(8, features), grads,
        ],
        out_shape=[
            jax.ShapeDtypeStruct((count, units), bf16),
            jax.ShapeDtypeStruct((count, units), bf16),
            jax.ShapeDtypeStruct((features, count), bf16),
            jax.ShapeDtypeStruct((count, features), bf16),
            jax.ShapeDtypeStruct((count, features), f32),
            jax.ShapeDtypeStruct((count, features), bf16),
            jax.ShapeDtypeStruct((width, count), bf16),
            jax.ShapeDtypeStruct((8, features), f32),
            grad_shape,
        ],
        scratch_shapes=[
            pltpu.VMEM((count, features), f32),
            pltpu.VMEM((count, features), bf16),
            pltpu.VMEM((count, units), bf16),
            pltpu.VMEM((width, count), bf16),
        ],
        compiler_params=pltpu.CompilerParams(
            vmem_limit_bytes=FFN_LIMIT, dimension_semantics=("arbitrary",)
        ),
        cost_estimate=pl.CostEstimate(
            flops=6 * count * features * units, bytes_accessed=34 << 20, transcendentals=0
        ),
        name="ffn_forward",
    )(pos, hidden, vec, dy, b1, *late, *early[0], *early[1])


def ffn_backward(wide, last, *refs):
    pos, dh_low, u_turned, slope, *refs = refs
    late, refs = ([], refs) if last else (refs[:4], refs[4:])
    ups, downs, refs = refs[:4], refs[4:8], refs[8:]
    if last:
        du_in, dh, h_ref, vec, own_ref, oth_ref, db_ref, dh1, dh1_low, sums, total, low_all = refs
    else:
        own_ref, oth_ref, db_ref, total, low_all = refs
    t = pl.program_id(0)
    count, features = dh_low.shape
    width = features // 2

    def tile(ups, downs, before):
        db = 0.0
        step = features // len(ups)
        for r in row_blocks(count, 256):
            grad = 0.0
            for i, w in enumerate(downs):
                grad = grad + dot(dh_low[r, i * step : i * step + step], w[...])
            grad = grad * slope[r, :].astype(f32)
            db = db + jnp.sum(grad, 0, keepdims=True)
            low = grad.astype(bf16)
            low_all[r, :] = low
            for i, w in enumerate(ups):
                value = dot_nt(low, w[...])
                columns = slice(i * step, i * step + step)
                total[r, columns] = value if before is None else before[r, columns] + value
        db_ref[...] = db
        low = low_all[...]
        store_blocks(oth_ref, u_turned[width:, :], low)
        store_blocks(own_ref, u_turned[:width, :], low)

    if last:

        @pl.when(t == 0)
        def _():
            tile(ups, downs, du_in)

    else:
        for i in range(2):

            @pl.when(t == i)
            def _(i=i):
                a, b = late[2 * i : 2 * i + 2]
                tile((a.at[0], b.at[0]), (a.at[1], b.at[1]), total if i else None)

    @pl.when(t >= (1 if last else 2))
    def _():
        tile(ups, downs, total)

    if last:

        @pl.when(t == pl.num_programs(0) - 1)
        def _():
            sums[...] = jnp.zeros_like(sums)
            for r in row_blocks(count):
                center, factor = moments(h_ref[r, :])
                normed = center * factor
                du = total[r, :] + dh[r, :]
                back = norm_back(du * (1.0 + vec[0:1, :]), normed, factor)
                turn_into_whole(dh1, r, back, pos, wide)
                turn_into_whole(dh1_low, r, back.astype(bf16), pos, wide)
                sums[0:1, :] += jnp.sum(du, 0, keepdims=True)
                sums[1:2, :] += jnp.sum(du * normed, 0, keepdims=True)
                sums[2:3, :] += jnp.sum(back, 0, keepdims=True)


BACK_TILE = 512


def run_ffn_backward(pos, dh_low, u_turned, slope, late, early, tail):
    count, features = dh_low.shape
    wide = lax.axis_size("wide")
    width = features // 2
    block = features // wide
    last = tail is not None
    late_tiles = 2
    assert late[0].shape[2] == BACK_TILE
    half_tiles = early[0][0].shape[1] // BACK_TILE // 2
    tiles = half_tiles if last else late_tiles + half_tiles
    ins = [pos, dh_low, u_turned, slope]
    if last:
        at_slope = lambda t: (0, late_tiles + t)
        at_early = lambda t: (0, t)
    else:
        at_slope = lambda t: (0, jnp.where(t < late_tiles, t, t + half_tiles))
        at_early = lambda t: (0, half_tiles + jnp.maximum(t - late_tiles, 0))
    in_specs = [
        pl.BlockSpec(memory_space=pltpu.SMEM), once(count, features), once(features, count),
        pl.BlockSpec((count, BACK_TILE), at_slope),
    ]
    if not last:
        in_specs += [once(2, width, BACK_TILE)] * 4
        ins += list(late)
    in_specs += [pl.BlockSpec((width // 2, BACK_TILE), at_early)] * 8
    ins += [*early[0], *early[1]]
    grads = pl.BlockSpec((wide // 2, block, BACK_TILE), lambda t: (0, 0, t))
    grad_shape = jax.ShapeDtypeStruct((wide // 2, block, tiles * BACK_TILE), bf16)
    out_specs = [grads, grads, pl.BlockSpec((1, BACK_TILE), lambda t: (0, t))]
    out_shape = [grad_shape, grad_shape, jax.ShapeDtypeStruct((1, tiles * BACK_TILE), f32)]
    scratch = [pltpu.VMEM((count, BACK_TILE), bf16)]
    if last:
        ins += list(tail)
        in_specs += [once(count, features)] * 3 + [once(8, features)]
        out_specs += [once(count, features), once(count, features), once(8, features)]
        out_shape += [
            jax.ShapeDtypeStruct((count, features), f32),
            jax.ShapeDtypeStruct((count, features), bf16),
            jax.ShapeDtypeStruct((8, features), f32),
        ]
        scratch = [pltpu.VMEM((count, features), f32)] + scratch
    else:
        out_specs.append(once(count, features))
        out_shape.append(jax.ShapeDtypeStruct((count, features), f32))
    return pl.pallas_call(
        functools.partial(ffn_backward, wide, last),
        grid=(tiles,),
        in_specs=in_specs,
        out_specs=out_specs,
        out_shape=out_shape,
        scratch_shapes=scratch,
        compiler_params=pltpu.CompilerParams(
            vmem_limit_bytes=BACK_LIMIT, dimension_semantics=("arbitrary",)
        ),
        cost_estimate=pl.CostEstimate(
            flops=6 * count * features * tiles * BACK_TILE, bytes_accessed=17 << 20, transcendentals=0
        ),
        name="ffn_backward",
    )(*ins)


def swap_hop(v, hop):
    kind, bit = hop
    return swap_wide(v, 2 << bit) if kind == "wide" else swap_narrow(v, 1 << bit)


class Scatter:
    def __init__(self, own, other, axes, mine, extra=None):
        self.parts = [] if own is None else [(own, ())]
        self.other = other
        self.axes, self.mine = dict(axes), mine
        self.extra = [] if extra is None else [(extra[0], ())]
        self.extra_other = None if extra is None else extra[1]

    def cross(self):
        own = self.parts[0][0]
        self.parts.append((swap_wide(self.other, 1).reshape(own.shape), ()))
        if self.extra:
            self.extra.append((swap_wide(self.extra_other, 1), ()))

    def columns(self, first, count):
        unit = Scatter(None, None, self.axes, self.mine)
        unit.parts = [(v, path + (("columns", (first, count)),)) for v, path in self.parts]
        return unit

    def plan(self, hop):
        self.hop = hop
        axis = self.axes.pop(hop, None)
        keep = 0 if axis is None else self.mine[hop]
        more = lambda parts, i: [(v, path + ((axis, i),)) for v, path in parts]
        leaving, extra = more(self.parts, 1 - keep), more(self.extra, 1 - keep)
        self.parts, self.extra = more(self.parts, keep), more(self.extra, keep)
        if axis is not None:
            self.axes = {h: a - (a > axis) for h, a in self.axes.items()}
        return leaving, extra

    def send(self, hop):
        leaving, extra = self.plan(hop)
        self.leaving = low_of(leaving)
        if extra:
            self.leaving = jnp.concatenate([self.leaving, low_of(extra)], -2)

    def receive(self):
        came = swap_hop(self.leaving, self.hop)
        if self.extra:
            rows = self.parts[0][0].shape[-2]
            self.extra.append((came[..., rows:, :], ()))
            came = came[..., :rows, :]
        self.parts.append((came, ()))


def join(values, *units):
    values, came = lax.optimization_barrier((values, [unit.parts[-1][0] for unit in units]))
    for unit, v in zip(units, came):
        unit.parts[-1] = (v, unit.parts[-1][1])
    return values


def start(first, *sends, fused=True):
    plans = [unit.plan(hop_to) for unit, hop_to in sends]
    assert not any(extra for _, extra in plans)
    first, *leaving = tie(
        first, *(low_many if fused else lambda s: [low_of(p) for p in s])([p for p, _ in plans])
    )
    for (unit, _), v in zip(sends, leaving):
        unit.leaving = v
        unit.receive()
    return first


class Given:
    def __init__(self, giver, taker):
        self.giver, self.taker = giver, taker

    def plan(self, hop_to):
        self.hop = hop_to
        return self.giver.parts, []

    def send(self, hop_to):
        self.leaving = low_of(self.plan(hop_to)[0])

    def receive(self):
        self.taker.parts.append((swap_hop(self.leaving, self.hop), ()))


class Several:
    def __init__(self, *units):
        self.units = units

    def send(self, hop_to):
        self.hop = hop_to
        for unit in self.units:
            unit.send(hop_to)
        self.sizes = [unit.leaving.shape[-1] for unit in self.units]
        self.leaving = jnp.concatenate([unit.leaving for unit in self.units], -1)

    def receive(self):
        came = swap_hop(self.leaving, self.hop)
        first = 0
        for unit, size in zip(self.units, self.sizes):
            taker = unit.taker if isinstance(unit, Given) else unit
            taker.parts.append((came, (("columns", (first, size)),)))
            first += size


def low_many_kernel(slices, *refs):
    count = len(slices)
    flat = [cut for cuts in slices for cut in cuts]
    ins, outs = refs[: len(flat)], refs[len(flat) : len(flat) + count]
    buffers, sems = refs[len(flat) + count : -1], refs[-1]
    copies = []
    for i, (starts, sizes, axes) in enumerate(flat):
        at = tuple(
            pl.ds(first, size) if axis in axes else first
            for axis, (first, size) in enumerate(zip(starts, sizes))
        )
        copies.append(pltpu.make_async_copy(ins[i].at[at], buffers[i], sems.at[i]))
        copies[-1].start()
    i = 0
    for out, cuts in zip(outs, slices):
        total = None
        for _ in cuts:
            copies[i].wait()
            value = buffers[i][...].astype(f32)
            total = value if total is None else total + value
            i += 1
        out[...] = total.astype(bf16)


def low_many(sends):
    fit = lambda cut: (
        all(isinstance(i, int) for i in cut[0])
        and cut[0][-1] % 128 == 0
        and cut[1][-1] % 128 == 0
        and len(cut[2]) >= 2
    )
    cuts = [[cut_of(part) for part in parts] for parts in sends]
    chosen = [i for i, some in enumerate(cuts) if all(fit(cut) for cut in some)]
    out = [None if i in chosen else low_of(parts) for i, parts in enumerate(sends)]
    if not chosen:
        return out
    shape = lambda cut: tuple(cut[1][axis] for axis in cut[2])
    arrays = [v for i in chosen for v, _ in sends[i]]
    buffers = [pltpu.VMEM(shape(cut), bf16) for i in chosen for cut in cuts[i]]
    results = pl.pallas_call(
        functools.partial(low_many_kernel, [cuts[i] for i in chosen]),
        in_specs=[pl.BlockSpec(memory_space=pl.ANY)] * len(arrays),
        out_specs=[pl.BlockSpec(memory_space=pltpu.VMEM)] * len(chosen),
        out_shape=[jax.ShapeDtypeStruct(shape(cuts[i][0]), bf16) for i in chosen],
        scratch_shapes=buffers + [pltpu.SemaphoreType.DMA((len(arrays),))],
        compiler_params=pltpu.CompilerParams(vmem_limit_bytes=VMEM_LIMIT),
        name="sums",
    )(*arrays)
    for i, v in zip(chosen, results):
        out[i] = v
    return out


def cut_of(part):
    v, path = part
    starts, sizes, axes = [0] * v.ndim, list(v.shape), list(range(v.ndim))
    for axis, i in path:
        if axis is None:
            sizes[-1] //= 2
            starts[-1] += i * sizes[-1]
        elif axis == "columns":
            starts[-1] += i[0]
            sizes[-1] = i[1]
        else:
            at = axes.pop(axis)
            starts[at], sizes[at] = i, 1
    return starts, sizes, axes


def taken(part):
    v = part[0]
    starts, sizes, axes = cut_of(part)
    if all(isinstance(i, int) for i in starts):
        v = lax.slice(v, starts, [i + n for i, n in zip(starts, sizes)])
    else:
        v = lax.dynamic_slice(v, [jnp.int32(i) for i in starts], sizes)
    return v.reshape([sizes[at] for at in axes])


def sum_of(parts, view=lambda v: v):
    return sum(view(taken(p)).astype(f32) for p in parts)


def low_of(parts, view=lambda v: v):
    return sum_of(parts, view).astype(bf16)


def per_device(tokens, segment_ids, attn_weight, vectors, ffn_weight, ffn_bias, out_grad):
    wide, narrow = lax.axis_size("wide"), lax.axis_size("narrow")
    w, z = lax.axis_index("wide"), lax.axis_index("narrow")
    chip, core = lax.div(w, 2), lax.rem(w, 2)
    bits = chip_bits()
    up = list(range(bits))
    down = up[::-1]
    pos = jnp.stack([chip, core, z]).astype(jnp.int32)
    count, features = tokens.shape
    half = features // 2

    rows_each = attn_weight.shape[0]
    each, each_bias = vectors.shape[0], ffn_bias.shape[0]
    small = jnp.concatenate([vectors, ffn_bias, jnp.zeros((features - each - each_bias,), bf16)])
    small = jnp.concatenate([small[None], jnp.zeros((7, features), bf16)])
    v = jnp.concatenate([attn_weight, small])
    attn = v[None]
    units = ffn_weight.shape[2]
    width = units // SUBS
    tail = units - width
    every = range(bits)
    steps = list(range(narrow_bits()))[::-1]
    orders = (up, down)

    def along(v, step, axis):
        return jnp.concatenate([v, swap_narrow(v, 1 << step)], axis)

    late = [(ffn_weight[i, :, tail:], []) for i in range(2)]
    for i, step in enumerate(steps):
        attn = along(attn, step, 0)
        if i == 0:
            (attn, *v) = tie(attn, *[v for v, _ in late])
            late = [(v, done) for v, (_, done) in zip(v, late)]
    for i in every:
        late = [hop(v, done, order[i]) for (v, done), order in zip(late, orders)]
    late = [v.reshape(half, width) for v, _ in late]
    rows = features // wide
    late[1] = late[1].reshape(-1, 2, rows, width).swapaxes(0, 1).reshape(half, width)
    late = jnp.stack(late)
    early, attn, late = tie(ffn_weight[:, :, :tail], attn, late)
    attn = [(attn[:, :, :half], []), (attn[:, :rows_each, half:], [])]
    for i in range(max(bits, len(steps))):
        if i < bits:
            attn = [hop(v, done, order[i]) for (v, done), order in zip(attn, orders)]
        if i < len(steps):
            early = along(early, steps[i], 2)
        early, a, b = tie(early, *[v for v, _ in attn])
        attn = [(a, attn[0][1]), (b, attn[1][1])]
    attn_a, attn_b = [v.reshape((wide // 2,) + v.shape[bits:]) for v, _ in attn]
    early = [(early[which], []) for which in range(2)]
    late, attn_a, attn_b, *firsts = tie(late, attn_a, attn_b, *[v for v, _ in early])
    halves = [attn_a, swap_wide(attn_a, 1), attn_b, swap_wide(attn_b, 1)]
    for i in every[:-1]:
        early = [hop(v, done, order[i]) for v, (_, done), order in zip(firsts, early, orders)]
        if i < len(steps) - 1:
            late = along(late, steps[i], 2)
        if i == 0:
            tokens_now, *firsts = tie(tokens, *[v for v, _ in early])
        else:
            firsts = [v for v, _ in early]
    for step in steps[bits - 1 : -1]:
        late = along(late, step, 2)
    late_came = swap_narrow(late, 1 << steps[-1])

    small = jnp.concatenate([h[:, :, rows_each, : each + each_bias] for h in halves[:2]])
    small = small.reshape(-1, each + each_bias)
    slots = jnp.arange(wide * narrow)
    slot_core, slot_chip, slot_z = (
        slots // (wide * narrow // 2), (slots // narrow) % (wide // 2), slots % narrow,
    )
    slot_w = (slot_chip ^ chip) * 2 + (slot_core ^ core)
    whole_at = slot_w * narrow + (turned(slot_z, narrow_bits()) ^ z)
    bias_at = slot_z * wide + slot_w
    spots = jnp.arange(wide * narrow)[:, None]
    vec_rows = dot((spots == whole_at[None, :]).astype(bf16), small[:, :each]).reshape(8, features)
    bias_rel = dot((spots == bias_at[None, :]).astype(bf16), small[:, each:])
    bias_rel = bias_rel.reshape(narrow, units)
    bias_rel = jnp.concatenate(
        [bias_rel[:, tail:].reshape(1, -1), bias_rel[:, :tail].reshape(1, -1)], 1
    )
    bq, bv, bo, s1, bf, s2, g1, g2 = [vec_rows[i] for i in range(8)]
    slot_vec = to_slots_quick(jnp.stack([g1, s1, bf, g2, s2, s2, s2, s2]), pos, chip, core)
    dy = to_slots_quick(out_grad, pos, chip, core)
    in_kernel = (features // wide) % 128 == 0

    def core_rows(v, which):
        t = v.reshape(count, -1, 2, narrow * rows_each)
        return pick(t, 2, which).reshape(count, half).T

    x_rows = [core_rows(tokens, core), core_rows(tokens, 1 - core)]

    biases = jnp.stack([bq, bv, bo, bo, bo, bo, bo, bo])
    tokens_now, dy, slot_vec, bias_rel, *x_rows = tie(tokens_now, dy, slot_vec, bias_rel, *x_rows)
    *kept, mixed, hidden = run_attend_forward(pos, tokens_now, segment_ids, biases, *halves)
    o_rows = [core_rows(mixed, core), core_rows(mixed, 1 - core)]
    last_hop = [swap_wide(v, 2 << order[-1]) for v, order in zip(firsts, orders)]
    late = [late, late_came]
    firsts = [v.reshape(half // 2, -1) for v in firsts]
    first_crossed = [swap_wide(v, 1) for v in firsts]
    hidden, *late = tie(hidden, *late)
    late_crossed = [swap_wide(v, 1) for v in late]
    hidden, *rest = tie(hidden, *first_crossed, *o_rows)
    first_crossed, o_rows = rest[:2], rest[2:]
    if not in_kernel:
        hidden = to_slots(hidden, chip, core)
    last_hop = [v.reshape(half // 2, -1) for v in last_hop]
    hidden, late_0, late_1, *last_hop = tie(hidden, *late_crossed, *last_hop)
    early = [
        (own, v, crossed, swap_wide(v, 1))
        for own, v, crossed in zip(firsts, last_hop, first_crossed)
    ]
    late = [late[0], late_0, late[1], late_1]
    slope, act, u_turned, result, dh, dh_low, dh_own, sums_two, other = run_ffn_forward(
        pos, hidden, slot_vec, dy, bias_rel, late, early
    )
    if not in_kernel:
        result = from_slots(result, chip, core)

    late_width, half_early = narrow * width, narrow * tail // 2
    axes = {("wide", bit): bits - 1 - bit for bit in range(bits)}
    chips = lambda order: [("wide", bit) for bit in order]
    along = [("narrow", bit) for bit in range(narrow_bits())]

    def ffn_unit(own, other):
        own = own.reshape((2,) * bits + own.shape[1:])
        unit = Scatter(own, other, axes, dict.fromkeys(axes, 0))
        unit.cross()
        return unit

    downs = ffn_unit(run_down(dh_own, act), other)
    down_0, down_a, down_b = (
        downs.columns(0, late_width), downs.columns(late_width, half_early),
        downs.columns(late_width + half_early, half_early),
    )
    low = start(
        dh_low, (down_0, along[0]), (down_a, ("wide", down[0])), (down_b, ("wide", up[0])),
        fused=False,
    )
    own, other, *rest = run_ffn_backward(pos, low, u_turned, slope, late, early, None)
    own, other, *rest = join([own, other, *rest], down_0, down_a, down_b)
    dbs = [rest[0]]
    up_a = ffn_unit(own, other)
    sends = [(down_a, hop_to) for hop_to in chips(down[1:2])]
    sends += [(down_b, hop_to) for hop_to in chips(up[1:2])]
    low = start(low, (down_0, along[1]), *sends)
    own, other, *rest = run_ffn_backward(
        pos, low, u_turned, slope, late, early, (rest[1], dh, hidden, slot_vec)
    )
    own, other, *rest = join([own, other, *rest], up_a, down_0, down_a, down_b)
    dbs.append(rest[0])
    grad_sum, grad_low, sums_one = rest[1:]
    up_b = ffn_unit(own, other)
    up_late, up_upper = up_a.columns(0, late_width), up_a.columns(late_width, half_early)
    for unit, order in ((down_a, down), (down_b, up)):
        for hop_to in chips(order[2:]):
            unit.send(hop_to)
            unit.receive()
    if not in_kernel:
        grad_sum = from_slots(grad_sum, chip, core)
        grad_low = from_slots(grad_low, chip, core)

    low_bits = bits - 2
    names = chips([bits - 1, bits - 2] + list(range(low_bits))[::-1]) + along[::-1]
    attn_axes = {name: axis for axis, name in enumerate(names)}
    mine = {("wide", bit): bit_of(chip, bit) for bit in range(bits)}
    mine.update({("narrow", bit): bit_of(z, bit) for bit in range(narrow_bits())})
    added = grad_sum
    attn_units = []
    slot_sums = from_slots(jnp.concatenate([sums_one[:3], sums_two[:3]]), chip, core)
    gs1, gg1, gbo, gs2, gg2, gbf = [slot_sums[i] for i in range(6)]
    db = jnp.concatenate([dbs[1], dbs[0][:, late_width:]], 1).reshape(narrow, tail)
    db = jnp.concatenate([db, dbs[0][:, :late_width].reshape(narrow, width)], 1)
    db = db.reshape(narrow, wide, each_bias)
    db = jnp.stack([pick(db, 0, turned(i ^ z, narrow_bits())) for i in range(narrow)], 1)

    def small_rows(vec):
        lanes = lambda v: jnp.pad(v[:, :, None], ((0, 0),) * 3 + ((0, half - v.shape[2]),))
        rows = jnp.concatenate([lanes(vec.reshape(wide, narrow, each)), lanes(db)], 2)
        rows = jnp.pad(rows, ((0, 0), (0, 0), (0, 6), (0, 0)))
        rows = rows.astype(bf16).reshape((2,) * (bits + 1 + narrow_bits()) + rows.shape[2:])
        return pick(rows, bits, core), pick(rows, bits, 1 - core)

    sums = jnp.stack([jnp.zeros_like(gs1)] * 2 + [gbo, gs1, gbf, gs2, gg1, gg2])
    for part in range(2):
        if part == 0:
            sends = [(up_late, ("wide", up[0])), (up_upper, ("wide", down[0]))]
            sends += [(Given(down_b, down_a), along[0])]
            low = start(grad_low, *sends)
        else:
            sends = [(up_late, hop_to) for hop_to in chips(up[1:2])]
            sends += [(up_upper, hop_to) for hop_to in chips(down[1:2])]
            sends += [(up_b, ("wide", up[0])), (down_a, along[1])]
            sends += [(attn_units[0], ("wide", down[0]))]
            low = start(low, *sends)
        own, other, added, sums = run_attend_backward(
            part, pos, low, added, sums, kept, x_rows + o_rows, halves
        )
        if part == 0:
            ready = (up_late, up_upper, down_a, up_b)
        else:
            ready = (up_late, up_upper, down_a, up_b, down_0)
        if part == 0:
            own, other, added, sums = join([own, other, added, sums], *ready)
        else:
            own, added, sums = join([own, added, sums], *ready)
        shape = (2,) * len(names) + (rows_each, half)
        unit = Scatter(
            own.reshape(shape), other, attn_axes, mine, None if part == 0 else small_rows(sums)
        )
        unit.cross()
        attn_units.append(unit)
    grad_tokens = added

    def move(unit, *hops):
        for hop_to in hops:
            unit.send(hop_to)
            unit.receive()

    a, b = attn_units
    move(up_late, *chips(up[2:]))
    move(up_upper, *chips(down[2:]))
    move(down_a, *along[2:])
    move(down_0, *along[2:])
    move(b, ("wide", up[0]))
    move(up_b, *chips(up[1:]))
    move(a, *chips(down[1:]))
    move(b, *chips(up[1:]))
    move(Several(up_late, Given(up_upper, up_b)), along[0])
    move(down_0, *chips(down))
    for hop_to in along[1:]:
        move(Several(up_late, up_b), hop_to)
    move(a, *along)
    move(b, *along)
    grad_ffn = jnp.stack(
        [
            jnp.concatenate([sum_of(up_b.parts), sum_of(up_late.parts)], -1),
            jnp.concatenate([sum_of(down_a.parts), sum_of(down_0.parts)], -1),
        ]
    )
    grad_attn = jnp.concatenate([sum_of(u.parts) for u in attn_units], -1)
    tally = sum_of(b.extra)
    return (
        result, grad_tokens, grad_attn, tally[0, :each], grad_ffn, tally[1, :each_bias],
    )


def solution(mesh):
    return jax.shard_map(
        per_device,
        mesh=mesh,
        in_specs=(
            P(("wide", "narrow"), None),
            P(("wide", "narrow"), None),
            P(("wide", "narrow"), None),
            P(("wide", "narrow")),
            P(None, "wide", "narrow"),
            P(("narrow", "wide")),
            P(("wide", "narrow"), None),
        ),
        out_specs=(
            P(("wide", "narrow"), None),
            P(("wide", "narrow"), None),
            P(("wide", "narrow"), None),
            P(("wide", "narrow")),
            P(None, "wide", "narrow"),
            P(("narrow", "wide")),
        ),
        check_vma=False,
    )
```

```python
import functools

import jax
import jax.numpy as jnp
from jax import lax
from jax.experimental import pallas as pl
from jax.experimental.pallas import tpu as pltpu
from jax.sharding import PartitionSpec as P

HEADS = 16
HEAD = 64
SUBS = 4
VMEM_LIMIT = 56 * 1024 * 1024
FFN_LIMIT = 44 * 1024 * 1024
ATTEND_BACK_LIMIT = 56 * 1024 * 1024
BACK_LIMIT = 40 * 1024 * 1024

f32 = jnp.float32
bf16 = jnp.bfloat16

NT = (((1,), (1,)), ((), ()))
TN = (((0,), (0,)), ((), ()))


def dot(a, b):
    return jnp.dot(a, b, preferred_element_type=f32)


def dot_nt(a, b):
    return lax.dot_general(a, b, NT, preferred_element_type=f32)


def dot_tn(a, b):
    return lax.dot_general(a, b, TN, preferred_element_type=f32)


def swap_wide(v, mask):
    size = lax.axis_size("wide")
    return lax.ppermute(v, "wide", [(w, w ^ mask) for w in range(size)])


def swap_narrow(v, mask):
    size = lax.axis_size("narrow")
    return lax.ppermute(v, "narrow", [(z, z ^ mask) for z in range(size)])


def chip_bits():
    return (lax.axis_size("wide") // 2).bit_length() - 1


def narrow_bits():
    return lax.axis_size("narrow").bit_length() - 1


def turned(index, bits):
    out = 0
    for bit in range(bits):
        out = out + ((index >> bit) & 1) * (1 << (bits - 1 - bit))
    return out


def gather_narrow(v, axis):
    for bit in reversed(range(narrow_bits())):
        v = jnp.concatenate([v, swap_narrow(v, 1 << bit)], axis)
    return v


def hop(v, done, bit):
    axis = sum(1 for b in done if b > bit)
    return jnp.stack([v, swap_wide(v, 2 << bit)], axis), done + [bit]


def bit_of(index, bit):
    return lax.rem(lax.div(index, 1 << bit), 2)


def pick(v, axis, index):
    return lax.dynamic_index_in_dim(v, index, axis, keepdims=False)


def to_slots(v, chip, core):
    bits = chip_bits()
    lead = v.shape[:-1]
    block = v.shape[-1] // lax.axis_size("wide")
    t = v.reshape(lead + (2,) * (bits + 1) + (block,))
    n = len(lead)
    for bit in range(bits):
        axis = n + bits - 1 - bit
        t = jnp.where(bit_of(chip, bit) == 1, jnp.flip(t, axis), t)
    t = jnp.where(core == 1, jnp.flip(t, n + bits), t)
    t = jnp.moveaxis(t, n + bits, n)
    return t.reshape(v.shape)


def from_slots(v, chip, core):
    bits = chip_bits()
    lead = v.shape[:-1]
    block = v.shape[-1] // lax.axis_size("wide")
    n = len(lead)
    t = v.reshape(lead + (2,) * (bits + 1) + (block,))
    t = jnp.moveaxis(t, n, n + bits)
    for bit in range(bits):
        axis = n + bits - 1 - bit
        t = jnp.where(bit_of(chip, bit) == 1, jnp.flip(t, axis), t)
    t = jnp.where(core == 1, jnp.flip(t, n + bits), t)
    return t.reshape(v.shape)


def slot_lanes(pos, block, wide, lanes):
    at = ((block % 2) ^ pos[1]) * (wide // 2) + ((block // 2) ^ pos[0])
    return pl.ds(pl.multiple_of(at * lanes, lanes), lanes)


def whole_lanes(pos, slot, wide, lanes):
    core, chip = divmod(slot, wide // 2)
    at = (chip ^ pos[0]) * 2 + (core ^ pos[1])
    return pl.ds(pl.multiple_of(at * lanes, lanes), lanes)


def permute_kernel(wide, pos, v_ref, out_ref):
    lanes = v_ref.shape[1] // wide
    for b in range(wide):
        out_ref[:, slot_lanes(pos, b, wide, lanes)] = v_ref[:, b * lanes : (b + 1) * lanes]


def to_slots_quick(v, pos, chip, core):
    wide = lax.axis_size("wide")
    if (v.shape[1] // wide) % 128:
        return to_slots(v, chip, core)
    return pl.pallas_call(
        functools.partial(permute_kernel, wide),
        in_specs=[pl.BlockSpec(memory_space=pltpu.SMEM), pl.BlockSpec(memory_space=pltpu.VMEM)],
        out_specs=pl.BlockSpec(memory_space=pltpu.VMEM),
        out_shape=jax.ShapeDtypeStruct(v.shape, v.dtype),
        name="permute",
    )(pos, v)


def tie(*values):
    return lax.optimization_barrier(values)


def load_rows(pos, geometry, own, other, matrix, first, count, place, sem):
    narrow, per_matrix, rows = geometry[:3]

    def body(j, carry):
        block = matrix * per_matrix + first + j
        w = block // narrow
        z = block % narrow
        chip = (w // 2) ^ pos[0]
        core = (w % 2) ^ pos[1]
        step = turned(z ^ pos[2], narrow.bit_length() - 1)

        @pl.when(core == 0)
        def _():
            pltpu.make_async_copy(own.at[chip, step, pl.ds(0, rows)], place(j), sem).start()

        @pl.when(core == 1)
        def _():
            pltpu.make_async_copy(other.at[chip, step, pl.ds(0, rows)], place(j), sem).start()

        return carry

    lax.fori_loop(0, count, body, 0)


def attend_forward(
    geometry, pos, x_ref, seg_row, seg_col, vec_ref, bo_ref, own_a, oth_a, own_b, oth_b,
    q_ref, k_ref, v_ref, p_ref, o_ref, h_ref, w_in, w_out, mask, sems,
):
    g = pl.program_id(0)
    steps = pl.num_programs(0)
    _, blocks, rows, wide = geometry
    sources = ((own_a, oth_a), (own_b, oth_b))

    @pl.when(g == 0)
    def _():
        for half in range(2):
            for m in range(3):
                load_rows(
                    pos, geometry, *sources[half], m, 0, blocks,
                    lambda j, half=half, m=m: w_in.at[half, m, pl.ds(pl.multiple_of(j * rows, rows), rows)],
                    sems.at[half],
                )
        for half in range(2):
            load_rows(
                pos, geometry, *sources[half], 3, 0, blocks,
                lambda j, half=half: w_out.at[half, pl.ds(pl.multiple_of(j * rows, rows), rows)],
                sems.at[2],
            )
        mask[...] = jnp.where(seg_col[...] == seg_row[...], 0.0, -1e30).astype(f32)
        pltpu.make_async_copy(w_in.at[0], w_in.at[0], sems.at[0]).wait()

    @pl.when(g == steps // 2)
    def _():
        pltpu.make_async_copy(w_in.at[1], w_in.at[1], sems.at[1]).wait()

    half = g // (steps // 2)
    columns = pl.ds(pl.multiple_of(lax.rem(g, steps // 2) * 256, 256), 256)
    x = x_ref[...]
    query = (dot(x, w_in[half, 0, :, columns]) + vec_ref[0:1, :]).astype(bf16)
    query = query * jnp.asarray(HEAD**-0.5, bf16)
    key = dot(x, w_in[half, 1, :, columns]).astype(bf16)
    value = (dot(x, w_in[half, 2, :, columns]) + vec_ref[1:2, :]).astype(bf16)
    q_ref[...] = query
    k_ref[...] = key
    v_ref[...] = value
    lane = lax.broadcasted_iota(jnp.int32, (1, 128), 1)
    for pair in range(2):
        part = slice(pair * 128, pair * 128 + 128)
        q2, k2, v2 = query[:, part], key[:, part], value[:, part]
        v2t = v2.T
        outs = []
        for sub in range(2):
            mine = (lane < HEAD) if sub == 0 else (lane >= HEAD)
            scores = dot_nt(k2, jnp.where(mine, q2, jnp.zeros_like(q2))) + mask[...]
            raised = jnp.exp(scores - jnp.max(scores, 0, keepdims=True))
            probs = (raised * (1.0 / jnp.sum(raised, 0, keepdims=True))).astype(bf16)
            p_ref[pair * 2 + sub] = probs
            outs.append(dot(v2t[sub * HEAD : sub * HEAD + HEAD], probs))
        mixed = jnp.concatenate(outs, 0).T.astype(bf16)
        o_ref[:, pl.ds(pl.multiple_of(g * 256 + pair * 128, 128), 128)] = mixed

    @pl.when(g == steps - 1)
    def _():
        pltpu.make_async_copy(w_out, w_out, sems.at[2]).wait()
        width = w_out.shape[2]
        lanes = 2 * width // wide
        for half in range(2):
            cols = slice(half * width, half * width + width)
            hidden = x_ref[:, cols].astype(f32) + dot(o_ref[...], w_out[half]) + bo_ref[0:1, cols]
            if lanes % 128:
                h_ref[:, cols] = hidden
            else:
                for b in range(wide // 2):
                    at = slot_lanes(pos, half * (wide // 2) + b, wide, lanes)
                    h_ref[:, at] = hidden[:, b * lanes : (b + 1) * lanes]


def run_attend_forward(pos, tokens, segment_ids, biases, own_a, oth_a, own_b, oth_b):
    count, features = tokens.shape
    rows = own_b.shape[2]
    geometry = (own_b.shape[1], features // rows, rows, own_b.shape[0] * 2)
    groups = features // 256
    whole = lambda *shape: pl.BlockSpec(shape, lambda g, pos: (0,) * len(shape))
    column = pl.BlockSpec((count, 256), lambda g, pos: (0, g))
    anywhere = pl.BlockSpec(memory_space=pl.ANY)
    width = features // 2
    return pl.pallas_call(
        functools.partial(attend_forward, geometry),
        grid_spec=pltpu.PrefetchScalarGridSpec(
            num_scalar_prefetch=1,
            grid=(groups,),
            in_specs=[
                whole(count, features), whole(1, count), whole(count, 1),
                pl.BlockSpec((8, 256), lambda g, pos: (0, g)), whole(8, features),
                anywhere, anywhere, anywhere, anywhere,
            ],
            out_specs=[
                column, column, column,
                pl.BlockSpec((4, count, count), lambda g, pos: (g, 0, 0)),
                whole(count, features), whole(count, features),
            ],
            scratch_shapes=[
                pltpu.VMEM((2, 3, features, width), bf16),
                pltpu.VMEM((2, features, width), bf16),
                pltpu.VMEM((count, count), f32),
                pltpu.SemaphoreType.DMA((3,)),
            ],
        ),
        out_shape=[
            jax.ShapeDtypeStruct((count, features), bf16),
            jax.ShapeDtypeStruct((count, features), bf16),
            jax.ShapeDtypeStruct((count, features), bf16),
            jax.ShapeDtypeStruct((HEADS, count, count), bf16),
            jax.ShapeDtypeStruct((count, features), bf16),
            jax.ShapeDtypeStruct((count, features), f32),
        ],
        compiler_params=pltpu.CompilerParams(
            vmem_limit_bytes=VMEM_LIMIT, dimension_semantics=("arbitrary",)
        ),
        cost_estimate=pl.CostEstimate(
            flops=2 * count * features * features * 8, bytes_accessed=24 << 20, transcendentals=0
        ),
        name="attend_forward",
    )(
        pos, tokens, segment_ids.reshape(1, count), segment_ids.reshape(count, 1),
        biases, biases[2:3] + jnp.zeros((8, 1), f32), own_a, oth_a, own_b, oth_b,
    )


def attend_backward(
    geometry, half, pos, dh_ref, add_ref, sums_in, q_ref, k_ref, v_ref, p_ref, x_own, x_oth, o_own, o_oth,
    own_a, oth_a, own_b, oth_b, gown_ref, goth_ref, dx_ref, bias_ref, w_in, w_out, rows_in, sems,
):
    g = pl.program_id(0)
    features = dh_ref.shape[1]
    _, blocks, rows, _ = geometry
    sources = ((own_a, oth_a), (own_b, oth_b))

    @pl.when(g == 0)
    def _():
        for part in range(2):
            load_rows(
                pos, geometry, *sources[part], 3, half * (blocks // 2), blocks // 2,
                lambda j, part=part: w_out.at[part, pl.ds(pl.multiple_of(j * rows, rows), rows)],
                sems.at[0],
            )
        for m in range(3):
            load_rows(
                pos, geometry, *sources[half], m, 0, blocks,
                lambda j, m=m: w_in.at[m, pl.ds(pl.multiple_of(j * rows, rows), rows)],
                sems.at[1],
            )
        pltpu.make_async_copy(add_ref, dx_ref, sems.at[2]).start()
        for i, source in enumerate((x_own, x_oth, o_own, o_oth)):
            pltpu.make_async_copy(source, rows_in.at[i], sems.at[3]).start()
        pltpu.make_async_copy(w_out, w_out, sems.at[0]).wait()

    span = pl.ds(pl.multiple_of(g * 256, 256), 256)
    width = features // 2
    low = dh_ref[...]
    grad_mixed = (
        dot_nt(low[:, :width], w_out[0, span, :]) + dot_nt(low[:, width:], w_out[1, span, :])
    ).astype(bf16)
    lane = lax.broadcasted_iota(jnp.int32, (1, 128), 1)
    lows = [[], [], []]
    sums = [[], []]
    for pair in range(2):
        part = slice(pair * 128, pair * 128 + 128)
        q2, k2, v2 = q_ref[:, part], k_ref[:, part], v_ref[:, part]
        do2 = grad_mixed[:, part]
        k2t = k2.T
        zero = jnp.zeros_like(q2)
        dv = dk = None
        dqs = []
        for sub in range(2):
            mine = (lane < HEAD) if sub == 0 else (lane >= HEAD)
            probs = p_ref[pair * 2 + sub]
            do_mine = jnp.where(mine, do2, zero)
            grad_probs = dot_nt(v2, do_mine)
            wide_probs = probs.astype(f32)
            inner = jnp.sum(wide_probs * grad_probs, 0, keepdims=True)
            grad_scores = (wide_probs * (grad_probs - inner)).astype(bf16)
            dv_part = dot(probs, do_mine)
            dk_part = dot(grad_scores, jnp.where(mine, q2, zero))
            dv = dv_part if dv is None else dv + dv_part
            dk = dk_part if dk is None else dk + dk_part
            dqs.append(dot(k2t[sub * HEAD : sub * HEAD + HEAD], grad_scores))
        dq = jnp.concatenate(dqs, 0).T * HEAD**-0.5
        sums[0].append(jnp.sum(dq, 0, keepdims=True))
        sums[1].append(jnp.sum(dv, 0, keepdims=True))
        for store, value in zip(lows, (dq, dk, dv)):
            store.append(value.astype(bf16))
    joined = [jnp.concatenate(s, 1) for s in lows]

    @pl.when(g == 0)
    def _():
        pltpu.make_async_copy(rows_in, rows_in, sems.at[3]).wait()

    low = dh_ref[:, pl.ds(pl.multiple_of(half * width + g * 256, 256), 256)]
    for m, right in enumerate(joined + [low]):
        first = 0 if m < 3 else 2
        goth_ref[m] = dot(rows_in[first + 1], right).astype(bf16)
        gown_ref[m] = dot(rows_in[first], right).astype(bf16)

    @pl.when(g == 0)
    def _():
        bias_ref[...] = sums_in[...]

    for row in range(2):
        at = pl.ds(pl.multiple_of(half * width + g * 256, 256), 256)
        bias_ref[row : row + 1, at] = jnp.concatenate(sums[row], 1)

    @pl.when(g == 0)
    def _():
        pltpu.make_async_copy(w_in, w_in, sems.at[1]).wait()
        pltpu.make_async_copy(dx_ref, dx_ref, sems.at[2]).wait()

    dx_ref[...] += (
        dot_nt(joined[0], w_in[0, :, span])
        + dot_nt(joined[1], w_in[1, :, span])
        + dot_nt(joined[2], w_in[2, :, span])
    )


def run_attend_backward(half, pos, grad_sum, added, sums, kept, rows_of, weights):
    q, k, v, probs = kept
    own_a, oth_a, own_b, oth_b = weights
    count, features = q.shape
    rows = own_b.shape[2]
    geometry = (own_b.shape[1], features // rows, rows, own_b.shape[0] * 2)
    groups = features // 512
    whole = lambda *shape: pl.BlockSpec(shape, lambda g, pos: (0,) * len(shape))
    column = pl.BlockSpec((count, 256), lambda g, pos: (0, half * groups + g))
    anywhere = pl.BlockSpec(memory_space=pl.ANY)
    width = features // 2
    return pl.pallas_call(
        functools.partial(attend_backward, geometry, half),
        grid_spec=pltpu.PrefetchScalarGridSpec(
            num_scalar_prefetch=1,
            grid=(groups,),
            in_specs=[
                whole(count, features), anywhere, whole(8, features), column, column, column,
                pl.BlockSpec((4, count, count), lambda g, pos: (half * groups + g, 0, 0)),
                anywhere, anywhere, anywhere, anywhere,
                anywhere, anywhere, anywhere, anywhere,
            ],
            out_specs=[
                pl.BlockSpec((4, width, 256), lambda g, pos: (0, 0, g)),
                pl.BlockSpec((4, width, 256), lambda g, pos: (0, 0, g)),
                whole(count, features),
                whole(8, features),
            ],
            scratch_shapes=[
                pltpu.VMEM((3, features, width), bf16),
                pltpu.VMEM((2, width, width), bf16),
                pltpu.VMEM((4, width, count), bf16),
                pltpu.SemaphoreType.DMA((4,)),
            ],
        ),
        out_shape=[
            jax.ShapeDtypeStruct((4, width, width), bf16),
            jax.ShapeDtypeStruct((4, width, width), bf16),
            jax.ShapeDtypeStruct((count, features), f32),
            jax.ShapeDtypeStruct((8, features), f32),
        ],
        compiler_params=pltpu.CompilerParams(
            vmem_limit_bytes=ATTEND_BACK_LIMIT, dimension_semantics=("arbitrary",)
        ),
        cost_estimate=pl.CostEstimate(
            flops=2 * count * features * features * 6, bytes_accessed=16 << 20, transcendentals=0
        ),
        name="attend_backward",
    )(pos, grad_sum, added, sums, q, k, v, probs, *rows_of, own_a, oth_a, own_b, oth_b)


def moments(hidden):
    center = hidden - jnp.mean(hidden, -1, keepdims=True)
    return center, lax.rsqrt(jnp.mean(center * center, -1, keepdims=True) + 1e-12)


def norm_back(grad, normed, factor):
    return factor * (
        grad
        - jnp.mean(grad, -1, keepdims=True)
        - normed * jnp.mean(grad * normed, -1, keepdims=True)
    )


def gelu_pair(a):
    z = jnp.abs(a) * (0.5**0.5)
    t = 1.0 / (1.0 + 0.3275911 * z)
    poly = t * (
        0.127414796 + t * (-0.142248368 + t * (0.7107068705 + t * (-0.7265760135 + t * 0.5307027145)))
    )
    bell = jnp.exp(-0.5 * (a * a))
    tail = poly * bell
    phi = jnp.where(a >= 0, 1.0 - tail, tail)
    return a * phi, phi + a * (bell * 0.3989422804014327)


ROWS_AT_ONCE = 128
TILE = 1024


def row_blocks(count, step=ROWS_AT_ONCE):
    return [slice(r, r + step) for r in range(0, count, step)]


def turn_into_whole(ref, rows, value, pos, wide):
    features = value.shape[1]
    lanes = features // wide
    if lanes % 128:
        ref[rows, :] = value
    else:
        for slot in range(wide):
            ref[rows, whole_lanes(pos, slot, wide, lanes)] = value[
                :, slot * lanes : (slot + 1) * lanes
            ]


def store_blocks(ref, turned_rows, right):
    chips, block = ref.shape[0], ref.shape[1]
    step = max(1, 256 // block)
    for k in range(0, chips, step):
        value = dot(turned_rows[k * block : (k + step) * block, :], right).astype(bf16)
        for i in range(step):
            ref[k + i] = value[i * block : (i + 1) * block]


def once(*shape):
    return pl.BlockSpec(
        shape, lambda t: (0,) * len(shape), pipeline_mode=pl.Buffered(buffer_count=1)
    )


def odd_last_places(wide):
    half = wide // 2
    return [slot // half * half + slot % 2 * (half // 2) + slot % half // 2 for slot in range(wide)]


def ffn_forward(
    wide, tiles, pos, h_ref, vec, dy, b1, l0a, l0b, l1a, l1b, *refs
):
    ups, downs, refs = refs[:4], refs[4:8], refs[8:]
    (
    slope_ref, act_ref, u_out, result, dh, dh_low, dh_own, sums, oth_ref,
    total, u_low, act_all, dh_turned,
    ) = refs
    t = pl.program_id(0)
    count, features = h_ref.shape
    width = features // 2
    quarter = width // 2
    block = features // wide
    odd_last = [block * p for p in odd_last_places(wide)]

    @pl.when(t == 0)
    def _():
        for r in row_blocks(count):
            center, factor = moments(h_ref[r, :])
            low = (center * factor * (1.0 + vec[0:1, :]) + vec[1:2, :]).astype(bf16)
            u_low[r, :] = low
            u_out[:, r] = low.T

    def tile(ups, downs, first, at, size):
        columns = pl.ds(pl.multiple_of(t * TILE + at, 256), size)
        step = features // len(ups)
        for r in row_blocks(count, 512):
            a = b1[0:1, columns]
            for i, w in enumerate(ups):
                a = a + dot(u_low[r, i * step : i * step + step], w[...])
            act, slope = gelu_pair(a)
            act = act.astype(bf16)
            act_all[r, columns] = act
            act_ref[r, at : at + size] = act
            slope_ref[r, at : at + size] = slope.astype(bf16)
            for i, w in enumerate(downs):
                value = dot_nt(act, w[...])
                if first:
                    total[r, i * step : i * step + step] = value
                else:
                    total[r, i * step : i * step + step] += value

    @pl.when(t == 0)
    def _():
        size = TILE // 2
        tile((l0a.at[0], l0b.at[0]), (l0a.at[1], l0b.at[1]), True, 0, size)
        tile((l1a.at[0], l1b.at[0]), (l1a.at[1], l1b.at[1]), False, size, size)

    @pl.when((t > 0) & (t < tiles))
    def _():
        tile(ups, downs, False, 0, TILE)

    @pl.when(t == tiles - 1)
    def _():
        sums[...] = jnp.zeros_like(sums)
        for r in row_blocks(count):
            center, factor = moments(h_ref[r, :])
            u = center * factor * (1.0 + vec[0:1, :]) + vec[1:2, :]
            ffn = jnp.concatenate([total[r, at : at + block] for at in odd_last], 1)
            center, factor = moments(u + ffn + vec[2:3, :])
            normed = center * factor
            final = (normed * (1.0 + vec[3:4, :]) + vec[4:5, :]).astype(bf16)
            turn_into_whole(result, r, final, pos, wide)
            grad = dy[r, :].astype(f32)
            back = norm_back(grad * (1.0 + vec[3:4, :]), normed, factor)
            dh[r, :] = back
            low = back.astype(bf16)
            for slot, at in enumerate(odd_last):
                dh_low[r, at : at + block] = low[:, slot * block : (slot + 1) * block]
            dh_own[:, r] = low[:, :width].T
            dh_turned[:, r] = low[:, width:].T
            sums[0:1, :] += jnp.sum(grad, 0, keepdims=True)
            sums[1:2, :] += jnp.sum(grad * normed, 0, keepdims=True)
            sums[2:3, :] += jnp.sum(back, 0, keepdims=True)

    @pl.when(t >= tiles)
    def _():
        columns = pl.ds(pl.multiple_of((t - tiles) * TILE, TILE), TILE)
        store_blocks(oth_ref, dh_turned[...], act_all[:, columns])


def down_kernel(left, right, out_ref):
    store_blocks(out_ref, left[...], right[...])


def run_down(dh_own, act):
    width, count = dh_own.shape
    units = act.shape[1]
    wide = lax.axis_size("wide")
    block = 2 * width // wide
    return pl.pallas_call(
        down_kernel,
        grid=(units // TILE,),
        in_specs=[once(width, count), pl.BlockSpec((count, TILE), lambda t: (0, t))],
        out_specs=pl.BlockSpec((wide // 2, block, TILE), lambda t: (0, 0, t)),
        out_shape=jax.ShapeDtypeStruct((wide // 2, block, units), bf16),
        compiler_params=pltpu.CompilerParams(
            vmem_limit_bytes=24 << 20, dimension_semantics=("arbitrary",)
        ),
        cost_estimate=pl.CostEstimate(
            flops=2 * count * width * units, bytes_accessed=9 << 20, transcendentals=0
        ),
        name="down_own",
    )(dh_own, act)


def run_ffn_forward(pos, hidden, vec, dy, b1, late, early):
    count, features = hidden.shape
    wide = lax.axis_size("wide")
    width = features // 2
    units = b1.shape[1]
    tiles = units // TILE
    block = features // wide
    tall = pl.BlockSpec((width // 2, TILE), lambda t: (0, jnp.clip(t - 1, 0, tiles - 2)))
    grads = pl.BlockSpec((wide // 2, block, TILE), lambda t: (0, 0, jnp.maximum(t - tiles, 0)))
    grad_shape = jax.ShapeDtypeStruct((wide // 2, block, units), bf16)
    return pl.pallas_call(
        functools.partial(ffn_forward, wide, tiles),
        grid=(2 * tiles,),
        in_specs=[
            pl.BlockSpec(memory_space=pltpu.SMEM), once(count, features), once(8, features),
            once(count, features), once(1, units),
        ] + [once(2, width, TILE // 2)] * 4 + [tall] * 8,
        out_specs=[
            pl.BlockSpec((count, TILE), lambda t: (0, jnp.minimum(t, tiles - 1))),
            pl.BlockSpec((count, TILE), lambda t: (0, jnp.minimum(t, tiles - 1))),
            once(features, count), once(count, features), once(count, features),
            once(count, features), once(width, count), once(8, features), grads,
        ],
        out_shape=[
            jax.ShapeDtypeStruct((count, units), bf16),
            jax.ShapeDtypeStruct((count, units), bf16),
            jax.ShapeDtypeStruct((features, count), bf16),
            jax.ShapeDtypeStruct((count, features), bf16),
            jax.ShapeDtypeStruct((count, features), f32),
            jax.ShapeDtypeStruct((count, features), bf16),
            jax.ShapeDtypeStruct((width, count), bf16),
            jax.ShapeDtypeStruct((8, features), f32),
            grad_shape,
        ],
        scratch_shapes=[
            pltpu.VMEM((count, features), f32),
            pltpu.VMEM((count, features), bf16),
            pltpu.VMEM((count, units), bf16),
            pltpu.VMEM((width, count), bf16),
        ],
        compiler_params=pltpu.CompilerParams(
            vmem_limit_bytes=FFN_LIMIT, dimension_semantics=("arbitrary",)
        ),
        cost_estimate=pl.CostEstimate(
            flops=6 * count * features * units, bytes_accessed=34 << 20, transcendentals=0
        ),
        name="ffn_forward",
    )(pos, hidden, vec, dy, b1, *late, *early[0], *early[1])


def ffn_backward(wide, last, *refs):
    pos, dh_low, u_turned, slope, *refs = refs
    late, refs = ([], refs) if last else (refs[:4], refs[4:])
    ups, downs, refs = refs[:4], refs[4:8], refs[8:]
    if last:
        du_in, dh, h_ref, vec, own_ref, oth_ref, db_ref, dh1, dh1_low, sums, total, low_all = refs
    else:
        own_ref, oth_ref, db_ref, total, low_all = refs
    t = pl.program_id(0)
    count, features = dh_low.shape
    width = features // 2

    def tile(ups, downs, before):
        db = 0.0
        step = features // len(ups)
        for r in row_blocks(count, 512):
            grad = 0.0
            for i, w in enumerate(downs):
                grad = grad + dot(dh_low[r, i * step : i * step + step], w[...])
            grad = grad * slope[r, :].astype(f32)
            db = db + jnp.sum(grad, 0, keepdims=True)
            low = grad.astype(bf16)
            low_all[r, :] = low
            for i, w in enumerate(ups):
                value = dot_nt(low, w[...])
                columns = slice(i * step, i * step + step)
                total[r, columns] = value if before is None else before[r, columns] + value
        db_ref[...] = db
        low = low_all[...]
        store_blocks(oth_ref, u_turned[width:, :], low)
        store_blocks(own_ref, u_turned[:width, :], low)

    if last:

        @pl.when(t == 0)
        def _():
            tile(ups, downs, du_in)

    else:
        for i in range(2):

            @pl.when(t == i)
            def _(i=i):
                a, b = late[2 * i : 2 * i + 2]
                tile((a.at[0], b.at[0]), (a.at[1], b.at[1]), total if i else None)

    @pl.when(t >= (1 if last else 2))
    def _():
        tile(ups, downs, total)

    if last:

        @pl.when(t == pl.num_programs(0) - 1)
        def _():
            sums[...] = jnp.zeros_like(sums)
            for r in row_blocks(count):
                center, factor = moments(h_ref[r, :])
                normed = center * factor
                du = total[r, :] + dh[r, :]
                back = norm_back(du * (1.0 + vec[0:1, :]), normed, factor)
                turn_into_whole(dh1, r, back, pos, wide)
                turn_into_whole(dh1_low, r, back.astype(bf16), pos, wide)
                sums[0:1, :] += jnp.sum(du, 0, keepdims=True)
                sums[1:2, :] += jnp.sum(du * normed, 0, keepdims=True)
                sums[2:3, :] += jnp.sum(back, 0, keepdims=True)


BACK_TILE = 512


def run_ffn_backward(pos, dh_low, u_turned, slope, late, early, tail):
    count, features = dh_low.shape
    wide = lax.axis_size("wide")
    width = features // 2
    block = features // wide
    last = tail is not None
    late_tiles = 2
    assert late[0].shape[2] == BACK_TILE
    half_tiles = early[0][0].shape[1] // BACK_TILE // 2
    tiles = half_tiles if last else late_tiles + half_tiles
    ins = [pos, dh_low, u_turned, slope]
    if last:
        at_slope = lambda t: (0, late_tiles + t)
        at_early = lambda t: (0, t)
    else:
        at_slope = lambda t: (0, jnp.where(t < late_tiles, t, t + half_tiles))
        at_early = lambda t: (0, half_tiles + jnp.maximum(t - late_tiles, 0))
    in_specs = [
        pl.BlockSpec(memory_space=pltpu.SMEM), once(count, features), once(features, count),
        pl.BlockSpec((count, BACK_TILE), at_slope),
    ]
    if not last:
        in_specs += [once(2, width, BACK_TILE)] * 4
        ins += list(late)
    in_specs += [pl.BlockSpec((width // 2, BACK_TILE), at_early)] * 8
    ins += [*early[0], *early[1]]
    grads = pl.BlockSpec((wide // 2, block, BACK_TILE), lambda t: (0, 0, t))
    grad_shape = jax.ShapeDtypeStruct((wide // 2, block, tiles * BACK_TILE), bf16)
    out_specs = [grads, grads, pl.BlockSpec((1, BACK_TILE), lambda t: (0, t))]
    out_shape = [grad_shape, grad_shape, jax.ShapeDtypeStruct((1, tiles * BACK_TILE), f32)]
    scratch = [pltpu.VMEM((count, BACK_TILE), bf16)]
    if last:
        ins += list(tail)
        in_specs += [once(count, features)] * 3 + [once(8, features)]
        out_specs += [once(count, features), once(count, features), once(8, features)]
        out_shape += [
            jax.ShapeDtypeStruct((count, features), f32),
            jax.ShapeDtypeStruct((count, features), bf16),
            jax.ShapeDtypeStruct((8, features), f32),
        ]
        scratch = [pltpu.VMEM((count, features), f32)] + scratch
    else:
        out_specs.append(once(count, features))
        out_shape.append(jax.ShapeDtypeStruct((count, features), f32))
    return pl.pallas_call(
        functools.partial(ffn_backward, wide, last),
        grid=(tiles,),
        in_specs=in_specs,
        out_specs=out_specs,
        out_shape=out_shape,
        scratch_shapes=scratch,
        compiler_params=pltpu.CompilerParams(
            vmem_limit_bytes=BACK_LIMIT, dimension_semantics=("arbitrary",)
        ),
        cost_estimate=pl.CostEstimate(
            flops=6 * count * features * tiles * BACK_TILE, bytes_accessed=17 << 20, transcendentals=0
        ),
        name="ffn_backward",
    )(*ins)


def swap_hop(v, hop):
    kind, bit = hop
    return swap_wide(v, 2 << bit) if kind == "wide" else swap_narrow(v, 1 << bit)


class Scatter:
    def __init__(self, own, other, axes, mine, extra=None):
        self.parts = [] if own is None else [(own, ())]
        self.other = other
        self.axes, self.mine = dict(axes), mine
        self.extra = [] if extra is None else [(extra[0], ())]
        self.extra_other = None if extra is None else extra[1]

    def cross(self):
        own = self.parts[0][0]
        self.parts.append((swap_wide(self.other, 1).reshape(own.shape), ()))
        if self.extra:
            self.extra.append((swap_wide(self.extra_other, 1), ()))

    def columns(self, first, count):
        unit = Scatter(None, None, self.axes, self.mine)
        unit.parts = [(v, path + (("columns", (first, count)),)) for v, path in self.parts]
        return unit

    def plan(self, hop):
        self.hop = hop
        axis = self.axes.pop(hop, None)
        keep = 0 if axis is None else self.mine[hop]
        more = lambda parts, i: [(v, path + ((axis, i),)) for v, path in parts]
        leaving, extra = more(self.parts, 1 - keep), more(self.extra, 1 - keep)
        self.parts, self.extra = more(self.parts, keep), more(self.extra, keep)
        if axis is not None:
            self.axes = {h: a - (a > axis) for h, a in self.axes.items()}
        return leaving, extra

    def send(self, hop):
        leaving, extra = self.plan(hop)
        self.leaving = low_of(leaving)
        if extra:
            self.leaving = jnp.concatenate([self.leaving, low_of(extra)], -2)

    def receive(self):
        came = swap_hop(self.leaving, self.hop)
        if self.extra:
            rows = self.parts[0][0].shape[-2]
            self.extra.append((came[..., rows:, :], ()))
            came = came[..., :rows, :]
        self.parts.append((came, ()))


def join(values, *units):
    values, came = lax.optimization_barrier((values, [unit.parts[-1][0] for unit in units]))
    for unit, v in zip(units, came):
        unit.parts[-1] = (v, unit.parts[-1][1])
    return values


def start(first, *sends, fused=True):
    plans = [unit.plan(hop_to) for unit, hop_to in sends]
    assert not any(extra for _, extra in plans)
    first, *leaving = tie(
        first, *(low_many if fused else lambda s: [low_of(p) for p in s])([p for p, _ in plans])
    )
    for (unit, _), v in zip(sends, leaving):
        unit.leaving = v
        unit.receive()
    return first


class Given:
    def __init__(self, giver, taker):
        self.giver, self.taker = giver, taker

    def plan(self, hop_to):
        self.hop = hop_to
        return self.giver.parts, []

    def send(self, hop_to):
        self.leaving = low_of(self.plan(hop_to)[0])

    def receive(self):
        self.taker.parts.append((swap_hop(self.leaving, self.hop), ()))


class Several:
    def __init__(self, *units):
        self.units = units

    def send(self, hop_to):
        self.hop = hop_to
        for unit in self.units:
            unit.send(hop_to)
        self.sizes = [unit.leaving.shape[-1] for unit in self.units]
        self.leaving = jnp.concatenate([unit.leaving for unit in self.units], -1)

    def receive(self):
        came = swap_hop(self.leaving, self.hop)
        first = 0
        for unit, size in zip(self.units, self.sizes):
            taker = unit.taker if isinstance(unit, Given) else unit
            taker.parts.append((came, (("columns", (first, size)),)))
            first += size


def low_many_kernel(slices, *refs):
    count = len(slices)
    flat = [cut for cuts in slices for cut in cuts]
    ins, outs = refs[: len(flat)], refs[len(flat) : len(flat) + count]
    buffers, sems = refs[len(flat) + count : -1], refs[-1]
    copies = []
    for i, (starts, sizes, axes) in enumerate(flat):
        at = tuple(
            pl.ds(first, size) if axis in axes else first
            for axis, (first, size) in enumerate(zip(starts, sizes))
        )
        copies.append(pltpu.make_async_copy(ins[i].at[at], buffers[i], sems.at[i]))
        copies[-1].start()
    i = 0
    for out, cuts in zip(outs, slices):
        total = None
        for _ in cuts:
            copies[i].wait()
            value = buffers[i][...].astype(f32)
            total = value if total is None else total + value
            i += 1
        out[...] = total.astype(bf16)


def low_many(sends):
    fit = lambda cut: (
        all(isinstance(i, int) for i in cut[0])
        and cut[0][-1] % 128 == 0
        and cut[1][-1] % 128 == 0
        and len(cut[2]) >= 2
    )
    cuts = [[cut_of(part) for part in parts] for parts in sends]
    chosen = [i for i, some in enumerate(cuts) if all(fit(cut) for cut in some)]
    out = [None if i in chosen else low_of(parts) for i, parts in enumerate(sends)]
    if not chosen:
        return out
    shape = lambda cut: tuple(cut[1][axis] for axis in cut[2])
    arrays = [v for i in chosen for v, _ in sends[i]]
    buffers = [pltpu.VMEM(shape(cut), bf16) for i in chosen for cut in cuts[i]]
    results = pl.pallas_call(
        functools.partial(low_many_kernel, [cuts[i] for i in chosen]),
        in_specs=[pl.BlockSpec(memory_space=pl.ANY)] * len(arrays),
        out_specs=[pl.BlockSpec(memory_space=pltpu.VMEM)] * len(chosen),
        out_shape=[jax.ShapeDtypeStruct(shape(cuts[i][0]), bf16) for i in chosen],
        scratch_shapes=buffers + [pltpu.SemaphoreType.DMA((len(arrays),))],
        compiler_params=pltpu.CompilerParams(vmem_limit_bytes=VMEM_LIMIT),
        name="sums",
    )(*arrays)
    for i, v in zip(chosen, results):
        out[i] = v
    return out


def cut_of(part):
    v, path = part
    starts, sizes, axes = [0] * v.ndim, list(v.shape), list(range(v.ndim))
    for axis, i in path:
        if axis is None:
            sizes[-1] //= 2
            starts[-1] += i * sizes[-1]
        elif axis == "columns":
            starts[-1] += i[0]
            sizes[-1] = i[1]
        else:
            at = axes.pop(axis)
            starts[at], sizes[at] = i, 1
    return starts, sizes, axes


def taken(part):
    v = part[0]
    starts, sizes, axes = cut_of(part)
    if all(isinstance(i, int) for i in starts):
        v = lax.slice(v, starts, [i + n for i, n in zip(starts, sizes)])
    else:
        v = lax.dynamic_slice(v, [jnp.int32(i) for i in starts], sizes)
    return v.reshape([sizes[at] for at in axes])


def sum_of(parts, view=lambda v: v):
    return sum(view(taken(p)).astype(f32) for p in parts)


def low_of(parts, view=lambda v: v):
    return sum_of(parts, view).astype(bf16)


def per_device(tokens, segment_ids, attn_weight, vectors, ffn_weight, ffn_bias, out_grad):
    wide, narrow = lax.axis_size("wide"), lax.axis_size("narrow")
    w, z = lax.axis_index("wide"), lax.axis_index("narrow")
    chip, core = lax.div(w, 2), lax.rem(w, 2)
    bits = chip_bits()
    up = list(range(bits))
    down = up[::-1]
    pos = jnp.stack([chip, core, z]).astype(jnp.int32)
    count, features = tokens.shape
    half = features // 2

    rows_each = attn_weight.shape[0]
    each, each_bias = vectors.shape[0], ffn_bias.shape[0]
    small = jnp.concatenate([vectors, ffn_bias, jnp.zeros((features - each - each_bias,), bf16)])
    small = jnp.concatenate([small[None], jnp.zeros((7, features), bf16)])
    v = jnp.concatenate([attn_weight, small])
    attn = v[None]
    units = ffn_weight.shape[2]
    width = units // SUBS
    tail = units - width
    every = range(bits)
    steps = list(range(narrow_bits()))[::-1]
    orders = (up, down)

    def along(v, step, axis):
        return jnp.concatenate([v, swap_narrow(v, 1 << step)], axis)

    late = [(ffn_weight[i, :, tail:], []) for i in range(2)]
    for i, step in enumerate(steps):
        attn = along(attn, step, 0)
        if i == 0:
            (attn, *v) = tie(attn, *[v for v, _ in late])
            late = [(v, done) for v, (_, done) in zip(v, late)]
    for i in every:
        late = [hop(v, done, order[i]) for (v, done), order in zip(late, orders)]
    late = [v.reshape(half, width) for v, _ in late]
    rows = features // wide
    late[1] = late[1].reshape(-1, 2, rows, width).swapaxes(0, 1).reshape(half, width)
    late = jnp.stack(late)
    early, attn, late = tie(ffn_weight[:, :, :tail], attn, late)
    attn = [(attn[:, :, :half], []), (attn[:, :rows_each, half:], [])]
    for i in range(max(bits, len(steps))):
        if i < bits:
            attn = [hop(v, done, order[i]) for (v, done), order in zip(attn, orders)]
        if i < len(steps):
            early = along(early, steps[i], 2)
        early, a, b = tie(early, *[v for v, _ in attn])
        attn = [(a, attn[0][1]), (b, attn[1][1])]
    attn_a, attn_b = [v.reshape((wide // 2,) + v.shape[bits:]) for v, _ in attn]
    early = [(early[which], []) for which in range(2)]
    late, attn_a, attn_b, *firsts = tie(late, attn_a, attn_b, *[v for v, _ in early])
    halves = [attn_a, swap_wide(attn_a, 1), attn_b, swap_wide(attn_b, 1)]
    for i in every[:-1]:
        early = [hop(v, done, order[i]) for v, (_, done), order in zip(firsts, early, orders)]
        if i < len(steps) - 1:
            late = along(late, steps[i], 2)
        if i == 0:
            tokens_now, *firsts = tie(tokens, *[v for v, _ in early])
        else:
            firsts = [v for v, _ in early]
    for step in steps[bits - 1 : -1]:
        late = along(late, step, 2)
    late_came = swap_narrow(late, 1 << steps[-1])

    small = jnp.concatenate([h[:, :, rows_each, : each + each_bias] for h in halves[:2]])
    small = small.reshape(-1, each + each_bias)
    slots = jnp.arange(wide * narrow)
    slot_core, slot_chip, slot_z = (
        slots // (wide * narrow // 2), (slots // narrow) % (wide // 2), slots % narrow,
    )
    slot_w = (slot_chip ^ chip) * 2 + (slot_core ^ core)
    whole_at = slot_w * narrow + (turned(slot_z, narrow_bits()) ^ z)
    bias_at = slot_z * wide + slot_w
    spots = jnp.arange(wide * narrow)[:, None]
    vec_rows = dot((spots == whole_at[None, :]).astype(bf16), small[:, :each]).reshape(8, features)
    bias_rel = dot((spots == bias_at[None, :]).astype(bf16), small[:, each:])
    bias_rel = bias_rel.reshape(narrow, units)
    bias_rel = jnp.concatenate(
        [bias_rel[:, tail:].reshape(1, -1), bias_rel[:, :tail].reshape(1, -1)], 1
    )
    bq, bv, bo, s1, bf, s2, g1, g2 = [vec_rows[i] for i in range(8)]
    slot_vec = to_slots_quick(jnp.stack([g1, s1, bf, g2, s2, s2, s2, s2]), pos, chip, core)
    dy = to_slots_quick(out_grad, pos, chip, core)
    in_kernel = (features // wide) % 128 == 0

    def core_rows(v, which):
        t = v.reshape(count, -1, 2, narrow * rows_each)
        return pick(t, 2, which).reshape(count, half).T

    x_rows = [core_rows(tokens, core), core_rows(tokens, 1 - core)]

    biases = jnp.stack([bq, bv, bo, bo, bo, bo, bo, bo])
    tokens_now, dy, slot_vec, bias_rel, *x_rows = tie(tokens_now, dy, slot_vec, bias_rel, *x_rows)
    *kept, mixed, hidden = run_attend_forward(pos, tokens_now, segment_ids, biases, *halves)
    o_rows = [core_rows(mixed, core), core_rows(mixed, 1 - core)]
    last_hop = [swap_wide(v, 2 << order[-1]) for v, order in zip(firsts, orders)]
    late = [late, late_came]
    firsts = [v.reshape(half // 2, -1) for v in firsts]
    first_crossed = [swap_wide(v, 1) for v in firsts]
    hidden, *late = tie(hidden, *late)
    late_crossed = [swap_wide(v, 1) for v in late]
    hidden, *rest = tie(hidden, *first_crossed, *o_rows)
    first_crossed, o_rows = rest[:2], rest[2:]
    if not in_kernel:
        hidden = to_slots(hidden, chip, core)
    last_hop = [v.reshape(half // 2, -1) for v in last_hop]
    hidden, late_0, late_1, *last_hop = tie(hidden, *late_crossed, *last_hop)
    early = [
        (own, v, crossed, swap_wide(v, 1))
        for own, v, crossed in zip(firsts, last_hop, first_crossed)
    ]
    late = [late[0], late_0, late[1], late_1]
    slope, act, u_turned, result, dh, dh_low, dh_own, sums_two, other = run_ffn_forward(
        pos, hidden, slot_vec, dy, bias_rel, late, early
    )
    if not in_kernel:
        result = from_slots(result, chip, core)

    late_width, half_early = narrow * width, narrow * tail // 2
    axes = {("wide", bit): bits - 1 - bit for bit in range(bits)}
    chips = lambda order: [("wide", bit) for bit in order]
    along = [("narrow", bit) for bit in range(narrow_bits())]

    def ffn_unit(own, other):
        own = own.reshape((2,) * bits + own.shape[1:])
        unit = Scatter(own, other, axes, dict.fromkeys(axes, 0))
        unit.cross()
        return unit

    downs = ffn_unit(run_down(dh_own, act), other)
    down_0, down_a, down_b = (
        downs.columns(0, late_width), downs.columns(late_width, half_early),
        downs.columns(late_width + half_early, half_early),
    )
    low = start(
        dh_low, (down_0, along[0]), (down_a, ("wide", down[0])), (down_b, ("wide", up[0])),
        fused=False,
    )
    own, other, *rest = run_ffn_backward(pos, low, u_turned, slope, late, early, None)
    own, other, *rest = join([own, other, *rest], down_0, down_a, down_b)
    dbs = [rest[0]]
    up_a = ffn_unit(own, other)
    sends = [(down_a, hop_to) for hop_to in chips(down[1:2])]
    sends += [(down_b, hop_to) for hop_to in chips(up[1:2])]
    low = start(low, (down_0, along[1]), *sends)
    own, other, *rest = run_ffn_backward(
        pos, low, u_turned, slope, late, early, (rest[1], dh, hidden, slot_vec)
    )
    own, other, *rest = join([own, other, *rest], up_a, down_0, down_a, down_b)
    dbs.append(rest[0])
    grad_sum, grad_low, sums_one = rest[1:]
    up_b = ffn_unit(own, other)
    up_late, up_upper = up_a.columns(0, late_width), up_a.columns(late_width, half_early)
    for unit, order in ((down_a, down), (down_b, up)):
        for hop_to in chips(order[2:]):
            unit.send(hop_to)
            unit.receive()
    if not in_kernel:
        grad_sum = from_slots(grad_sum, chip, core)
        grad_low = from_slots(grad_low, chip, core)

    low_bits = bits - 2
    names = chips([bits - 1, bits - 2] + list(range(low_bits))[::-1]) + along[::-1]
    attn_axes = {name: axis for axis, name in enumerate(names)}
    mine = {("wide", bit): bit_of(chip, bit) for bit in range(bits)}
    mine.update({("narrow", bit): bit_of(z, bit) for bit in range(narrow_bits())})
    added = grad_sum
    attn_units = []
    slot_sums = from_slots(jnp.concatenate([sums_one[:3], sums_two[:3]]), chip, core)
    gs1, gg1, gbo, gs2, gg2, gbf = [slot_sums[i] for i in range(6)]
    db = jnp.concatenate([dbs[1], dbs[0][:, late_width:]], 1).reshape(narrow, tail)
    db = jnp.concatenate([db, dbs[0][:, :late_width].reshape(narrow, width)], 1)
    db = db.reshape(narrow, wide, each_bias)
    db = jnp.stack([pick(db, 0, turned(i ^ z, narrow_bits())) for i in range(narrow)], 1)

    def small_rows(vec):
        lanes = lambda v: jnp.pad(v[:, :, None], ((0, 0),) * 3 + ((0, half - v.shape[2]),))
        rows = jnp.concatenate([lanes(vec.reshape(wide, narrow, each)), lanes(db)], 2)
        rows = jnp.pad(rows, ((0, 0), (0, 0), (0, 6), (0, 0)))
        rows = rows.astype(bf16).reshape((2,) * (bits + 1 + narrow_bits()) + rows.shape[2:])
        return pick(rows, bits, core), pick(rows, bits, 1 - core)

    sums = jnp.stack([jnp.zeros_like(gs1)] * 2 + [gbo, gs1, gbf, gs2, gg1, gg2])
    for part in range(2):
        if part == 0:
            sends = [(up_late, ("wide", up[0])), (up_upper, ("wide", down[0]))]
            sends += [(Given(down_b, down_a), along[0])]
            low = start(grad_low, *sends)
        else:
            sends = [(up_late, hop_to) for hop_to in chips(up[1:2])]
            sends += [(up_upper, hop_to) for hop_to in chips(down[1:2])]
            sends += [(up_b, ("wide", up[0])), (down_a, along[1])]
            sends += [(attn_units[0], ("wide", down[0]))]
            low = start(low, *sends)
        own, other, added, sums = run_attend_backward(
            part, pos, low, added, sums, kept, x_rows + o_rows, halves
        )
        if part == 0:
            ready = (up_late, up_upper, down_a, up_b)
        else:
            ready = (up_late, up_upper, down_a, up_b, down_0)
        if part == 0:
            own, other, added, sums = join([own, other, added, sums], *ready)
        else:
            own, added, sums = join([own, added, sums], *ready)
        shape = (2,) * len(names) + (rows_each, half)
        unit = Scatter(
            own.reshape(shape), other, attn_axes, mine, None if part == 0 else small_rows(sums)
        )
        unit.cross()
        attn_units.append(unit)
    grad_tokens = added

    def move(unit, *hops):
        for hop_to in hops:
            unit.send(hop_to)
            unit.receive()

    a, b = attn_units
    move(up_late, *chips(up[2:]))
    move(up_upper, *chips(down[2:]))
    move(down_a, *along[2:])
    move(down_0, *along[2:])
    move(b, ("wide", up[0]))
    move(up_b, *chips(up[1:]))
    move(a, *chips(down[1:]))
    move(b, *chips(up[1:]))
    move(Several(up_late, Given(up_upper, up_b)), along[0])
    move(down_0, *chips(down))
    for hop_to in along[1:]:
        move(Several(up_late, up_b), hop_to)
    move(a, *along)
    move(b, *along)
    grad_ffn = jnp.stack(
        [
            jnp.concatenate([sum_of(up_b.parts), sum_of(up_late.parts)], -1),
            jnp.concatenate([sum_of(down_a.parts), sum_of(down_0.parts)], -1),
        ]
    )
    grad_attn = jnp.concatenate([sum_of(u.parts) for u in attn_units], -1)
    tally = sum_of(b.extra)
    return (
        result, grad_tokens, grad_attn, tally[0, :each], grad_ffn, tally[1, :each_bias],
    )


def solution(mesh):
    return jax.shard_map(
        per_device,
        mesh=mesh,
        in_specs=(
            P(("wide", "narrow"), None),
            P(("wide", "narrow"), None),
            P(("wide", "narrow"), None),
            P(("wide", "narrow")),
            P(None, "wide", "narrow"),
            P(("narrow", "wide")),
            P(("wide", "narrow"), None),
        ),
        out_specs=(
            P(("wide", "narrow"), None),
            P(("wide", "narrow"), None),
            P(("wide", "narrow"), None),
            P(("wide", "narrow")),
            P(None, "wide", "narrow"),
            P(("narrow", "wide")),
        ),
        check_vma=False,
    )
```

```python
import functools

import jax
import jax.numpy as jnp
from jax import lax
from jax.experimental import pallas as pl
from jax.experimental.pallas import tpu as pltpu
from jax.sharding import PartitionSpec as P

HEADS = 16
HEAD = 64
SUBS = 4
VMEM_LIMIT = 56 * 1024 * 1024
FFN_LIMIT = 44 * 1024 * 1024
ATTEND_BACK_LIMIT = 56 * 1024 * 1024
BACK_LIMIT = 40 * 1024 * 1024

f32 = jnp.float32
bf16 = jnp.bfloat16

NT = (((1,), (1,)), ((), ()))
TN = (((0,), (0,)), ((), ()))


def dot(a, b):
    return jnp.dot(a, b, preferred_element_type=f32)


def dot_nt(a, b):
    return lax.dot_general(a, b, NT, preferred_element_type=f32)


def dot_tn(a, b):
    return lax.dot_general(a, b, TN, preferred_element_type=f32)


def swap_wide(v, mask):
    size = lax.axis_size("wide")
    return lax.ppermute(v, "wide", [(w, w ^ mask) for w in range(size)])


def swap_narrow(v, mask):
    size = lax.axis_size("narrow")
    return lax.ppermute(v, "narrow", [(z, z ^ mask) for z in range(size)])


def chip_bits():
    return (lax.axis_size("wide") // 2).bit_length() - 1


def narrow_bits():
    return lax.axis_size("narrow").bit_length() - 1


def turned(index, bits):
    out = 0
    for bit in range(bits):
        out = out + ((index >> bit) & 1) * (1 << (bits - 1 - bit))
    return out


def gather_narrow(v, axis):
    for bit in reversed(range(narrow_bits())):
        v = jnp.concatenate([v, swap_narrow(v, 1 << bit)], axis)
    return v


def hop(v, done, bit):
    axis = sum(1 for b in done if b > bit)
    return jnp.stack([v, swap_wide(v, 2 << bit)], axis), done + [bit]


def bit_of(index, bit):
    return lax.rem(lax.div(index, 1 << bit), 2)


def pick(v, axis, index):
    return lax.dynamic_index_in_dim(v, index, axis, keepdims=False)


def to_slots(v, chip, core):
    bits = chip_bits()
    lead = v.shape[:-1]
    block = v.shape[-1] // lax.axis_size("wide")
    t = v.reshape(lead + (2,) * (bits + 1) + (block,))
    n = len(lead)
    for bit in range(bits):
        axis = n + bits - 1 - bit
        t = jnp.where(bit_of(chip, bit) == 1, jnp.flip(t, axis), t)
    t = jnp.where(core == 1, jnp.flip(t, n + bits), t)
    t = jnp.moveaxis(t, n + bits, n)
    return t.reshape(v.shape)


def from_slots(v, chip, core):
    bits = chip_bits()
    lead = v.shape[:-1]
    block = v.shape[-1] // lax.axis_size("wide")
    n = len(lead)
    t = v.reshape(lead + (2,) * (bits + 1) + (block,))
    t = jnp.moveaxis(t, n, n + bits)
    for bit in range(bits):
        axis = n + bits - 1 - bit
        t = jnp.where(bit_of(chip, bit) == 1, jnp.flip(t, axis), t)
    t = jnp.where(core == 1, jnp.flip(t, n + bits), t)
    return t.reshape(v.shape)


def slot_lanes(pos, block, wide, lanes):
    at = ((block % 2) ^ pos[1]) * (wide // 2) + ((block // 2) ^ pos[0])
    return pl.ds(pl.multiple_of(at * lanes, lanes), lanes)


def whole_lanes(pos, slot, wide, lanes):
    core, chip = divmod(slot, wide // 2)
    at = (chip ^ pos[0]) * 2 + (core ^ pos[1])
    return pl.ds(pl.multiple_of(at * lanes, lanes), lanes)


def permute_kernel(wide, pos, v_ref, out_ref):
    lanes = v_ref.shape[1] // wide
    for b in range(wide):
        out_ref[:, slot_lanes(pos, b, wide, lanes)] = v_ref[:, b * lanes : (b + 1) * lanes]


def to_slots_quick(v, pos, chip, core):
    wide = lax.axis_size("wide")
    if (v.shape[1] // wide) % 128:
        return to_slots(v, chip, core)
    return pl.pallas_call(
        functools.partial(permute_kernel, wide),
        in_specs=[pl.BlockSpec(memory_space=pltpu.SMEM), pl.BlockSpec(memory_space=pltpu.VMEM)],
        out_specs=pl.BlockSpec(memory_space=pltpu.VMEM),
        out_shape=jax.ShapeDtypeStruct(v.shape, v.dtype),
        name="permute",
    )(pos, v)


def tie(*values):
    return lax.optimization_barrier(values)


def load_rows(pos, geometry, own, other, matrix, first, count, place, sem):
    narrow, per_matrix, rows = geometry[:3]

    def body(j, carry):
        block = matrix * per_matrix + first + j
        w = block // narrow
        z = block % narrow
        chip = (w // 2) ^ pos[0]
        core = (w % 2) ^ pos[1]
        step = turned(z ^ pos[2], narrow.bit_length() - 1)

        @pl.when(core == 0)
        def _():
            pltpu.make_async_copy(own.at[chip, step, pl.ds(0, rows)], place(j), sem).start()

        @pl.when(core == 1)
        def _():
            pltpu.make_async_copy(other.at[chip, step, pl.ds(0, rows)], place(j), sem).start()

        return carry

    lax.fori_loop(0, count, body, 0)


def attend_forward(
    geometry, pos, x_ref, seg_row, seg_col, vec_ref, bo_ref, own_a, oth_a, own_b, oth_b,
    q_ref, k_ref, v_ref, p_ref, o_ref, h_ref, w_in, w_out, mask, sems,
):
    g = pl.program_id(0)
    steps = pl.num_programs(0)
    _, blocks, rows, wide = geometry
    sources = ((own_a, oth_a), (own_b, oth_b))

    @pl.when(g == 0)
    def _():
        for half in range(2):
            for m in range(3):
                load_rows(
                    pos, geometry, *sources[half], m, 0, blocks,
                    lambda j, half=half, m=m: w_in.at[half, m, pl.ds(pl.multiple_of(j * rows, rows), rows)],
                    sems.at[half],
                )
        for half in range(2):
            load_rows(
                pos, geometry, *sources[half], 3, 0, blocks,
                lambda j, half=half: w_out.at[half, pl.ds(pl.multiple_of(j * rows, rows), rows)],
                sems.at[2],
            )
        mask[...] = jnp.where(seg_col[...] == seg_row[...], 0.0, -1e30).astype(f32)
        pltpu.make_async_copy(w_in.at[0], w_in.at[0], sems.at[0]).wait()

    @pl.when(g == steps // 2)
    def _():
        pltpu.make_async_copy(w_in.at[1], w_in.at[1], sems.at[1]).wait()

    half = g // (steps // 2)
    columns = pl.ds(pl.multiple_of(lax.rem(g, steps // 2) * 256, 256), 256)
    x = x_ref[...]
    query = (dot(x, w_in[half, 0, :, columns]) + vec_ref[0:1, :]).astype(bf16)
    query = query * jnp.asarray(HEAD**-0.5, bf16)
    key = dot(x, w_in[half, 1, :, columns]).astype(bf16)
    value = (dot(x, w_in[half, 2, :, columns]) + vec_ref[1:2, :]).astype(bf16)
    q_ref[...] = query
    k_ref[...] = key
    v_ref[...] = value
    lane = lax.broadcasted_iota(jnp.int32, (1, 128), 1)
    for pair in range(2):
        part = slice(pair * 128, pair * 128 + 128)
        q2, k2, v2 = query[:, part], key[:, part], value[:, part]
        v2t = v2.T
        outs = []
        for sub in range(2):
            mine = (lane < HEAD) if sub == 0 else (lane >= HEAD)
            scores = dot_nt(k2, jnp.where(mine, q2, jnp.zeros_like(q2))) + mask[...]
            raised = jnp.exp(scores - jnp.max(scores, 0, keepdims=True))
            probs = (raised * (1.0 / jnp.sum(raised, 0, keepdims=True))).astype(bf16)
            p_ref[pair * 2 + sub] = probs
            outs.append(dot(v2t[sub * HEAD : sub * HEAD + HEAD], probs))
        mixed = jnp.concatenate(outs, 0).T.astype(bf16)
        o_ref[:, pl.ds(pl.multiple_of(g * 256 + pair * 128, 128), 128)] = mixed

    @pl.when(g == steps - 1)
    def _():
        pltpu.make_async_copy(w_out, w_out, sems.at[2]).wait()
        width = w_out.shape[2]
        lanes = 2 * width // wide
        for half in range(2):
            cols = slice(half * width, half * width + width)
            hidden = x_ref[:, cols].astype(f32) + dot(o_ref[...], w_out[half]) + bo_ref[0:1, cols]
            if lanes % 128:
                h_ref[:, cols] = hidden
            else:
                for b in range(wide // 2):
                    at = slot_lanes(pos, half * (wide // 2) + b, wide, lanes)
                    h_ref[:, at] = hidden[:, b * lanes : (b + 1) * lanes]


def run_attend_forward(pos, tokens, segment_ids, biases, own_a, oth_a, own_b, oth_b):
    count, features = tokens.shape
    rows = own_b.shape[2]
    geometry = (own_b.shape[1], features // rows, rows, own_b.shape[0] * 2)
    groups = features // 256
    whole = lambda *shape: pl.BlockSpec(shape, lambda g, pos: (0,) * len(shape))
    column = pl.BlockSpec((count, 256), lambda g, pos: (0, g))
    anywhere = pl.BlockSpec(memory_space=pl.ANY)
    width = features // 2
    return pl.pallas_call(
        functools.partial(attend_forward, geometry),
        grid_spec=pltpu.PrefetchScalarGridSpec(
            num_scalar_prefetch=1,
            grid=(groups,),
            in_specs=[
                whole(count, features), whole(1, count), whole(count, 1),
                pl.BlockSpec((8, 256), lambda g, pos: (0, g)), whole(8, features),
                anywhere, anywhere, anywhere, anywhere,
            ],
            out_specs=[
                column, column, column,
                pl.BlockSpec((4, count, count), lambda g, pos: (g, 0, 0)),
                whole(count, features), whole(count, features),
            ],
            scratch_shapes=[
                pltpu.VMEM((2, 3, features, width), bf16),
                pltpu.VMEM((2, features, width), bf16),
                pltpu.VMEM((count, count), f32),
                pltpu.SemaphoreType.DMA((3,)),
            ],
        ),
        out_shape=[
            jax.ShapeDtypeStruct((count, features), bf16),
            jax.ShapeDtypeStruct((count, features), bf16),
            jax.ShapeDtypeStruct((count, features), bf16),
            jax.ShapeDtypeStruct((HEADS, count, count), bf16),
            jax.ShapeDtypeStruct((count, features), bf16),
            jax.ShapeDtypeStruct((count, features), f32),
        ],
        compiler_params=pltpu.CompilerParams(
            vmem_limit_bytes=VMEM_LIMIT, dimension_semantics=("arbitrary",)
        ),
        cost_estimate=pl.CostEstimate(
            flops=2 * count * features * features * 8, bytes_accessed=24 << 20, transcendentals=0
        ),
        name="attend_forward",
    )(
        pos, tokens, segment_ids.reshape(1, count), segment_ids.reshape(count, 1),
        biases, biases[2:3] + jnp.zeros((8, 1), f32), own_a, oth_a, own_b, oth_b,
    )


def attend_backward(
    geometry, half, pos, dh_ref, add_ref, sums_in, q_ref, k_ref, v_ref, p_ref, x_own, x_oth, o_own, o_oth,
    own_a, oth_a, own_b, oth_b, gown_ref, goth_ref, dx_ref, bias_ref, w_in, w_out, rows_in, sems,
):
    g = pl.program_id(0)
    features = dh_ref.shape[1]
    _, blocks, rows, _ = geometry
    sources = ((own_a, oth_a), (own_b, oth_b))

    @pl.when(g == 0)
    def _():
        for part in range(2):
            load_rows(
                pos, geometry, *sources[part], 3, half * (blocks // 2), blocks // 2,
                lambda j, part=part: w_out.at[part, pl.ds(pl.multiple_of(j * rows, rows), rows)],
                sems.at[0],
            )
        for m in range(3):
            load_rows(
                pos, geometry, *sources[half], m, 0, blocks,
                lambda j, m=m: w_in.at[m, pl.ds(pl.multiple_of(j * rows, rows), rows)],
                sems.at[1],
            )
        pltpu.make_async_copy(add_ref, dx_ref, sems.at[2]).start()
        for i, source in enumerate((x_own, x_oth, o_own, o_oth)):
            pltpu.make_async_copy(source, rows_in.at[i], sems.at[3]).start()
        pltpu.make_async_copy(w_out, w_out, sems.at[0]).wait()

    span = pl.ds(pl.multiple_of(g * 256, 256), 256)
    width = features // 2
    low = dh_ref[...]
    grad_mixed = (
        dot_nt(low[:, :width], w_out[0, span, :]) + dot_nt(low[:, width:], w_out[1, span, :])
    ).astype(bf16)
    lane = lax.broadcasted_iota(jnp.int32, (1, 128), 1)
    lows = [[], [], []]
    sums = [[], []]
    for pair in range(2):
        part = slice(pair * 128, pair * 128 + 128)
        q2, k2, v2 = q_ref[:, part], k_ref[:, part], v_ref[:, part]
        do2 = grad_mixed[:, part]
        k2t = k2.T
        zero = jnp.zeros_like(q2)
        dv = dk = None
        dqs = []
        for sub in range(2):
            mine = (lane < HEAD) if sub == 0 else (lane >= HEAD)
            probs = p_ref[pair * 2 + sub]
            do_mine = jnp.where(mine, do2, zero)
            grad_probs = dot_nt(v2, do_mine)
            wide_probs = probs.astype(f32)
            inner = jnp.sum(wide_probs * grad_probs, 0, keepdims=True)
            grad_scores = (wide_probs * (grad_probs - inner)).astype(bf16)
            dv_part = dot(probs, do_mine)
            dk_part = dot(grad_scores, jnp.where(mine, q2, zero))
            dv = dv_part if dv is None else dv + dv_part
            dk = dk_part if dk is None else dk + dk_part
            dqs.append(dot(k2t[sub * HEAD : sub * HEAD + HEAD], grad_scores))
        dq = jnp.concatenate(dqs, 0).T * HEAD**-0.5
        sums[0].append(jnp.sum(dq, 0, keepdims=True))
        sums[1].append(jnp.sum(dv, 0, keepdims=True))
        for store, value in zip(lows, (dq, dk, dv)):
            store.append(value.astype(bf16))
    joined = [jnp.concatenate(s, 1) for s in lows]

    @pl.when(g == 0)
    def _():
        pltpu.make_async_copy(rows_in, rows_in, sems.at[3]).wait()

    low = dh_ref[:, pl.ds(pl.multiple_of(half * width + g * 256, 256), 256)]
    for m, right in enumerate(joined + [low]):
        first = 0 if m < 3 else 2
        goth_ref[m] = dot(rows_in[first + 1], right).astype(bf16)
        gown_ref[m] = dot(rows_in[first], right).astype(bf16)

    @pl.when(g == 0)
    def _():
        bias_ref[...] = sums_in[...]

    for row in range(2):
        at = pl.ds(pl.multiple_of(half * width + g * 256, 256), 256)
        bias_ref[row : row + 1, at] = jnp.concatenate(sums[row], 1)

    @pl.when(g == 0)
    def _():
        pltpu.make_async_copy(w_in, w_in, sems.at[1]).wait()
        pltpu.make_async_copy(dx_ref, dx_ref, sems.at[2]).wait()

    dx_ref[...] += (
        dot_nt(joined[0], w_in[0, :, span])
        + dot_nt(joined[1], w_in[1, :, span])
        + dot_nt(joined[2], w_in[2, :, span])
    )


def run_attend_backward(half, pos, grad_sum, added, sums, kept, rows_of, weights):
    q, k, v, probs = kept
    own_a, oth_a, own_b, oth_b = weights
    count, features = q.shape
    rows = own_b.shape[2]
    geometry = (own_b.shape[1], features // rows, rows, own_b.shape[0] * 2)
    groups = features // 512
    whole = lambda *shape: pl.BlockSpec(shape, lambda g, pos: (0,) * len(shape))
    column = pl.BlockSpec((count, 256), lambda g, pos: (0, half * groups + g))
    anywhere = pl.BlockSpec(memory_space=pl.ANY)
    width = features // 2
    return pl.pallas_call(
        functools.partial(attend_backward, geometry, half),
        grid_spec=pltpu.PrefetchScalarGridSpec(
            num_scalar_prefetch=1,
            grid=(groups,),
            in_specs=[
                whole(count, features), anywhere, whole(8, features), column, column, column,
                pl.BlockSpec((4, count, count), lambda g, pos: (half * groups + g, 0, 0)),
                anywhere, anywhere, anywhere, anywhere,
                anywhere, anywhere, anywhere, anywhere,
            ],
            out_specs=[
                pl.BlockSpec((4, width, 256), lambda g, pos: (0, 0, g)),
                pl.BlockSpec((4, width, 256), lambda g, pos: (0, 0, g)),
                whole(count, features),
                whole(8, features),
            ],
            scratch_shapes=[
                pltpu.VMEM((3, features, width), bf16),
                pltpu.VMEM((2, width, width), bf16),
                pltpu.VMEM((4, width, count), bf16),
                pltpu.SemaphoreType.DMA((4,)),
            ],
        ),
        out_shape=[
            jax.ShapeDtypeStruct((4, width, width), bf16),
            jax.ShapeDtypeStruct((4, width, width), bf16),
            jax.ShapeDtypeStruct((count, features), f32),
            jax.ShapeDtypeStruct((8, features), f32),
        ],
        compiler_params=pltpu.CompilerParams(
            vmem_limit_bytes=ATTEND_BACK_LIMIT, dimension_semantics=("arbitrary",)
        ),
        cost_estimate=pl.CostEstimate(
            flops=2 * count * features * features * 6, bytes_accessed=16 << 20, transcendentals=0
        ),
        name="attend_backward",
    )(pos, grad_sum, added, sums, q, k, v, probs, *rows_of, own_a, oth_a, own_b, oth_b)


def moments(hidden):
    center = hidden - jnp.mean(hidden, -1, keepdims=True)
    return center, lax.rsqrt(jnp.mean(center * center, -1, keepdims=True) + 1e-12)


def norm_back(grad, normed, factor):
    return factor * (
        grad
        - jnp.mean(grad, -1, keepdims=True)
        - normed * jnp.mean(grad * normed, -1, keepdims=True)
    )


def gelu_pair(a):
    z = jnp.abs(a) * (0.5**0.5)
    t = 1.0 / (1.0 + 0.3275911 * z)
    poly = t * (
        0.127414796 + t * (-0.142248368 + t * (0.7107068705 + t * (-0.7265760135 + t * 0.5307027145)))
    )
    bell = jnp.exp(-0.5 * (a * a))
    tail = poly * bell
    phi = jnp.where(a >= 0, 1.0 - tail, tail)
    return a * phi, phi + a * (bell * 0.3989422804014327)


ROWS_AT_ONCE = 128
TILE = 1024


def row_blocks(count, step=ROWS_AT_ONCE):
    return [slice(r, r + step) for r in range(0, count, step)]


def turn_into_whole(ref, rows, value, pos, wide):
    features = value.shape[1]
    lanes = features // wide
    if lanes % 128:
        ref[rows, :] = value
    else:
        for slot in range(wide):
            ref[rows, whole_lanes(pos, slot, wide, lanes)] = value[
                :, slot * lanes : (slot + 1) * lanes
            ]


def store_blocks(ref, turned_rows, right):
    chips, block = ref.shape[0], ref.shape[1]
    step = max(1, 256 // block)
    for k in range(0, chips, step):
        value = dot(turned_rows[k * block : (k + step) * block, :], right).astype(bf16)
        for i in range(step):
            ref[k + i] = value[i * block : (i + 1) * block]


def once(*shape):
    return pl.BlockSpec(
        shape, lambda t: (0,) * len(shape), pipeline_mode=pl.Buffered(buffer_count=1)
    )


def odd_last_places(wide):
    half = wide // 2
    return [slot // half * half + slot % 2 * (half // 2) + slot % half // 2 for slot in range(wide)]


def ffn_forward(
    wide, tiles, pos, h_ref, vec, dy, b1, l0a, l0b, l1a, l1b, *refs
):
    ups, downs, refs = refs[:4], refs[4:8], refs[8:]
    (
    slope_ref, act_ref, u_out, result, dh, dh_low, dh_own, sums, oth_ref,
    total, u_low, act_all, dh_turned,
    ) = refs
    t = pl.program_id(0)
    count, features = h_ref.shape
    width = features // 2
    quarter = width // 2
    block = features // wide
    odd_last = [block * p for p in odd_last_places(wide)]

    @pl.when(t == 0)
    def _():
        for r in row_blocks(count):
            center, factor = moments(h_ref[r, :])
            low = (center * factor * (1.0 + vec[0:1, :]) + vec[1:2, :]).astype(bf16)
            u_low[r, :] = low
            u_out[:, r] = low.T

    def tile(ups, downs, first, at, size):
        columns = pl.ds(pl.multiple_of(t * TILE + at, 256), size)
        step = features // len(ups)
        for r in row_blocks(count, 512):
            a = b1[0:1, columns]
            for i, w in enumerate(ups):
                a = a + dot(u_low[r, i * step : i * step + step], w[...])
            act, slope = gelu_pair(a)
            act = act.astype(bf16)
            act_all[r, columns] = act
            act_ref[r, at : at + size] = act
            slope_ref[r, at : at + size] = slope.astype(bf16)
            for i, w in enumerate(downs):
                value = dot_nt(act, w[...])
                if first:
                    total[r, i * step : i * step + step] = value
                else:
                    total[r, i * step : i * step + step] += value

    @pl.when(t == 0)
    def _():
        size = TILE // 2
        tile((l0a.at[0], l0b.at[0]), (l0a.at[1], l0b.at[1]), True, 0, size)
        tile((l1a.at[0], l1b.at[0]), (l1a.at[1], l1b.at[1]), False, size, size)

    @pl.when((t > 0) & (t < tiles))
    def _():
        tile(ups, downs, False, 0, TILE)

    @pl.when(t == tiles - 1)
    def _():
        sums[...] = jnp.zeros_like(sums)
        for r in row_blocks(count):
            center, factor = moments(h_ref[r, :])
            u = center * factor * (1.0 + vec[0:1, :]) + vec[1:2, :]
            ffn = jnp.concatenate([total[r, at : at + block] for at in odd_last], 1)
            center, factor = moments(u + ffn + vec[2:3, :])
            normed = center * factor
            final = (normed * (1.0 + vec[3:4, :]) + vec[4:5, :]).astype(bf16)
            turn_into_whole(result, r, final, pos, wide)
            grad = dy[r, :].astype(f32)
            back = norm_back(grad * (1.0 + vec[3:4, :]), normed, factor)
            dh[r, :] = back
            low = back.astype(bf16)
            for slot, at in enumerate(odd_last):
                dh_low[r, at : at + block] = low[:, slot * block : (slot + 1) * block]
            dh_own[:, r] = low[:, :width].T
            dh_turned[:, r] = low[:, width:].T
            sums[0:1, :] += jnp.sum(grad, 0, keepdims=True)
            sums[1:2, :] += jnp.sum(grad * normed, 0, keepdims=True)
            sums[2:3, :] += jnp.sum(back, 0, keepdims=True)

    @pl.when(t >= tiles)
    def _():
        columns = pl.ds(pl.multiple_of((t - tiles) * TILE, TILE), TILE)
        store_blocks(oth_ref, dh_turned[...], act_all[:, columns])


def down_kernel(left, right, out_ref):
    store_blocks(out_ref, left[...], right[...])


def run_down(dh_own, act):
    width, count = dh_own.shape
    units = act.shape[1]
    wide = lax.axis_size("wide")
    block = 2 * width // wide
    return pl.pallas_call(
        down_kernel,
        grid=(units // TILE,),
        in_specs=[once(width, count), pl.BlockSpec((count, TILE), lambda t: (0, t))],
        out_specs=pl.BlockSpec((wide // 2, block, TILE), lambda t: (0, 0, t)),
        out_shape=jax.ShapeDtypeStruct((wide // 2, block, units), bf16),
        compiler_params=pltpu.CompilerParams(
            vmem_limit_bytes=24 << 20, dimension_semantics=("arbitrary",)
        ),
        cost_estimate=pl.CostEstimate(
            flops=2 * count * width * units, bytes_accessed=9 << 20, transcendentals=0
        ),
        name="down_own",
    )(dh_own, act)


def run_ffn_forward(pos, hidden, vec, dy, b1, late, early):
    count, features = hidden.shape
    wide = lax.axis_size("wide")
    width = features // 2
    units = b1.shape[1]
    tiles = units // TILE
    block = features // wide
    tall = pl.BlockSpec((width // 2, TILE), lambda t: (0, jnp.clip(t - 1, 0, tiles - 2)))
    grads = pl.BlockSpec((wide // 2, block, TILE), lambda t: (0, 0, jnp.maximum(t - tiles, 0)))
    grad_shape = jax.ShapeDtypeStruct((wide // 2, block, units), bf16)
    return pl.pallas_call(
        functools.partial(ffn_forward, wide, tiles),
        grid=(2 * tiles,),
        in_specs=[
            pl.BlockSpec(memory_space=pltpu.SMEM), once(count, features), once(8, features),
            once(count, features), once(1, units),
        ] + [once(2, width, TILE // 2)] * 4 + [tall] * 8,
        out_specs=[
            pl.BlockSpec((count, TILE), lambda t: (0, jnp.minimum(t, tiles - 1))),
            pl.BlockSpec((count, TILE), lambda t: (0, jnp.minimum(t, tiles - 1))),
            once(features, count), once(count, features), once(count, features),
            once(count, features), once(width, count), once(8, features), grads,
        ],
        out_shape=[
            jax.ShapeDtypeStruct((count, units), bf16),
            jax.ShapeDtypeStruct((count, units), bf16),
            jax.ShapeDtypeStruct((features, count), bf16),
            jax.ShapeDtypeStruct((count, features), bf16),
            jax.ShapeDtypeStruct((count, features), f32),
            jax.ShapeDtypeStruct((count, features), bf16),
            jax.ShapeDtypeStruct((width, count), bf16),
            jax.ShapeDtypeStruct((8, features), f32),
            grad_shape,
        ],
        scratch_shapes=[
            pltpu.VMEM((count, features), f32),
            pltpu.VMEM((count, features), bf16),
            pltpu.VMEM((count, units), bf16),
            pltpu.VMEM((width, count), bf16),
        ],
        compiler_params=pltpu.CompilerParams(
            vmem_limit_bytes=FFN_LIMIT, dimension_semantics=("arbitrary",)
        ),
        cost_estimate=pl.CostEstimate(
            flops=6 * count * features * units, bytes_accessed=34 << 20, transcendentals=0
        ),
        name="ffn_forward",
    )(pos, hidden, vec, dy, b1, *late, *early[0], *early[1])


def ffn_backward(wide, last, *refs):
    pos, dh_low, u_turned, slope, *refs = refs
    late, refs = ([], refs) if last else (refs[:4], refs[4:])
    ups, downs, refs = refs[:4], refs[4:8], refs[8:]
    if last:
        du_in, dh, h_ref, vec, own_ref, oth_ref, db_ref, dh1, dh1_low, sums, total, low_all = refs
    else:
        own_ref, oth_ref, db_ref, total, low_all = refs
    t = pl.program_id(0)
    count, features = dh_low.shape
    width = features // 2

    def tile(ups, downs, before):
        db = 0.0
        step = features // len(ups)
        for r in row_blocks(count, 512):
            grad = 0.0
            for i, w in enumerate(downs):
                grad = grad + dot(dh_low[r, i * step : i * step + step], w[...])
            grad = grad * slope[r, :].astype(f32)
            db = db + jnp.sum(grad, 0, keepdims=True)
            low = grad.astype(bf16)
            low_all[r, :] = low
            for i, w in enumerate(ups):
                value = dot_nt(low, w[...])
                columns = slice(i * step, i * step + step)
                total[r, columns] = value if before is None else before[r, columns] + value
        db_ref[...] = db
        low = low_all[...]
        store_blocks(oth_ref, u_turned[width:, :], low)
        store_blocks(own_ref, u_turned[:width, :], low)

    if last:

        @pl.when(t == 0)
        def _():
            tile(ups, downs, du_in)

    else:
        for i in range(2):

            @pl.when(t == i)
            def _(i=i):
                a, b = late[2 * i : 2 * i + 2]
                tile((a.at[0], b.at[0]), (a.at[1], b.at[1]), total if i else None)

    @pl.when(t >= (1 if last else 2))
    def _():
        tile(ups, downs, total)

    if last:

        @pl.when(t == pl.num_programs(0) - 1)
        def _():
            sums[...] = jnp.zeros_like(sums)
            for r in row_blocks(count):
                center, factor = moments(h_ref[r, :])
                normed = center * factor
                du = total[r, :] + dh[r, :]
                back = norm_back(du * (1.0 + vec[0:1, :]), normed, factor)
                turn_into_whole(dh1, r, back, pos, wide)
                turn_into_whole(dh1_low, r, back.astype(bf16), pos, wide)
                sums[0:1, :] += jnp.sum(du, 0, keepdims=True)
                sums[1:2, :] += jnp.sum(du * normed, 0, keepdims=True)
                sums[2:3, :] += jnp.sum(back, 0, keepdims=True)


BACK_TILE = 512


def run_ffn_backward(pos, dh_low, u_turned, slope, late, early, tail):
    count, features = dh_low.shape
    wide = lax.axis_size("wide")
    width = features // 2
    block = features // wide
    last = tail is not None
    late_tiles = 2
    assert late[0].shape[2] == BACK_TILE
    half_tiles = early[0][0].shape[1] // BACK_TILE // 2
    tiles = half_tiles if last else late_tiles + half_tiles
    ins = [pos, dh_low, u_turned, slope]
    if last:
        at_slope = lambda t: (0, late_tiles + t)
        at_early = lambda t: (0, t)
    else:
        at_slope = lambda t: (0, jnp.where(t < late_tiles, t, t + half_tiles))
        at_early = lambda t: (0, half_tiles + jnp.maximum(t - late_tiles, 0))
    in_specs = [
        pl.BlockSpec(memory_space=pltpu.SMEM), once(count, features), once(features, count),
        pl.BlockSpec((count, BACK_TILE), at_slope),
    ]
    if not last:
        in_specs += [once(2, width, BACK_TILE)] * 4
        ins += list(late)
    in_specs += [pl.BlockSpec((width // 2, BACK_TILE), at_early)] * 8
    ins += [*early[0], *early[1]]
    grads = pl.BlockSpec((wide // 2, block, BACK_TILE), lambda t: (0, 0, t))
    grad_shape = jax.ShapeDtypeStruct((wide // 2, block, tiles * BACK_TILE), bf16)
    out_specs = [grads, grads, pl.BlockSpec((1, BACK_TILE), lambda t: (0, t))]
    out_shape = [grad_shape, grad_shape, jax.ShapeDtypeStruct((1, tiles * BACK_TILE), f32)]
    scratch = [pltpu.VMEM((count, BACK_TILE), bf16)]
    if last:
        ins += list(tail)
        in_specs += [once(count, features)] * 3 + [once(8, features)]
        out_specs += [once(count, features), once(count, features), once(8, features)]
        out_shape += [
            jax.ShapeDtypeStruct((count, features), f32),
            jax.ShapeDtypeStruct((count, features), bf16),
            jax.ShapeDtypeStruct((8, features), f32),
        ]
        scratch = [pltpu.VMEM((count, features), f32)] + scratch
    else:
        out_specs.append(once(count, features))
        out_shape.append(jax.ShapeDtypeStruct((count, features), f32))
    return pl.pallas_call(
        functools.partial(ffn_backward, wide, last),
        grid=(tiles,),
        in_specs=in_specs,
        out_specs=out_specs,
        out_shape=out_shape,
        scratch_shapes=scratch,
        compiler_params=pltpu.CompilerParams(
            vmem_limit_bytes=BACK_LIMIT, dimension_semantics=("arbitrary",)
        ),
        cost_estimate=pl.CostEstimate(
            flops=6 * count * features * tiles * BACK_TILE, bytes_accessed=17 << 20, transcendentals=0
        ),
        name="ffn_backward",
    )(*ins)


def swap_hop(v, hop):
    kind, bit = hop
    return swap_wide(v, 2 << bit) if kind == "wide" else swap_narrow(v, 1 << bit)


class Scatter:
    def __init__(self, own, other, axes, mine, extra=None):
        self.parts = [] if own is None else [(own, ())]
        self.other = other
        self.axes, self.mine = dict(axes), mine
        self.extra = [] if extra is None else [(extra[0], ())]
        self.extra_other = None if extra is None else extra[1]

    def cross(self):
        own = self.parts[0][0]
        self.parts.append((swap_wide(self.other, 1).reshape(own.shape), ()))
        if self.extra:
            self.extra.append((swap_wide(self.extra_other, 1), ()))

    def columns(self, first, count):
        unit = Scatter(None, None, self.axes, self.mine)
        unit.parts = [(v, path + (("columns", (first, count)),)) for v, path in self.parts]
        return unit

    def plan(self, hop):
        self.hop = hop
        axis = self.axes.pop(hop, None)
        keep = 0 if axis is None else self.mine[hop]
        more = lambda parts, i: [(v, path + ((axis, i),)) for v, path in parts]
        leaving, extra = more(self.parts, 1 - keep), more(self.extra, 1 - keep)
        self.parts, self.extra = more(self.parts, keep), more(self.extra, keep)
        if axis is not None:
            self.axes = {h: a - (a > axis) for h, a in self.axes.items()}
        return leaving, extra

    def send(self, hop):
        leaving, extra = self.plan(hop)
        self.leaving = low_of(leaving)
        if extra:
            self.leaving = jnp.concatenate([self.leaving, low_of(extra)], -2)

    def receive(self):
        came = swap_hop(self.leaving, self.hop)
        if self.extra:
            rows = self.parts[0][0].shape[-2]
            self.extra.append((came[..., rows:, :], ()))
            came = came[..., :rows, :]
        self.parts.append((came, ()))


def join(values, *units):
    values, came = lax.optimization_barrier((values, [unit.parts[-1][0] for unit in units]))
    for unit, v in zip(units, came):
        unit.parts[-1] = (v, unit.parts[-1][1])
    return values


def start(first, *sends, fused=True):
    plans = [unit.plan(hop_to) for unit, hop_to in sends]
    assert not any(extra for _, extra in plans)
    first, *leaving = tie(
        first, *(low_many if fused else lambda s: [low_of(p) for p in s])([p for p, _ in plans])
    )
    for (unit, _), v in zip(sends, leaving):
        unit.leaving = v
        unit.receive()
    return first


class Given:
    def __init__(self, giver, taker):
        self.giver, self.taker = giver, taker

    def plan(self, hop_to):
        self.hop = hop_to
        return self.giver.parts, []

    def send(self, hop_to):
        self.leaving = low_of(self.plan(hop_to)[0])

    def receive(self):
        self.taker.parts.append((swap_hop(self.leaving, self.hop), ()))


class Several:
    def __init__(self, *units):
        self.units = units

    def send(self, hop_to):
        self.hop = hop_to
        for unit in self.units:
            unit.send(hop_to)
        self.sizes = [unit.leaving.shape[-1] for unit in self.units]
        self.leaving = jnp.concatenate([unit.leaving for unit in self.units], -1)

    def receive(self):
        came = swap_hop(self.leaving, self.hop)
        first = 0
        for unit, size in zip(self.units, self.sizes):
            taker = unit.taker if isinstance(unit, Given) else unit
            taker.parts.append((came, (("columns", (first, size)),)))
            first += size


def low_many_kernel(slices, *refs):
    count = len(slices)
    flat = [cut for cuts in slices for cut in cuts]
    ins, outs = refs[: len(flat)], refs[len(flat) : len(flat) + count]
    buffers, sems = refs[len(flat) + count : -1], refs[-1]
    copies = []
    for i, (starts, sizes, axes) in enumerate(flat):
        at = tuple(
            pl.ds(first, size) if axis in axes else first
            for axis, (first, size) in enumerate(zip(starts, sizes))
        )
        copies.append(pltpu.make_async_copy(ins[i].at[at], buffers[i], sems.at[i]))
        copies[-1].start()
    i = 0
    for out, cuts in zip(outs, slices):
        total = None
        for _ in cuts:
            copies[i].wait()
            value = buffers[i][...].astype(f32)
            total = value if total is None else total + value
            i += 1
        out[...] = total.astype(bf16)


def low_many(sends):
    fit = lambda cut: (
        all(isinstance(i, int) for i in cut[0])
        and cut[0][-1] % 128 == 0
        and cut[1][-1] % 128 == 0
        and len(cut[2]) >= 2
    )
    cuts = [[cut_of(part) for part in parts] for parts in sends]
    chosen = [i for i, some in enumerate(cuts) if all(fit(cut) for cut in some)]
    out = [None if i in chosen else low_of(parts) for i, parts in enumerate(sends)]
    if not chosen:
        return out
    shape = lambda cut: tuple(cut[1][axis] for axis in cut[2])
    arrays = [v for i in chosen for v, _ in sends[i]]
    buffers = [pltpu.VMEM(shape(cut), bf16) for i in chosen for cut in cuts[i]]
    results = pl.pallas_call(
        functools.partial(low_many_kernel, [cuts[i] for i in chosen]),
        in_specs=[pl.BlockSpec(memory_space=pl.ANY)] * len(arrays),
        out_specs=[pl.BlockSpec(memory_space=pltpu.VMEM)] * len(chosen),
        out_shape=[jax.ShapeDtypeStruct(shape(cuts[i][0]), bf16) for i in chosen],
        scratch_shapes=buffers + [pltpu.SemaphoreType.DMA((len(arrays),))],
        compiler_params=pltpu.CompilerParams(vmem_limit_bytes=VMEM_LIMIT),
        name="sums",
    )(*arrays)
    for i, v in zip(chosen, results):
        out[i] = v
    return out


def cut_of(part):
    v, path = part
    starts, sizes, axes = [0] * v.ndim, list(v.shape), list(range(v.ndim))
    for axis, i in path:
        if axis is None:
            sizes[-1] //= 2
            starts[-1] += i * sizes[-1]
        elif axis == "columns":
            starts[-1] += i[0]
            sizes[-1] = i[1]
        else:
            at = axes.pop(axis)
            starts[at], sizes[at] = i, 1
    return starts, sizes, axes


def taken(part):
    v = part[0]
    starts, sizes, axes = cut_of(part)
    if all(isinstance(i, int) for i in starts):
        v = lax.slice(v, starts, [i + n for i, n in zip(starts, sizes)])
    else:
        v = lax.dynamic_slice(v, [jnp.int32(i) for i in starts], sizes)
    return v.reshape([sizes[at] for at in axes])


def sum_of(parts, view=lambda v: v):
    return sum(view(taken(p)).astype(f32) for p in parts)


def low_of(parts, view=lambda v: v):
    return sum_of(parts, view).astype(bf16)


def per_device(tokens, segment_ids, attn_weight, vectors, ffn_weight, ffn_bias, out_grad):
    wide, narrow = lax.axis_size("wide"), lax.axis_size("narrow")
    w, z = lax.axis_index("wide"), lax.axis_index("narrow")
    chip, core = lax.div(w, 2), lax.rem(w, 2)
    bits = chip_bits()
    up = list(range(bits))
    down = up[::-1]
    pos = jnp.stack([chip, core, z]).astype(jnp.int32)
    count, features = tokens.shape
    half = features // 2

    rows_each = attn_weight.shape[0]
    each, each_bias = vectors.shape[0], ffn_bias.shape[0]
    small = jnp.concatenate([vectors, ffn_bias, jnp.zeros((features - each - each_bias,), bf16)])
    small = jnp.concatenate([small[None], jnp.zeros((7, features), bf16)])
    v = jnp.concatenate([attn_weight, small])
    attn = v[None]
    units = ffn_weight.shape[2]
    width = units // SUBS
    tail = units - width
    every = range(bits)
    steps = list(range(narrow_bits()))[::-1]
    orders = (up, down)

    def along(v, step, axis):
        return jnp.concatenate([v, swap_narrow(v, 1 << step)], axis)

    late = [(ffn_weight[i, :, tail:], []) for i in range(2)]
    for i, step in enumerate(steps):
        attn = along(attn, step, 0)
        if i == 0:
            (attn, *v) = tie(attn, *[v for v, _ in late])
            late = [(v, done) for v, (_, done) in zip(v, late)]
    for i in every:
        late = [hop(v, done, order[i]) for (v, done), order in zip(late, orders)]
    late = [v.reshape(half, width) for v, _ in late]
    rows = features // wide
    late[1] = late[1].reshape(-1, 2, rows, width).swapaxes(0, 1).reshape(half, width)
    late = jnp.stack(late)
    early, attn, late = tie(ffn_weight[:, :, :tail], attn, late)
    attn = [(attn[:, :, :half], []), (attn[:, :rows_each, half:], [])]
    for i in range(max(bits, len(steps))):
        if i < bits:
            attn = [hop(v, done, order[i]) for (v, done), order in zip(attn, orders)]
        if i < len(steps):
            early = along(early, steps[i], 2)
        early, a, b = tie(early, *[v for v, _ in attn])
        attn = [(a, attn[0][1]), (b, attn[1][1])]
    attn_a, attn_b = [v.reshape((wide // 2,) + v.shape[bits:]) for v, _ in attn]
    early = [(early[which], []) for which in range(2)]
    late, attn_a, attn_b, *firsts = tie(late, attn_a, attn_b, *[v for v, _ in early])
    halves = [attn_a, swap_wide(attn_a, 1), attn_b, swap_wide(attn_b, 1)]
    for i in every[:-1]:
        early = [hop(v, done, order[i]) for v, (_, done), order in zip(firsts, early, orders)]
        if i < len(steps) - 1:
            late = along(late, steps[i], 2)
        if i == 0:
            tokens_now, *firsts = tie(tokens, *[v for v, _ in early])
        else:
            firsts = [v for v, _ in early]
    for step in steps[bits - 1 : -1]:
        late = along(late, step, 2)
    late_came = swap_narrow(late, 1 << steps[-1])

    small = jnp.concatenate([h[:, :, rows_each, : each + each_bias] for h in halves[:2]])
    small = small.reshape(-1, each + each_bias)
    slots = jnp.arange(wide * narrow)
    slot_core, slot_chip, slot_z = (
        slots // (wide * narrow // 2), (slots // narrow) % (wide // 2), slots % narrow,
    )
    slot_w = (slot_chip ^ chip) * 2 + (slot_core ^ core)
    whole_at = slot_w * narrow + (turned(slot_z, narrow_bits()) ^ z)
    bias_at = slot_z * wide + slot_w
    spots = jnp.arange(wide * narrow)[:, None]
    vec_rows = dot((spots == whole_at[None, :]).astype(bf16), small[:, :each]).reshape(8, features)
    bias_rel = dot((spots == bias_at[None, :]).astype(bf16), small[:, each:])
    bias_rel = bias_rel.reshape(narrow, units)
    bias_rel = jnp.concatenate(
        [bias_rel[:, tail:].reshape(1, -1), bias_rel[:, :tail].reshape(1, -1)], 1
    )
    bq, bv, bo, s1, bf, s2, g1, g2 = [vec_rows[i] for i in range(8)]
    slot_vec = to_slots_quick(jnp.stack([g1, s1, bf, g2, s2, s2, s2, s2]), pos, chip, core)
    dy = to_slots_quick(out_grad, pos, chip, core)
    in_kernel = (features // wide) % 128 == 0

    def core_rows(v, which):
        t = v.reshape(count, -1, 2, narrow * rows_each)
        return pick(t, 2, which).reshape(count, half).T

    x_rows = [core_rows(tokens, core), core_rows(tokens, 1 - core)]

    biases = jnp.stack([bq, bv, bo, bo, bo, bo, bo, bo])
    tokens_now, dy, slot_vec, bias_rel, *x_rows = tie(tokens_now, dy, slot_vec, bias_rel, *x_rows)
    *kept, mixed, hidden = run_attend_forward(pos, tokens_now, segment_ids, biases, *halves)
    o_rows = [core_rows(mixed, core), core_rows(mixed, 1 - core)]
    last_hop = [swap_wide(v, 2 << order[-1]) for v, order in zip(firsts, orders)]
    late = [late, late_came]
    firsts = [v.reshape(half // 2, -1) for v in firsts]
    first_crossed = [swap_wide(v, 1) for v in firsts]
    hidden, *late = tie(hidden, *late)
    late_crossed = [swap_wide(v, 1) for v in late]
    hidden, *rest = tie(hidden, *first_crossed, *o_rows)
    first_crossed, o_rows = rest[:2], rest[2:]
    if not in_kernel:
        hidden = to_slots(hidden, chip, core)
    last_hop = [v.reshape(half // 2, -1) for v in last_hop]
    hidden, late_0, late_1, *last_hop = tie(hidden, *late_crossed, *last_hop)
    early = [
        (own, v, crossed, swap_wide(v, 1))
        for own, v, crossed in zip(firsts, last_hop, first_crossed)
    ]
    late = [late[0], late_0, late[1], late_1]
    slope, act, u_turned, result, dh, dh_low, dh_own, sums_two, other = run_ffn_forward(
        pos, hidden, slot_vec, dy, bias_rel, late, early
    )
    if not in_kernel:
        result = from_slots(result, chip, core)

    late_width, half_early = narrow * width, narrow * tail // 2
    axes = {("wide", bit): bits - 1 - bit for bit in range(bits)}
    chips = lambda order: [("wide", bit) for bit in order]
    along = [("narrow", bit) for bit in range(narrow_bits())]

    def ffn_unit(own, other):
        own = own.reshape((2,) * bits + own.shape[1:])
        unit = Scatter(own, other, axes, dict.fromkeys(axes, 0))
        unit.cross()
        return unit

    downs = ffn_unit(run_down(dh_own, act), other)
    down_0, down_a, down_b = (
        downs.columns(0, late_width), downs.columns(late_width, half_early),
        downs.columns(late_width + half_early, half_early),
    )
    low = start(
        dh_low, (down_0, along[0]), (down_a, ("wide", down[0])), (down_b, ("wide", up[0])),
        fused=False,
    )
    own, other, *rest = run_ffn_backward(pos, low, u_turned, slope, late, early, None)
    own, other, *rest = join([own, other, *rest], down_0, down_a, down_b)
    dbs = [rest[0]]
    up_a = ffn_unit(own, other)
    sends = [(down_a, hop_to) for hop_to in chips(down[1:2])]
    sends += [(down_b, hop_to) for hop_to in chips(up[1:2])]
    low = start(low, (down_0, along[1]), *sends)
    own, other, *rest = run_ffn_backward(
        pos, low, u_turned, slope, late, early, (rest[1], dh, hidden, slot_vec)
    )
    own, other, *rest = join([own, other, *rest], up_a, down_0, down_a, down_b)
    dbs.append(rest[0])
    grad_sum, grad_low, sums_one = rest[1:]
    up_b = ffn_unit(own, other)
    up_late, up_upper = up_a.columns(0, late_width), up_a.columns(late_width, half_early)
    for unit, order in ((down_a, down), (down_b, up)):
        for hop_to in chips(order[2:]):
            unit.send(hop_to)
            unit.receive()
    if not in_kernel:
        grad_sum = from_slots(grad_sum, chip, core)
        grad_low = from_slots(grad_low, chip, core)

    low_bits = bits - 2
    names = chips([bits - 1, bits - 2] + list(range(low_bits))[::-1]) + along[::-1]
    attn_axes = {name: axis for axis, name in enumerate(names)}
    mine = {("wide", bit): bit_of(chip, bit) for bit in range(bits)}
    mine.update({("narrow", bit): bit_of(z, bit) for bit in range(narrow_bits())})
    added = grad_sum
    attn_units = []
    slot_sums = from_slots(jnp.concatenate([sums_one[:3], sums_two[:3]]), chip, core)
    gs1, gg1, gbo, gs2, gg2, gbf = [slot_sums[i] for i in range(6)]
    db = jnp.concatenate([dbs[1], dbs[0][:, late_width:]], 1).reshape(narrow, tail)
    db = jnp.concatenate([db, dbs[0][:, :late_width].reshape(narrow, width)], 1)
    db = db.reshape(narrow, wide, each_bias)
    db = jnp.stack([pick(db, 0, turned(i ^ z, narrow_bits())) for i in range(narrow)], 1)

    def small_rows(vec):
        lanes = lambda v: jnp.pad(v[:, :, None], ((0, 0),) * 3 + ((0, half - v.shape[2]),))
        rows = jnp.concatenate([lanes(vec.reshape(wide, narrow, each)), lanes(db)], 2)
        rows = jnp.pad(rows, ((0, 0), (0, 0), (0, 6), (0, 0)))
        rows = rows.astype(bf16).reshape((2,) * (bits + 1 + narrow_bits()) + rows.shape[2:])
        return pick(rows, bits, core), pick(rows, bits, 1 - core)

    sums = jnp.stack([jnp.zeros_like(gs1)] * 2 + [gbo, gs1, gbf, gs2, gg1, gg2])
    for part in range(2):
        if part == 0:
            sends = [(up_late, ("wide", up[0])), (up_upper, ("wide", down[0]))]
            sends += [(Given(down_b, down_a), along[0])]
            low = start(grad_low, *sends)
        else:
            sends = [(up_late, hop_to) for hop_to in chips(up[1:2])]
            sends += [(up_upper, hop_to) for hop_to in chips(down[1:2])]
            sends += [(up_b, ("wide", down[0])), (down_a, along[1])]
            sends += [(attn_units[0], ("wide", up[0]))]
            low = start(low, *sends)
        own, other, added, sums = run_attend_backward(
            part, pos, low, added, sums, kept, x_rows + o_rows, halves
        )
        if part == 0:
            ready = (up_late, up_upper, down_a, up_b)
        else:
            ready = (up_late, up_upper, down_a, up_b, down_0)
        if part == 0:
            own, other, added, sums = join([own, other, added, sums], *ready)
        else:
            own, added, sums = join([own, added, sums], *ready)
        shape = (2,) * len(names) + (rows_each, half)
        unit = Scatter(
            own.reshape(shape), other, attn_axes, mine, None if part == 0 else small_rows(sums)
        )
        unit.cross()
        attn_units.append(unit)
    grad_tokens = added

    def move(unit, *hops):
        for hop_to in hops:
            unit.send(hop_to)
            unit.receive()

    a, b = attn_units
    move(up_late, *chips(up[2:]))
    move(up_upper, *chips(down[2:]))
    move(down_a, *along[2:])
    move(down_0, *along[2:])
    move(b, ("wide", down[0]))
    move(up_b, *chips(down[1:]))
    move(a, *chips(up[1:]))
    move(b, *chips(down[1:]))
    move(Several(up_late, Given(up_upper, up_b)), along[0])
    move(down_0, *chips(down))
    for hop_to in along[1:]:
        move(Several(up_late, up_b), hop_to)
    move(a, *along)
    move(b, *along)
    grad_ffn = jnp.stack(
        [
            jnp.concatenate([sum_of(up_b.parts), sum_of(up_late.parts)], -1),
            jnp.concatenate([sum_of(down_a.parts), sum_of(down_0.parts)], -1),
        ]
    )
    grad_attn = jnp.concatenate([sum_of(u.parts) for u in attn_units], -1)
    tally = sum_of(b.extra)
    return (
        result, grad_tokens, grad_attn, tally[0, :each], grad_ffn, tally[1, :each_bias],
    )


def solution(mesh):
    return jax.shard_map(
        per_device,
        mesh=mesh,
        in_specs=(
            P(("wide", "narrow"), None),
            P(("wide", "narrow"), None),
            P(("wide", "narrow"), None),
            P(("wide", "narrow")),
            P(None, "wide", "narrow"),
            P(("narrow", "wide")),
            P(("wide", "narrow"), None),
        ),
        out_specs=(
            P(("wide", "narrow"), None),
            P(("wide", "narrow"), None),
            P(("wide", "narrow"), None),
            P(("wide", "narrow")),
            P(None, "wide", "narrow"),
            P(("narrow", "wide")),
        ),
        check_vma=False,
    )
```

```python
import functools

import jax
import jax.numpy as jnp
from jax import lax
from jax.experimental import pallas as pl
from jax.experimental.pallas import tpu as pltpu
from jax.sharding import PartitionSpec as P

HEADS = 16
HEAD = 64
SUBS = 4
VMEM_LIMIT = 56 * 1024 * 1024
FFN_LIMIT = 44 * 1024 * 1024
ATTEND_BACK_LIMIT = 56 * 1024 * 1024
BACK_LIMIT = 40 * 1024 * 1024

f32 = jnp.float32
bf16 = jnp.bfloat16

NT = (((1,), (1,)), ((), ()))
TN = (((0,), (0,)), ((), ()))


def dot(a, b):
    return jnp.dot(a, b, preferred_element_type=f32)


def dot_nt(a, b):
    return lax.dot_general(a, b, NT, preferred_element_type=f32)


def dot_tn(a, b):
    return lax.dot_general(a, b, TN, preferred_element_type=f32)


def swap_wide(v, mask):
    size = lax.axis_size("wide")
    return lax.ppermute(v, "wide", [(w, w ^ mask) for w in range(size)])


def swap_narrow(v, mask):
    size = lax.axis_size("narrow")
    return lax.ppermute(v, "narrow", [(z, z ^ mask) for z in range(size)])


def chip_bits():
    return (lax.axis_size("wide") // 2).bit_length() - 1


def narrow_bits():
    return lax.axis_size("narrow").bit_length() - 1


def turned(index, bits):
    out = 0
    for bit in range(bits):
        out = out + ((index >> bit) & 1) * (1 << (bits - 1 - bit))
    return out


def gather_narrow(v, axis):
    for bit in reversed(range(narrow_bits())):
        v = jnp.concatenate([v, swap_narrow(v, 1 << bit)], axis)
    return v


def hop(v, done, bit):
    axis = sum(1 for b in done if b > bit)
    return jnp.stack([v, swap_wide(v, 2 << bit)], axis), done + [bit]


def bit_of(index, bit):
    return lax.rem(lax.div(index, 1 << bit), 2)


def pick(v, axis, index):
    return lax.dynamic_index_in_dim(v, index, axis, keepdims=False)


def to_slots(v, chip, core):
    bits = chip_bits()
    lead = v.shape[:-1]
    block = v.shape[-1] // lax.axis_size("wide")
    t = v.reshape(lead + (2,) * (bits + 1) + (block,))
    n = len(lead)
    for bit in range(bits):
        axis = n + bits - 1 - bit
        t = jnp.where(bit_of(chip, bit) == 1, jnp.flip(t, axis), t)
    t = jnp.where(core == 1, jnp.flip(t, n + bits), t)
    t = jnp.moveaxis(t, n + bits, n)
    return t.reshape(v.shape)


def from_slots(v, chip, core):
    bits = chip_bits()
    lead = v.shape[:-1]
    block = v.shape[-1] // lax.axis_size("wide")
    n = len(lead)
    t = v.reshape(lead + (2,) * (bits + 1) + (block,))
    t = jnp.moveaxis(t, n, n + bits)
    for bit in range(bits):
        axis = n + bits - 1 - bit
        t = jnp.where(bit_of(chip, bit) == 1, jnp.flip(t, axis), t)
    t = jnp.where(core == 1, jnp.flip(t, n + bits), t)
    return t.reshape(v.shape)


def slot_lanes(pos, block, wide, lanes):
    at = ((block % 2) ^ pos[1]) * (wide // 2) + ((block // 2) ^ pos[0])
    return pl.ds(pl.multiple_of(at * lanes, lanes), lanes)


def whole_lanes(pos, slot, wide, lanes):
    core, chip = divmod(slot, wide // 2)
    at = (chip ^ pos[0]) * 2 + (core ^ pos[1])
    return pl.ds(pl.multiple_of(at * lanes, lanes), lanes)


def permute_kernel(wide, pos, v_ref, out_ref):
    lanes = v_ref.shape[1] // wide
    for b in range(wide):
        out_ref[:, slot_lanes(pos, b, wide, lanes)] = v_ref[:, b * lanes : (b + 1) * lanes]


def to_slots_quick(v, pos, chip, core):
    wide = lax.axis_size("wide")
    if (v.shape[1] // wide) % 128:
        return to_slots(v, chip, core)
    return pl.pallas_call(
        functools.partial(permute_kernel, wide),
        in_specs=[pl.BlockSpec(memory_space=pltpu.SMEM), pl.BlockSpec(memory_space=pltpu.VMEM)],
        out_specs=pl.BlockSpec(memory_space=pltpu.VMEM),
        out_shape=jax.ShapeDtypeStruct(v.shape, v.dtype),
        name="permute",
    )(pos, v)


def tie(*values):
    return lax.optimization_barrier(values)


def load_rows(pos, geometry, own, other, matrix, first, count, place, sem):
    narrow, per_matrix, rows = geometry[:3]

    def body(j, carry):
        block = matrix * per_matrix + first + j
        w = block // narrow
        z = block % narrow
        chip = (w // 2) ^ pos[0]
        core = (w % 2) ^ pos[1]
        step = turned(z ^ pos[2], narrow.bit_length() - 1)

        @pl.when(core == 0)
        def _():
            pltpu.make_async_copy(own.at[chip, step, pl.ds(0, rows)], place(j), sem).start()

        @pl.when(core == 1)
        def _():
            pltpu.make_async_copy(other.at[chip, step, pl.ds(0, rows)], place(j), sem).start()

        return carry

    lax.fori_loop(0, count, body, 0)


def attend_forward(
    geometry, pos, x_ref, seg_row, seg_col, vec_ref, bo_ref, own_a, oth_a, own_b, oth_b,
    q_ref, k_ref, v_ref, p_ref, o_ref, h_ref, w_in, w_out, mask, sems,
):
    g = pl.program_id(0)
    steps = pl.num_programs(0)
    _, blocks, rows, wide = geometry
    sources = ((own_a, oth_a), (own_b, oth_b))

    @pl.when(g == 0)
    def _():
        for half in range(2):
            for m in range(3):
                load_rows(
                    pos, geometry, *sources[half], m, 0, blocks,
                    lambda j, half=half, m=m: w_in.at[half, m, pl.ds(pl.multiple_of(j * rows, rows), rows)],
                    sems.at[half],
                )
        for half in range(2):
            load_rows(
                pos, geometry, *sources[half], 3, 0, blocks,
                lambda j, half=half: w_out.at[half, pl.ds(pl.multiple_of(j * rows, rows), rows)],
                sems.at[2],
            )
        mask[...] = jnp.where(seg_col[...] == seg_row[...], 0.0, -1e30).astype(f32)
        pltpu.make_async_copy(w_in.at[0], w_in.at[0], sems.at[0]).wait()

    @pl.when(g == steps // 2)
    def _():
        pltpu.make_async_copy(w_in.at[1], w_in.at[1], sems.at[1]).wait()

    half = g // (steps // 2)
    columns = pl.ds(pl.multiple_of(lax.rem(g, steps // 2) * 256, 256), 256)
    x = x_ref[...]
    query = (dot(x, w_in[half, 0, :, columns]) + vec_ref[0:1, :]).astype(bf16)
    query = query * jnp.asarray(HEAD**-0.5, bf16)
    key = dot(x, w_in[half, 1, :, columns]).astype(bf16)
    value = (dot(x, w_in[half, 2, :, columns]) + vec_ref[1:2, :]).astype(bf16)
    q_ref[...] = query
    k_ref[...] = key
    v_ref[...] = value
    lane = lax.broadcasted_iota(jnp.int32, (1, 128), 1)
    for pair in range(2):
        part = slice(pair * 128, pair * 128 + 128)
        q2, k2, v2 = query[:, part], key[:, part], value[:, part]
        v2t = v2.T
        outs = []
        for sub in range(2):
            mine = (lane < HEAD) if sub == 0 else (lane >= HEAD)
            scores = dot_nt(k2, jnp.where(mine, q2, jnp.zeros_like(q2))) + mask[...]
            raised = jnp.exp(scores - jnp.max(scores, 0, keepdims=True))
            probs = (raised * (1.0 / jnp.sum(raised, 0, keepdims=True))).astype(bf16)
            p_ref[pair * 2 + sub] = probs
            outs.append(dot(v2t[sub * HEAD : sub * HEAD + HEAD], probs))
        mixed = jnp.concatenate(outs, 0).T.astype(bf16)
        o_ref[:, pl.ds(pl.multiple_of(g * 256 + pair * 128, 128), 128)] = mixed

    @pl.when(g == steps - 1)
    def _():
        pltpu.make_async_copy(w_out, w_out, sems.at[2]).wait()
        width = w_out.shape[2]
        lanes = 2 * width // wide
        for half in range(2):
            cols = slice(half * width, half * width + width)
            hidden = x_ref[:, cols].astype(f32) + dot(o_ref[...], w_out[half]) + bo_ref[0:1, cols]
            if lanes % 128:
                h_ref[:, cols] = hidden
            else:
                for b in range(wide // 2):
                    at = slot_lanes(pos, half * (wide // 2) + b, wide, lanes)
                    h_ref[:, at] = hidden[:, b * lanes : (b + 1) * lanes]


def run_attend_forward(pos, tokens, segment_ids, biases, own_a, oth_a, own_b, oth_b):
    count, features = tokens.shape
    rows = own_b.shape[2]
    geometry = (own_b.shape[1], features // rows, rows, own_b.shape[0] * 2)
    groups = features // 256
    whole = lambda *shape: pl.BlockSpec(shape, lambda g, pos: (0,) * len(shape))
    column = pl.BlockSpec((count, 256), lambda g, pos: (0, g))
    anywhere = pl.BlockSpec(memory_space=pl.ANY)
    width = features // 2
    return pl.pallas_call(
        functools.partial(attend_forward, geometry),
        grid_spec=pltpu.PrefetchScalarGridSpec(
            num_scalar_prefetch=1,
            grid=(groups,),
            in_specs=[
                whole(count, features), whole(1, count), whole(count, 1),
                pl.BlockSpec((8, 256), lambda g, pos: (0, g)), whole(8, features),
                anywhere, anywhere, anywhere, anywhere,
            ],
            out_specs=[
                column, column, column,
                pl.BlockSpec((4, count, count), lambda g, pos: (g, 0, 0)),
                whole(count, features), whole(count, features),
            ],
            scratch_shapes=[
                pltpu.VMEM((2, 3, features, width), bf16),
                pltpu.VMEM((2, features, width), bf16),
                pltpu.VMEM((count, count), f32),
                pltpu.SemaphoreType.DMA((3,)),
            ],
        ),
        out_shape=[
            jax.ShapeDtypeStruct((count, features), bf16),
            jax.ShapeDtypeStruct((count, features), bf16),
            jax.ShapeDtypeStruct((count, features), bf16),
            jax.ShapeDtypeStruct((HEADS, count, count), bf16),
            jax.ShapeDtypeStruct((count, features), bf16),
            jax.ShapeDtypeStruct((count, features), f32),
        ],
        compiler_params=pltpu.CompilerParams(
            vmem_limit_bytes=VMEM_LIMIT, dimension_semantics=("arbitrary",)
        ),
        cost_estimate=pl.CostEstimate(
            flops=2 * count * features * features * 8, bytes_accessed=24 << 20, transcendentals=0
        ),
        name="attend_forward",
    )(
        pos, tokens, segment_ids.reshape(1, count), segment_ids.reshape(count, 1),
        biases, biases[2:3] + jnp.zeros((8, 1), f32), own_a, oth_a, own_b, oth_b,
    )


def attend_backward(
    geometry, half, pos, dh_ref, add_ref, sums_in, q_ref, k_ref, v_ref, p_ref, x_own, x_oth, o_own, o_oth,
    own_a, oth_a, own_b, oth_b, gown_ref, goth_ref, dx_ref, bias_ref, w_in, w_out, rows_in, sems,
):
    g = pl.program_id(0)
    features = dh_ref.shape[1]
    _, blocks, rows, _ = geometry
    sources = ((own_a, oth_a), (own_b, oth_b))

    @pl.when(g == 0)
    def _():
        for part in range(2):
            load_rows(
                pos, geometry, *sources[part], 3, half * (blocks // 2), blocks // 2,
                lambda j, part=part: w_out.at[part, pl.ds(pl.multiple_of(j * rows, rows), rows)],
                sems.at[0],
            )
        for m in range(3):
            load_rows(
                pos, geometry, *sources[half], m, 0, blocks,
                lambda j, m=m: w_in.at[m, pl.ds(pl.multiple_of(j * rows, rows), rows)],
                sems.at[1],
            )
        pltpu.make_async_copy(add_ref, dx_ref, sems.at[2]).start()
        for i, source in enumerate((x_own, x_oth, o_own, o_oth)):
            pltpu.make_async_copy(source, rows_in.at[i], sems.at[3]).start()
        pltpu.make_async_copy(w_out, w_out, sems.at[0]).wait()

    span = pl.ds(pl.multiple_of(g * 256, 256), 256)
    width = features // 2
    low = dh_ref[...]
    grad_mixed = (
        dot_nt(low[:, :width], w_out[0, span, :]) + dot_nt(low[:, width:], w_out[1, span, :])
    ).astype(bf16)
    lane = lax.broadcasted_iota(jnp.int32, (1, 128), 1)
    lows = [[], [], []]
    sums = [[], []]
    for pair in range(2):
        part = slice(pair * 128, pair * 128 + 128)
        q2, k2, v2 = q_ref[:, part], k_ref[:, part], v_ref[:, part]
        do2 = grad_mixed[:, part]
        k2t = k2.T
        zero = jnp.zeros_like(q2)
        dv = dk = None
        dqs = []
        for sub in range(2):
            mine = (lane < HEAD) if sub == 0 else (lane >= HEAD)
            probs = p_ref[pair * 2 + sub]
            do_mine = jnp.where(mine, do2, zero)
            grad_probs = dot_nt(v2, do_mine)
            wide_probs = probs.astype(f32)
            inner = jnp.sum(wide_probs * grad_probs, 0, keepdims=True)
            grad_scores = (wide_probs * (grad_probs - inner)).astype(bf16)
            dv_part = dot(probs, do_mine)
            dk_part = dot(grad_scores, jnp.where(mine, q2, zero))
            dv = dv_part if dv is None else dv + dv_part
            dk = dk_part if dk is None else dk + dk_part
            dqs.append(dot(k2t[sub * HEAD : sub * HEAD + HEAD], grad_scores))
        dq = jnp.concatenate(dqs, 0).T * HEAD**-0.5
        sums[0].append(jnp.sum(dq, 0, keepdims=True))
        sums[1].append(jnp.sum(dv, 0, keepdims=True))
        for store, value in zip(lows, (dq, dk, dv)):
            store.append(value.astype(bf16))
    joined = [jnp.concatenate(s, 1) for s in lows]

    @pl.when(g == 0)
    def _():
        pltpu.make_async_copy(rows_in, rows_in, sems.at[3]).wait()

    low = dh_ref[:, pl.ds(pl.multiple_of(half * width + g * 256, 256), 256)]
    for m, right in enumerate(joined + [low]):
        first = 0 if m < 3 else 2
        goth_ref[m] = dot(rows_in[first + 1], right).astype(bf16)
        gown_ref[m] = dot(rows_in[first], right).astype(bf16)

    @pl.when(g == 0)
    def _():
        bias_ref[...] = sums_in[...]

    for row in range(2):
        at = pl.ds(pl.multiple_of(half * width + g * 256, 256), 256)
        bias_ref[row : row + 1, at] = jnp.concatenate(sums[row], 1)

    @pl.when(g == 0)
    def _():
        pltpu.make_async_copy(w_in, w_in, sems.at[1]).wait()
        pltpu.make_async_copy(dx_ref, dx_ref, sems.at[2]).wait()

    dx_ref[...] += (
        dot_nt(joined[0], w_in[0, :, span])
        + dot_nt(joined[1], w_in[1, :, span])
        + dot_nt(joined[2], w_in[2, :, span])
    )


def run_attend_backward(half, pos, grad_sum, added, sums, kept, rows_of, weights):
    q, k, v, probs = kept
    own_a, oth_a, own_b, oth_b = weights
    count, features = q.shape
    rows = own_b.shape[2]
    geometry = (own_b.shape[1], features // rows, rows, own_b.shape[0] * 2)
    groups = features // 512
    whole = lambda *shape: pl.BlockSpec(shape, lambda g, pos: (0,) * len(shape))
    column = pl.BlockSpec((count, 256), lambda g, pos: (0, half * groups + g))
    anywhere = pl.BlockSpec(memory_space=pl.ANY)
    width = features // 2
    return pl.pallas_call(
        functools.partial(attend_backward, geometry, half),
        grid_spec=pltpu.PrefetchScalarGridSpec(
            num_scalar_prefetch=1,
            grid=(groups,),
            in_specs=[
                whole(count, features), anywhere, whole(8, features), column, column, column,
                pl.BlockSpec((4, count, count), lambda g, pos: (half * groups + g, 0, 0)),
                anywhere, anywhere, anywhere, anywhere,
                anywhere, anywhere, anywhere, anywhere,
            ],
            out_specs=[
                pl.BlockSpec((4, width, 256), lambda g, pos: (0, 0, g)),
                pl.BlockSpec((4, width, 256), lambda g, pos: (0, 0, g)),
                whole(count, features),
                whole(8, features),
            ],
            scratch_shapes=[
                pltpu.VMEM((3, features, width), bf16),
                pltpu.VMEM((2, width, width), bf16),
                pltpu.VMEM((4, width, count), bf16),
                pltpu.SemaphoreType.DMA((4,)),
            ],
        ),
        out_shape=[
            jax.ShapeDtypeStruct((4, width, width), bf16),
            jax.ShapeDtypeStruct((4, width, width), bf16),
            jax.ShapeDtypeStruct((count, features), f32),
            jax.ShapeDtypeStruct((8, features), f32),
        ],
        compiler_params=pltpu.CompilerParams(
            vmem_limit_bytes=ATTEND_BACK_LIMIT, dimension_semantics=("arbitrary",)
        ),
        cost_estimate=pl.CostEstimate(
            flops=2 * count * features * features * 6, bytes_accessed=16 << 20, transcendentals=0
        ),
        name="attend_backward",
    )(pos, grad_sum, added, sums, q, k, v, probs, *rows_of, own_a, oth_a, own_b, oth_b)


def moments(hidden):
    center = hidden - jnp.mean(hidden, -1, keepdims=True)
    return center, lax.rsqrt(jnp.mean(center * center, -1, keepdims=True) + 1e-12)


def norm_back(grad, normed, factor):
    return factor * (
        grad
        - jnp.mean(grad, -1, keepdims=True)
        - normed * jnp.mean(grad * normed, -1, keepdims=True)
    )


def gelu_pair(a):
    z = jnp.abs(a) * (0.5**0.5)
    t = 1.0 / (1.0 + 0.3275911 * z)
    poly = t * (
        0.127414796 + t * (-0.142248368 + t * (0.7107068705 + t * (-0.7265760135 + t * 0.5307027145)))
    )
    bell = jnp.exp(-0.5 * (a * a))
    tail = poly * bell
    phi = jnp.where(a >= 0, 1.0 - tail, tail)
    return a * phi, phi + a * (bell * 0.3989422804014327)


ROWS_AT_ONCE = 256
TILE = 1024


def row_blocks(count, step=ROWS_AT_ONCE):
    return [slice(r, r + step) for r in range(0, count, step)]


def turn_into_whole(ref, rows, value, pos, wide):
    features = value.shape[1]
    lanes = features // wide
    if lanes % 128:
        ref[rows, :] = value
    else:
        for slot in range(wide):
            ref[rows, whole_lanes(pos, slot, wide, lanes)] = value[
                :, slot * lanes : (slot + 1) * lanes
            ]


def store_blocks(ref, turned_rows, right):
    chips, block = ref.shape[0], ref.shape[1]
    step = max(1, 256 // block)
    for k in range(0, chips, step):
        value = dot(turned_rows[k * block : (k + step) * block, :], right).astype(bf16)
        for i in range(step):
            ref[k + i] = value[i * block : (i + 1) * block]


def once(*shape):
    return pl.BlockSpec(
        shape, lambda t: (0,) * len(shape), pipeline_mode=pl.Buffered(buffer_count=1)
    )


def odd_last_places(wide):
    half = wide // 2
    return [slot // half * half + slot % 2 * (half // 2) + slot % half // 2 for slot in range(wide)]


def ffn_forward(
    wide, tiles, pos, h_ref, vec, dy, b1, l0a, l0b, l1a, l1b, *refs
):
    ups, downs, refs = refs[:4], refs[4:8], refs[8:]
    (
    slope_ref, act_ref, u_out, result, dh, dh_low, dh_own, sums, oth_ref,
    total, u_low, act_all, dh_turned,
    ) = refs
    t = pl.program_id(0)
    count, features = h_ref.shape
    width = features // 2
    quarter = width // 2
    block = features // wide
    odd_last = [block * p for p in odd_last_places(wide)]

    @pl.when(t == 0)
    def _():
        for r in row_blocks(count):
            center, factor = moments(h_ref[r, :])
            low = (center * factor * (1.0 + vec[0:1, :]) + vec[1:2, :]).astype(bf16)
            u_low[r, :] = low
            u_out[:, r] = low.T

    def tile(ups, downs, first, at, size):
        columns = pl.ds(pl.multiple_of(t * TILE + at, 256), size)
        step = features // len(ups)
        for r in row_blocks(count, 512):
            a = b1[0:1, columns]
            for i, w in enumerate(ups):
                a = a + dot(u_low[r, i * step : i * step + step], w[...])
            act, slope = gelu_pair(a)
            act = act.astype(bf16)
            act_all[r, columns] = act
            act_ref[r, at : at + size] = act
            slope_ref[r, at : at + size] = slope.astype(bf16)
            for i, w in enumerate(downs):
                value = dot_nt(act, w[...])
                if first:
                    total[r, i * step : i * step + step] = value
                else:
                    total[r, i * step : i * step + step] += value

    @pl.when(t == 0)
    def _():
        size = TILE // 2
        tile((l0a.at[0], l0b.at[0]), (l0a.at[1], l0b.at[1]), True, 0, size)
        tile((l1a.at[0], l1b.at[0]), (l1a.at[1], l1b.at[1]), False, size, size)

    @pl.when((t > 0) & (t < tiles))
    def _():
        tile(ups, downs, False, 0, TILE)

    @pl.when(t == tiles - 1)
    def _():
        sums[...] = jnp.zeros_like(sums)
        for r in row_blocks(count):
            center, factor = moments(h_ref[r, :])
            u = center * factor * (1.0 + vec[0:1, :]) + vec[1:2, :]
            ffn = jnp.concatenate([total[r, at : at + block] for at in odd_last], 1)
            center, factor = moments(u + ffn + vec[2:3, :])
            normed = center * factor
            final = (normed * (1.0 + vec[3:4, :]) + vec[4:5, :]).astype(bf16)
            turn_into_whole(result, r, final, pos, wide)
            grad = dy[r, :].astype(f32)
            back = norm_back(grad * (1.0 + vec[3:4, :]), normed, factor)
            dh[r, :] = back
            low = back.astype(bf16)
            for slot, at in enumerate(odd_last):
                dh_low[r, at : at + block] = low[:, slot * block : (slot + 1) * block]
            dh_own[:, r] = low[:, :width].T
            dh_turned[:, r] = low[:, width:].T
            sums[0:1, :] += jnp.sum(grad, 0, keepdims=True)
            sums[1:2, :] += jnp.sum(grad * normed, 0, keepdims=True)
            sums[2:3, :] += jnp.sum(back, 0, keepdims=True)

    @pl.when(t >= tiles)
    def _():
        columns = pl.ds(pl.multiple_of((t - tiles) * TILE, TILE), TILE)
        store_blocks(oth_ref, dh_turned[...], act_all[:, columns])


def down_kernel(left, right, out_ref):
    store_blocks(out_ref, left[...], right[...])


def run_down(dh_own, act):
    width, count = dh_own.shape
    units = act.shape[1]
    wide = lax.axis_size("wide")
    block = 2 * width // wide
    return pl.pallas_call(
        down_kernel,
        grid=(units // TILE,),
        in_specs=[once(width, count), pl.BlockSpec((count, TILE), lambda t: (0, t))],
        out_specs=pl.BlockSpec((wide // 2, block, TILE), lambda t: (0, 0, t)),
        out_shape=jax.ShapeDtypeStruct((wide // 2, block, units), bf16),
        compiler_params=pltpu.CompilerParams(
            vmem_limit_bytes=24 << 20, dimension_semantics=("arbitrary",)
        ),
        cost_estimate=pl.CostEstimate(
            flops=2 * count * width * units, bytes_accessed=9 << 20, transcendentals=0
        ),
        name="down_own",
    )(dh_own, act)


def run_ffn_forward(pos, hidden, vec, dy, b1, late, early):
    count, features = hidden.shape
    wide = lax.axis_size("wide")
    width = features // 2
    units = b1.shape[1]
    tiles = units // TILE
    block = features // wide
    tall = pl.BlockSpec((width // 2, TILE), lambda t: (0, jnp.clip(t - 1, 0, tiles - 2)))
    grads = pl.BlockSpec((wide // 2, block, TILE), lambda t: (0, 0, jnp.maximum(t - tiles, 0)))
    grad_shape = jax.ShapeDtypeStruct((wide // 2, block, units), bf16)
    return pl.pallas_call(
        functools.partial(ffn_forward, wide, tiles),
        grid=(2 * tiles,),
        in_specs=[
            pl.BlockSpec(memory_space=pltpu.SMEM), once(count, features), once(8, features),
            once(count, features), once(1, units),
        ] + [once(2, width, TILE // 2)] * 4 + [tall] * 8,
        out_specs=[
            pl.BlockSpec((count, TILE), lambda t: (0, jnp.minimum(t, tiles - 1))),
            pl.BlockSpec((count, TILE), lambda t: (0, jnp.minimum(t, tiles - 1))),
            once(features, count), once(count, features), once(count, features),
            once(count, features), once(width, count), once(8, features), grads,
        ],
        out_shape=[
            jax.ShapeDtypeStruct((count, units), bf16),
            jax.ShapeDtypeStruct((count, units), bf16),
            jax.ShapeDtypeStruct((features, count), bf16),
            jax.ShapeDtypeStruct((count, features), bf16),
            jax.ShapeDtypeStruct((count, features), f32),
            jax.ShapeDtypeStruct((count, features), bf16),
            jax.ShapeDtypeStruct((width, count), bf16),
            jax.ShapeDtypeStruct((8, features), f32),
            grad_shape,
        ],
        scratch_shapes=[
            pltpu.VMEM((count, features), f32),
            pltpu.VMEM((count, features), bf16),
            pltpu.VMEM((count, units), bf16),
            pltpu.VMEM((width, count), bf16),
        ],
        compiler_params=pltpu.CompilerParams(
            vmem_limit_bytes=FFN_LIMIT, dimension_semantics=("arbitrary",)
        ),
        cost_estimate=pl.CostEstimate(
            flops=6 * count * features * units, bytes_accessed=34 << 20, transcendentals=0
        ),
        name="ffn_forward",
    )(pos, hidden, vec, dy, b1, *late, *early[0], *early[1])


def ffn_backward(wide, last, *refs):
    pos, dh_low, u_turned, slope, *refs = refs
    late, refs = ([], refs) if last else (refs[:4], refs[4:])
    ups, downs, refs = refs[:4], refs[4:8], refs[8:]
    if last:
        du_in, dh, h_ref, vec, own_ref, oth_ref, db_ref, dh1, dh1_low, sums, total, low_all = refs
    else:
        own_ref, oth_ref, db_ref, total, low_all = refs
    t = pl.program_id(0)
    count, features = dh_low.shape
    width = features // 2

    def tile(ups, downs, before):
        db = 0.0
        step = features // len(ups)
        for r in row_blocks(count, 512):
            grad = 0.0
            for i, w in enumerate(downs):
                grad = grad + dot(dh_low[r, i * step : i * step + step], w[...])
            grad = grad * slope[r, :].astype(f32)
            db = db + jnp.sum(grad, 0, keepdims=True)
            low = grad.astype(bf16)
            low_all[r, :] = low
            for i, w in enumerate(ups):
                value = dot_nt(low, w[...])
                columns = slice(i * step, i * step + step)
                total[r, columns] = value if before is None else before[r, columns] + value
        db_ref[...] = db
        low = low_all[...]
        store_blocks(oth_ref, u_turned[width:, :], low)
        store_blocks(own_ref, u_turned[:width, :], low)

    if last:

        @pl.when(t == 0)
        def _():
            tile(ups, downs, du_in)

    else:
        for i in range(2):

            @pl.when(t == i)
            def _(i=i):
                a, b = late[2 * i : 2 * i + 2]
                tile((a.at[0], b.at[0]), (a.at[1], b.at[1]), total if i else None)

    @pl.when(t >= (1 if last else 2))
    def _():
        tile(ups, downs, total)

    if last:

        @pl.when(t == pl.num_programs(0) - 1)
        def _():
            sums[...] = jnp.zeros_like(sums)
            for r in row_blocks(count):
                center, factor = moments(h_ref[r, :])
                normed = center * factor
                du = total[r, :] + dh[r, :]
                back = norm_back(du * (1.0 + vec[0:1, :]), normed, factor)
                turn_into_whole(dh1, r, back, pos, wide)
                turn_into_whole(dh1_low, r, back.astype(bf16), pos, wide)
                sums[0:1, :] += jnp.sum(du, 0, keepdims=True)
                sums[1:2, :] += jnp.sum(du * normed, 0, keepdims=True)
                sums[2:3, :] += jnp.sum(back, 0, keepdims=True)


BACK_TILE = 512


def run_ffn_backward(pos, dh_low, u_turned, slope, late, early, tail):
    count, features = dh_low.shape
    wide = lax.axis_size("wide")
    width = features // 2
    block = features // wide
    last = tail is not None
    late_tiles = 2
    assert late[0].shape[2] == BACK_TILE
    half_tiles = early[0][0].shape[1] // BACK_TILE // 2
    tiles = half_tiles if last else late_tiles + half_tiles
    ins = [pos, dh_low, u_turned, slope]
    if last:
        at_slope = lambda t: (0, late_tiles + t)
        at_early = lambda t: (0, t)
    else:
        at_slope = lambda t: (0, jnp.where(t < late_tiles, t, t + half_tiles))
        at_early = lambda t: (0, half_tiles + jnp.maximum(t - late_tiles, 0))
    in_specs = [
        pl.BlockSpec(memory_space=pltpu.SMEM), once(count, features), once(features, count),
        pl.BlockSpec((count, BACK_TILE), at_slope),
    ]
    if not last:
        in_specs += [once(2, width, BACK_TILE)] * 4
        ins += list(late)
    in_specs += [pl.BlockSpec((width // 2, BACK_TILE), at_early)] * 8
    ins += [*early[0], *early[1]]
    grads = pl.BlockSpec((wide // 2, block, BACK_TILE), lambda t: (0, 0, t))
    grad_shape = jax.ShapeDtypeStruct((wide // 2, block, tiles * BACK_TILE), bf16)
    out_specs = [grads, grads, pl.BlockSpec((1, BACK_TILE), lambda t: (0, t))]
    out_shape = [grad_shape, grad_shape, jax.ShapeDtypeStruct((1, tiles * BACK_TILE), f32)]
    scratch = [pltpu.VMEM((count, BACK_TILE), bf16)]
    if last:
        ins += list(tail)
        in_specs += [once(count, features)] * 3 + [once(8, features)]
        out_specs += [once(count, features), once(count, features), once(8, features)]
        out_shape += [
            jax.ShapeDtypeStruct((count, features), f32),
            jax.ShapeDtypeStruct((count, features), bf16),
            jax.ShapeDtypeStruct((8, features), f32),
        ]
        scratch = [pltpu.VMEM((count, features), f32)] + scratch
    else:
        out_specs.append(once(count, features))
        out_shape.append(jax.ShapeDtypeStruct((count, features), f32))
    return pl.pallas_call(
        functools.partial(ffn_backward, wide, last),
        grid=(tiles,),
        in_specs=in_specs,
        out_specs=out_specs,
        out_shape=out_shape,
        scratch_shapes=scratch,
        compiler_params=pltpu.CompilerParams(
            vmem_limit_bytes=BACK_LIMIT, dimension_semantics=("arbitrary",)
        ),
        cost_estimate=pl.CostEstimate(
            flops=6 * count * features * tiles * BACK_TILE, bytes_accessed=17 << 20, transcendentals=0
        ),
        name="ffn_backward",
    )(*ins)


def swap_hop(v, hop):
    kind, bit = hop
    return swap_wide(v, 2 << bit) if kind == "wide" else swap_narrow(v, 1 << bit)


class Scatter:
    def __init__(self, own, other, axes, mine, extra=None):
        self.parts = [] if own is None else [(own, ())]
        self.other = other
        self.axes, self.mine = dict(axes), mine
        self.extra = [] if extra is None else [(extra[0], ())]
        self.extra_other = None if extra is None else extra[1]

    def cross(self):
        own = self.parts[0][0]
        self.parts.append((swap_wide(self.other, 1).reshape(own.shape), ()))
        if self.extra:
            self.extra.append((swap_wide(self.extra_other, 1), ()))

    def columns(self, first, count):
        unit = Scatter(None, None, self.axes, self.mine)
        unit.parts = [(v, path + (("columns", (first, count)),)) for v, path in self.parts]
        return unit

    def plan(self, hop):
        self.hop = hop
        axis = self.axes.pop(hop, None)
        keep = 0 if axis is None else self.mine[hop]
        more = lambda parts, i: [(v, path + ((axis, i),)) for v, path in parts]
        leaving, extra = more(self.parts, 1 - keep), more(self.extra, 1 - keep)
        self.parts, self.extra = more(self.parts, keep), more(self.extra, keep)
        if axis is not None:
            self.axes = {h: a - (a > axis) for h, a in self.axes.items()}
        return leaving, extra

    def send(self, hop):
        leaving, extra = self.plan(hop)
        self.leaving = low_of(leaving)
        if extra:
            self.leaving = jnp.concatenate([self.leaving, low_of(extra)], -2)

    def receive(self):
        came = swap_hop(self.leaving, self.hop)
        if self.extra:
            rows = self.parts[0][0].shape[-2]
            self.extra.append((came[..., rows:, :], ()))
            came = came[..., :rows, :]
        self.parts.append((came, ()))


def join(values, *units):
    values, came = lax.optimization_barrier((values, [unit.parts[-1][0] for unit in units]))
    for unit, v in zip(units, came):
        unit.parts[-1] = (v, unit.parts[-1][1])
    return values


def start(first, *sends, fused=True):
    plans = [unit.plan(hop_to) for unit, hop_to in sends]
    assert not any(extra for _, extra in plans)
    first, *leaving = tie(
        first, *(low_many if fused else lambda s: [low_of(p) for p in s])([p for p, _ in plans])
    )
    for (unit, _), v in zip(sends, leaving):
        unit.leaving = v
        unit.receive()
    return first


class Given:
    def __init__(self, giver, taker):
        self.giver, self.taker = giver, taker

    def plan(self, hop_to):
        self.hop = hop_to
        return self.giver.parts, []

    def send(self, hop_to):
        self.leaving = low_of(self.plan(hop_to)[0])

    def receive(self):
        self.taker.parts.append((swap_hop(self.leaving, self.hop), ()))


class Several:
    def __init__(self, *units):
        self.units = units

    def send(self, hop_to):
        self.hop = hop_to
        for unit in self.units:
            unit.send(hop_to)
        self.sizes = [unit.leaving.shape[-1] for unit in self.units]
        self.leaving = jnp.concatenate([unit.leaving for unit in self.units], -1)

    def receive(self):
        came = swap_hop(self.leaving, self.hop)
        first = 0
        for unit, size in zip(self.units, self.sizes):
            taker = unit.taker if isinstance(unit, Given) else unit
            taker.parts.append((came, (("columns", (first, size)),)))
            first += size


def low_many_kernel(slices, *refs):
    count = len(slices)
    flat = [cut for cuts in slices for cut in cuts]
    ins, outs = refs[: len(flat)], refs[len(flat) : len(flat) + count]
    buffers, sems = refs[len(flat) + count : -1], refs[-1]
    copies = []
    for i, (starts, sizes, axes) in enumerate(flat):
        at = tuple(
            pl.ds(first, size) if axis in axes else first
            for axis, (first, size) in enumerate(zip(starts, sizes))
        )
        copies.append(pltpu.make_async_copy(ins[i].at[at], buffers[i], sems.at[i]))
        copies[-1].start()
    i = 0
    for out, cuts in zip(outs, slices):
        total = None
        for _ in cuts:
            copies[i].wait()
            value = buffers[i][...].astype(f32)
            total = value if total is None else total + value
            i += 1
        out[...] = total.astype(bf16)


def low_many(sends):
    fit = lambda cut: (
        all(isinstance(i, int) for i in cut[0])
        and cut[0][-1] % 128 == 0
        and cut[1][-1] % 128 == 0
        and len(cut[2]) >= 2
    )
    cuts = [[cut_of(part) for part in parts] for parts in sends]
    chosen = [i for i, some in enumerate(cuts) if all(fit(cut) for cut in some)]
    out = [None if i in chosen else low_of(parts) for i, parts in enumerate(sends)]
    if not chosen:
        return out
    shape = lambda cut: tuple(cut[1][axis] for axis in cut[2])
    arrays = [v for i in chosen for v, _ in sends[i]]
    buffers = [pltpu.VMEM(shape(cut), bf16) for i in chosen for cut in cuts[i]]
    results = pl.pallas_call(
        functools.partial(low_many_kernel, [cuts[i] for i in chosen]),
        in_specs=[pl.BlockSpec(memory_space=pl.ANY)] * len(arrays),
        out_specs=[pl.BlockSpec(memory_space=pltpu.VMEM)] * len(chosen),
        out_shape=[jax.ShapeDtypeStruct(shape(cuts[i][0]), bf16) for i in chosen],
        scratch_shapes=buffers + [pltpu.SemaphoreType.DMA((len(arrays),))],
        compiler_params=pltpu.CompilerParams(vmem_limit_bytes=VMEM_LIMIT),
        name="sums",
    )(*arrays)
    for i, v in zip(chosen, results):
        out[i] = v
    return out


def cut_of(part):
    v, path = part
    starts, sizes, axes = [0] * v.ndim, list(v.shape), list(range(v.ndim))
    for axis, i in path:
        if axis is None:
            sizes[-1] //= 2
            starts[-1] += i * sizes[-1]
        elif axis == "columns":
            starts[-1] += i[0]
            sizes[-1] = i[1]
        else:
            at = axes.pop(axis)
            starts[at], sizes[at] = i, 1
    return starts, sizes, axes


def taken(part):
    v = part[0]
    starts, sizes, axes = cut_of(part)
    if all(isinstance(i, int) for i in starts):
        v = lax.slice(v, starts, [i + n for i, n in zip(starts, sizes)])
    else:
        v = lax.dynamic_slice(v, [jnp.int32(i) for i in starts], sizes)
    return v.reshape([sizes[at] for at in axes])


def sum_of(parts, view=lambda v: v):
    return sum(view(taken(p)).astype(f32) for p in parts)


def low_of(parts, view=lambda v: v):
    return sum_of(parts, view).astype(bf16)


def per_device(tokens, segment_ids, attn_weight, vectors, ffn_weight, ffn_bias, out_grad):
    wide, narrow = lax.axis_size("wide"), lax.axis_size("narrow")
    w, z = lax.axis_index("wide"), lax.axis_index("narrow")
    chip, core = lax.div(w, 2), lax.rem(w, 2)
    bits = chip_bits()
    up = list(range(bits))
    down = up[::-1]
    pos = jnp.stack([chip, core, z]).astype(jnp.int32)
    count, features = tokens.shape
    half = features // 2

    rows_each = attn_weight.shape[0]
    each, each_bias = vectors.shape[0], ffn_bias.shape[0]
    small = jnp.concatenate([vectors, ffn_bias, jnp.zeros((features - each - each_bias,), bf16)])
    small = jnp.concatenate([small[None], jnp.zeros((7, features), bf16)])
    v = jnp.concatenate([attn_weight, small])
    attn = v[None]
    units = ffn_weight.shape[2]
    width = units // SUBS
    tail = units - width
    every = range(bits)
    steps = list(range(narrow_bits()))[::-1]
    orders = (up, down)

    def along(v, step, axis):
        return jnp.concatenate([v, swap_narrow(v, 1 << step)], axis)

    late = [(ffn_weight[i, :, tail:], []) for i in range(2)]
    for i, step in enumerate(steps):
        attn = along(attn, step, 0)
        if i == 0:
            (attn, *v) = tie(attn, *[v for v, _ in late])
            late = [(v, done) for v, (_, done) in zip(v, late)]
    for i in every:
        late = [hop(v, done, order[i]) for (v, done), order in zip(late, orders)]
    late = [v.reshape(half, width) for v, _ in late]
    rows = features // wide
    late[1] = late[1].reshape(-1, 2, rows, width).swapaxes(0, 1).reshape(half, width)
    late = jnp.stack(late)
    early, attn, late = tie(ffn_weight[:, :, :tail], attn, late)
    attn = [(attn[:, :, :half], []), (attn[:, :rows_each, half:], [])]
    for i in range(max(bits, len(steps))):
        if i < bits:
            attn = [hop(v, done, order[i]) for (v, done), order in zip(attn, orders)]
        if i < len(steps):
            early = along(early, steps[i], 2)
        early, a, b = tie(early, *[v for v, _ in attn])
        attn = [(a, attn[0][1]), (b, attn[1][1])]
    attn_a, attn_b = [v.reshape((wide // 2,) + v.shape[bits:]) for v, _ in attn]
    early = [(early[which], []) for which in range(2)]
    late, attn_a, attn_b, *firsts = tie(late, attn_a, attn_b, *[v for v, _ in early])
    halves = [attn_a, swap_wide(attn_a, 1), attn_b, swap_wide(attn_b, 1)]
    for i in every[:-1]:
        early = [hop(v, done, order[i]) for v, (_, done), order in zip(firsts, early, orders)]
        if i < len(steps) - 1:
            late = along(late, steps[i], 2)
        if i == 0:
            tokens_now, *firsts = tie(tokens, *[v for v, _ in early])
        else:
            firsts = [v for v, _ in early]
    for step in steps[bits - 1 : -1]:
        late = along(late, step, 2)
    late_came = swap_narrow(late, 1 << steps[-1])

    small = jnp.concatenate([h[:, :, rows_each, : each + each_bias] for h in halves[:2]])
    small = small.reshape(-1, each + each_bias)
    slots = jnp.arange(wide * narrow)
    slot_core, slot_chip, slot_z = (
        slots // (wide * narrow // 2), (slots // narrow) % (wide // 2), slots % narrow,
    )
    slot_w = (slot_chip ^ chip) * 2 + (slot_core ^ core)
    whole_at = slot_w * narrow + (turned(slot_z, narrow_bits()) ^ z)
    bias_at = slot_z * wide + slot_w
    spots = jnp.arange(wide * narrow)[:, None]
    vec_rows = dot((spots == whole_at[None, :]).astype(bf16), small[:, :each]).reshape(8, features)
    bias_rel = dot((spots == bias_at[None, :]).astype(bf16), small[:, each:])
    bias_rel = bias_rel.reshape(narrow, units)
    bias_rel = jnp.concatenate(
        [bias_rel[:, tail:].reshape(1, -1), bias_rel[:, :tail].reshape(1, -1)], 1
    )
    bq, bv, bo, s1, bf, s2, g1, g2 = [vec_rows[i] for i in range(8)]
    slot_vec = to_slots_quick(jnp.stack([g1, s1, bf, g2, s2, s2, s2, s2]), pos, chip, core)
    dy = to_slots_quick(out_grad, pos, chip, core)
    in_kernel = (features // wide) % 128 == 0

    def core_rows(v, which):
        t = v.reshape(count, -1, 2, narrow * rows_each)
        return pick(t, 2, which).reshape(count, half).T

    x_rows = [core_rows(tokens, core), core_rows(tokens, 1 - core)]

    biases = jnp.stack([bq, bv, bo, bo, bo, bo, bo, bo])
    tokens_now, dy, slot_vec, bias_rel, *x_rows = tie(tokens_now, dy, slot_vec, bias_rel, *x_rows)
    *kept, mixed, hidden = run_attend_forward(pos, tokens_now, segment_ids, biases, *halves)
    o_rows = [core_rows(mixed, core), core_rows(mixed, 1 - core)]
    last_hop = [swap_wide(v, 2 << order[-1]) for v, order in zip(firsts, orders)]
    late = [late, late_came]
    firsts = [v.reshape(half // 2, -1) for v in firsts]
    first_crossed = [swap_wide(v, 1) for v in firsts]
    hidden, *late = tie(hidden, *late)
    late_crossed = [swap_wide(v, 1) for v in late]
    hidden, *rest = tie(hidden, *first_crossed, *o_rows)
    first_crossed, o_rows = rest[:2], rest[2:]
    if not in_kernel:
        hidden = to_slots(hidden, chip, core)
    last_hop = [v.reshape(half // 2, -1) for v in last_hop]
    hidden, late_0, late_1, *last_hop = tie(hidden, *late_crossed, *last_hop)
    early = [
        (own, v, crossed, swap_wide(v, 1))
        for own, v, crossed in zip(firsts, last_hop, first_crossed)
    ]
    late = [late[0], late_0, late[1], late_1]
    slope, act, u_turned, result, dh, dh_low, dh_own, sums_two, other = run_ffn_forward(
        pos, hidden, slot_vec, dy, bias_rel, late, early
    )
    if not in_kernel:
        result = from_slots(result, chip, core)

    late_width, half_early = narrow * width, narrow * tail // 2
    axes = {("wide", bit): bits - 1 - bit for bit in range(bits)}
    chips = lambda order: [("wide", bit) for bit in order]
    along = [("narrow", bit) for bit in range(narrow_bits())]

    def ffn_unit(own, other):
        own = own.reshape((2,) * bits + own.shape[1:])
        unit = Scatter(own, other, axes, dict.fromkeys(axes, 0))
        unit.cross()
        return unit

    downs = ffn_unit(run_down(dh_own, act), other)
    down_0, down_a, down_b = (
        downs.columns(0, late_width), downs.columns(late_width, half_early),
        downs.columns(late_width + half_early, half_early),
    )
    low = start(
        dh_low, (down_0, along[0]), (down_a, ("wide", down[0])), (down_b, ("wide", up[0])),
        fused=False,
    )
    own, other, *rest = run_ffn_backward(pos, low, u_turned, slope, late, early, None)
    own, other, *rest = join([own, other, *rest], down_0, down_a, down_b)
    dbs = [rest[0]]
    up_a = ffn_unit(own, other)
    sends = [(down_a, hop_to) for hop_to in chips(down[1:2])]
    sends += [(down_b, hop_to) for hop_to in chips(up[1:2])]
    low = start(low, (down_0, along[1]), *sends)
    own, other, *rest = run_ffn_backward(
        pos, low, u_turned, slope, late, early, (rest[1], dh, hidden, slot_vec)
    )
    own, other, *rest = join([own, other, *rest], up_a, down_0, down_a, down_b)
    dbs.append(rest[0])
    grad_sum, grad_low, sums_one = rest[1:]
    up_b = ffn_unit(own, other)
    up_late, up_upper = up_a.columns(0, late_width), up_a.columns(late_width, half_early)
    for unit, order in ((down_a, down), (down_b, up)):
        for hop_to in chips(order[2:]):
            unit.send(hop_to)
            unit.receive()
    if not in_kernel:
        grad_sum = from_slots(grad_sum, chip, core)
        grad_low = from_slots(grad_low, chip, core)

    low_bits = bits - 2
    names = chips([bits - 1, bits - 2] + list(range(low_bits))[::-1]) + along[::-1]
    attn_axes = {name: axis for axis, name in enumerate(names)}
    mine = {("wide", bit): bit_of(chip, bit) for bit in range(bits)}
    mine.update({("narrow", bit): bit_of(z, bit) for bit in range(narrow_bits())})
    added = grad_sum
    attn_units = []
    slot_sums = from_slots(jnp.concatenate([sums_one[:3], sums_two[:3]]), chip, core)
    gs1, gg1, gbo, gs2, gg2, gbf = [slot_sums[i] for i in range(6)]
    db = jnp.concatenate([dbs[1], dbs[0][:, late_width:]], 1).reshape(narrow, tail)
    db = jnp.concatenate([db, dbs[0][:, :late_width].reshape(narrow, width)], 1)
    db = db.reshape(narrow, wide, each_bias)
    db = jnp.stack([pick(db, 0, turned(i ^ z, narrow_bits())) for i in range(narrow)], 1)

    def small_rows(vec):
        lanes = lambda v: jnp.pad(v[:, :, None], ((0, 0),) * 3 + ((0, half - v.shape[2]),))
        rows = jnp.concatenate([lanes(vec.reshape(wide, narrow, each)), lanes(db)], 2)
        rows = jnp.pad(rows, ((0, 0), (0, 0), (0, 6), (0, 0)))
        rows = rows.astype(bf16).reshape((2,) * (bits + 1 + narrow_bits()) + rows.shape[2:])
        return pick(rows, bits, core), pick(rows, bits, 1 - core)

    sums = jnp.stack([jnp.zeros_like(gs1)] * 2 + [gbo, gs1, gbf, gs2, gg1, gg2])
    for part in range(2):
        if part == 0:
            sends = [(up_late, ("wide", up[0])), (up_upper, ("wide", down[0]))]
            sends += [(Given(down_b, down_a), along[0])]
            low = start(grad_low, *sends)
        else:
            sends = [(up_late, hop_to) for hop_to in chips(up[1:2])]
            sends += [(up_upper, hop_to) for hop_to in chips(down[1:2])]
            sends += [(up_b, ("wide", down[0])), (down_a, along[1])]
            sends += [(attn_units[0], ("wide", up[0]))]
            low = start(low, *sends)
        own, other, added, sums = run_attend_backward(
            part, pos, low, added, sums, kept, x_rows + o_rows, halves
        )
        if part == 0:
            ready = (up_late, up_upper, down_a, up_b)
        else:
            ready = (up_late, up_upper, down_a, up_b, down_0)
        if part == 0:
            own, other, added, sums = join([own, other, added, sums], *ready)
        else:
            own, added, sums = join([own, added, sums], *ready)
        shape = (2,) * len(names) + (rows_each, half)
        unit = Scatter(
            own.reshape(shape), other, attn_axes, mine, None if part == 0 else small_rows(sums)
        )
        unit.cross()
        attn_units.append(unit)
    grad_tokens = added

    def move(unit, *hops):
        for hop_to in hops:
            unit.send(hop_to)
            unit.receive()

    a, b = attn_units
    move(up_late, *chips(up[2:]))
    move(up_upper, *chips(down[2:]))
    move(down_a, *along[2:])
    move(down_0, *along[2:])
    move(b, ("wide", down[0]))
    move(up_b, *chips(down[1:]))
    move(a, *chips(up[1:]))
    move(b, *chips(down[1:]))
    move(Several(up_late, Given(up_upper, up_b)), along[0])
    move(down_0, *chips(down))
    for hop_to in along[1:]:
        move(Several(up_late, up_b), hop_to)
    move(a, *along)
    move(b, *along)
    grad_ffn = jnp.stack(
        [
            jnp.concatenate([sum_of(up_b.parts), sum_of(up_late.parts)], -1),
            jnp.concatenate([sum_of(down_a.parts), sum_of(down_0.parts)], -1),
        ]
    )
    grad_attn = jnp.concatenate([sum_of(u.parts) for u in attn_units], -1)
    tally = sum_of(b.extra)
    return (
        result, grad_tokens, grad_attn, tally[0, :each], grad_ffn, tally[1, :each_bias],
    )


def solution(mesh):
    return jax.shard_map(
        per_device,
        mesh=mesh,
        in_specs=(
            P(("wide", "narrow"), None),
            P(("wide", "narrow"), None),
            P(("wide", "narrow"), None),
            P(("wide", "narrow")),
            P(None, "wide", "narrow"),
            P(("narrow", "wide")),
            P(("wide", "narrow"), None),
        ),
        out_specs=(
            P(("wide", "narrow"), None),
            P(("wide", "narrow"), None),
            P(("wide", "narrow"), None),
            P(("wide", "narrow")),
            P(None, "wide", "narrow"),
            P(("narrow", "wide")),
        ),
        check_vma=False,
    )
```
